32 devices in a mesh: dp: 4 (over y, x), blk: 8 (over z, core).
Axes of the slice: x: 2, y: 2, z: 4, core: 2. Of those that a mesh axis runs over, the one named last changes fastest.
Arguments:
- query_rows: bfloat16 [4, 1024, 1024], P('dp', 'blk'), may hold values from -160 to 160
- key_rows: bfloat16 [4, 1024, 1024], P('dp', 'blk'), may hold values from -6 to 6
- value_rows: bfloat16 [4, 1024, 1024], P('dp', 'blk'), may hold values from -6 to 6
- grad_out: bfloat16 [4, 1024, 1024], P('dp', 'blk'), may hold values from -6 to 6
- pos_keys: bfloat16 [512, 1024], P('blk'), may hold values from -3 to 3
- bias_content: float32 [1024], replicated, may hold values from -3 to 3
- bias_position: float32 [1024], replicated, may hold values from -3 to 3
Outputs:
- query_gradient: bfloat16 [4, 1024, 1024], P('dp', 'blk')
- grad_key: bfloat16 [4, 1024, 1024], P('dp', 'blk')
- grad_value: bfloat16 [4, 1024, 1024], P('dp', 'blk')
- grad_pos_keys: float32 [512, 1024], P('blk')
The draws below stay inside these ranges and needn't reach their ends.
All inputs are finite; a program needn't handle non-finite values.
Results may differ from the reference program's by a relative error of at most 0.015.
The reference program's roundings to bfloat16 on the way (of `query_content`, `query_position`, `attention_b` and `dscore`) count: a program that leaves them out, or rounds other values in their place, can miss the bound.
Values may be sent and summed in bfloat16 or wider, within the bound.
No kernel may reach another device: no remote copies, remote signals or barrier semaphores. Data moves between devices by JAX's collectives and lax.ppermute only.
A program may use at most 64 MiB of HBM per device.

```python
import jax
import jax.numpy as jnp
from jax import lax

H = 16
DH = 64
C = 128
D = 1024
BAND = 256
BATCH = 4
LEN = 1024
N_BLK = 8


def paired_fields(key):
    base_key = jax.random.fold_in(key, 11)
    key_query, key_keys = jax.random.split(base_key, 2)
    dims_all = (BATCH, LEN, D)
    query_field = jnp.clip(jax.random.normal(key_query, dims_all, jnp.float32), -5.0, 5.0)
    key_field = jnp.clip(jax.random.normal(key_keys, dims_all, jnp.float32), -5.0, 5.0)
    return (query_field, key_field)


def draw_query_rows(key, part):
    return paired_fields(key)[0].astype(jnp.bfloat16)


def draw_key_rows(key, part):
    return paired_fields(key)[1].astype(jnp.bfloat16)


def block_scale(rng, extent, cuts, low, top_value):
    loudness, own = 1.0, jax.random.fold_in(rng, 6)
    for dim, shards_of in cuts:
        draws = jnp.exp(jax.random.uniform(jax.random.fold_in(own, dim), (shards_of,), jnp.float32, low / len(cuts), top_value / len(cuts)))
        loudness = loudness * jnp.repeat(draws, extent[dim] // shards_of).reshape([-1 if axis == dim else 1 for axis in range(len(extent))])
    return loudness


def gaussian(stream_key, dims, scale, most, shards=(), kind=jnp.bfloat16):
    loudness = block_scale(stream_key, dims, shards, -0.22, 0.18) if shards else 1.0
    drawn = jax.random.normal(stream_key, dims, jnp.float32) * scale * loudness
    return jnp.minimum(jnp.maximum(drawn, -most), most).astype(kind)


def setup_inputs(seed: int = 0) -> dict:
    key_list = jax.random.split(jax.random.key(seed), 8)
    query_rows = draw_query_rows(jax.random.fold_in(key_list[7], 71), 0)
    key_rows = draw_key_rows(jax.random.fold_in(key_list[7], 71), 0)
    value_rows = gaussian(key_list[2], (BATCH, LEN, D), 1.0, 6.0, ((0, 4), (1, 8)))
    grad_out = gaussian(key_list[3], (BATCH, LEN, D), 1.0, 6.0, ((0, 4), (1, 8)))
    pos_keys = gaussian(key_list[4], (2 * BAND, D), 0.5, 3.0, ((0, 8),))
    bias_content = gaussian(key_list[5], (D,), 0.5, 3.0, (), jnp.float32)
    bias_position = gaussian(key_list[6], (D,), 0.5, 3.0, (), jnp.float32)
    return {"query_rows": query_rows, "key_rows": key_rows, "value_rows": value_rows, "grad_out": grad_out, "pos_keys": pos_keys, "bias_content": bias_content, "bias_position": bias_position}


def offset_table(frames):
    positions = jnp.arange(frames, dtype=jnp.int32)
    return (positions[:, None] - positions[None, :] + frames).astype(jnp.int32)


def relative_select(products):
    heads_count, frames = products.shape[0], products.shape[1]
    lookup = jnp.broadcast_to(offset_table(frames)[None], (heads_count, frames, frames))
    return jnp.take_along_axis(products, lookup, axis=2)


def relative_place(gradient, spread):
    heads_count, frames = gradient.shape[0], gradient.shape[1]
    positions = jnp.arange(frames, dtype=jnp.int32)
    zeroed = jnp.zeros((heads_count, frames, spread), gradient.dtype)
    return zeroed.at[:, positions[:, None], offset_table(frames)].set(gradient)


def split_heads(matrix):
    return matrix.reshape(matrix.shape[0], H, DH).astype(jnp.float32)


def join_head_axes(matrix):
    return matrix.reshape(matrix.shape[0], D)


def block_grads(query_content, query_position, own_keys, own_values, prev_keys, prev_values, grad_rows, band_own, band_prev):
    factor = DH ** -0.5
    content_h = split_heads(query_content)
    position_per_head = split_heads(query_position)
    keys_h = split_heads(jnp.concatenate([own_keys, prev_keys], axis=0))
    values_h = split_heads(jnp.concatenate([own_values, prev_values], axis=0))
    grad_h = split_heads(grad_rows)
    current_band_per_head = split_heads(band_own)
    earlier_band_per_head = split_heads(band_prev)
    content = jnp.einsum('ihd,jhd->hij', content_h, keys_h)
    current_position = relative_select(jnp.einsum('fju,tju->jft', position_per_head, current_band_per_head))
    earlier_position = relative_select(jnp.einsum('fju,tju->jft', position_per_head, earlier_band_per_head))
    scores = (content + jnp.concatenate([current_position, earlier_position], axis=2)) * factor
    row_max = jnp.max(scores, axis=2, keepdims=True)
    shifted = jnp.exp(scores - row_max)
    attention = shifted / jnp.sum(shifted, axis=2, keepdims=True)
    attention_b = lax.optimization_barrier(attention.astype(jnp.bfloat16))
    grad_weights = jnp.einsum('ihd,jhd->hij', grad_h, values_h)
    row_delta = jnp.sum(attention * grad_weights, axis=2, keepdims=True)
    dscore = lax.optimization_barrier((attention * (grad_weights - row_delta) * factor).astype(jnp.bfloat16))
    dscore_f = dscore.astype(jnp.float32)
    current_location = relative_place(dscore_f[:, :, :C], BAND)
    earlier_location = relative_place(dscore_f[:, :, C:], BAND)
    query_gradient = jnp.einsum('hij,jhd->ihd', dscore_f, keys_h)
    query_gradient = query_gradient + jnp.einsum('urk,kuo->ruo', current_location, current_band_per_head)
    query_gradient = query_gradient + jnp.einsum('urk,kuo->ruo', earlier_location, earlier_band_per_head)
    grad_keys = join_head_axes(jnp.einsum('hij,ihd->jhd', dscore_f, content_h))
    grad_values = join_head_axes(jnp.einsum('hij,ihd->jhd', attention_b.astype(jnp.float32), grad_h))
    current_band_gradient = join_head_axes(jnp.einsum('zfg,fzw->gzw', current_location, position_per_head))
    earlier_band_gradient = join_head_axes(jnp.einsum('zfg,fzw->gzw', earlier_location, position_per_head))
    return (join_head_axes(query_gradient).astype(jnp.bfloat16), grad_keys[:C], grad_keys[C:].astype(jnp.bfloat16),
            grad_values[:C], grad_values[C:].astype(jnp.bfloat16), current_band_gradient, earlier_band_gradient)


def reference(query_rows, key_rows, value_rows, grad_out, pos_keys, bias_content, bias_position):
    query_content = (query_rows.astype(jnp.float32) + bias_content).astype(jnp.bfloat16)
    query_position = (query_rows.astype(jnp.float32) + bias_position).astype(jnp.bfloat16)
    band_own = pos_keys[:BAND]
    band_prev = pos_keys[BAND:]

    def by_block(matrix):
        return matrix.reshape(BATCH * N_BLK, C, D)

    def previous(matrix):
        return jnp.roll(matrix.reshape(BATCH, N_BLK, C, D), 1, axis=1).reshape(BATCH * N_BLK, C, D)

    def to_owner(matrix):
        return jnp.roll(matrix.reshape(BATCH, N_BLK, C, D), -1, axis=1).reshape(BATCH, LEN, D)

    def step_one(band_sums, inputs):
        outcome = block_grads(*inputs, band_own, band_prev)
        return (band_sums[0] + outcome[5], band_sums[1] + outcome[6]), outcome[:5]

    initial = (jnp.zeros((BAND, D), jnp.float32), jnp.zeros((BAND, D), jnp.float32))
    band_sums, stacked = lax.scan(step_one, initial, (by_block(query_content), by_block(query_position),
                                                      by_block(key_rows), by_block(value_rows),
                                                      previous(key_rows), previous(value_rows), by_block(grad_out)))
    query_gradient = stacked[0].reshape(BATCH, LEN, D)
    key_part = lax.optimization_barrier(to_owner(stacked[2]))
    value_part = lax.optimization_barrier(to_owner(stacked[4]))
    grad_key = (stacked[1].reshape(BATCH, LEN, D) + key_part.astype(jnp.float32)).astype(jnp.bfloat16)
    grad_value = (stacked[3].reshape(BATCH, LEN, D) + value_part.astype(jnp.float32)).astype(jnp.bfloat16)
    grad_pos_keys = jnp.concatenate([band_sums[0], band_sums[1]], axis=0)
    return query_gradient, grad_key, grad_value, grad_pos_keys
```

```python
import functools

import jax
import jax.numpy as jnp
from jax import lax
from jax.experimental import pallas as pl
from jax.experimental.pallas import tpu as pltpu
from jax.sharding import PartitionSpec as P

DH = 64
W = 128
F32 = jnp.float32
BF16 = jnp.bfloat16


def mm(a, b):
    return jnp.dot(a, b, preferred_element_type=F32)


def mm_nt(a, b):
    return lax.dot_general(a, b, (((1,), (1,)), ((), ())), preferred_element_type=F32)


def mm_tn(a, b):
    return lax.dot_general(a, b, (((0,), (0,)), ((), ())), preferred_element_type=F32)


def iota(shape, axis):
    return lax.broadcasted_iota(jnp.int32, shape, axis)


def shear(x, frames):
    rows = [
        pltpu.roll(x[r : r + frames], frames + 1, 1, stride=1, stride_axis=0)
        for r in range(0, x.shape[0], frames)
    ]
    return jnp.concatenate(rows, axis=0)


def unit(q, k, v, g, k_prev, v_prev, band, bias_c, bias_p):
    frames = q[0].shape[0]
    span = 2 * frames
    factor = DH**-0.5
    lane = iota((frames, W), 1)
    head_mask = [(lane < DH).astype(F32).astype(BF16), (lane >= DH).astype(F32).astype(BF16)]

    def stack(x):
        return jnp.concatenate([x * head_mask[0], x * head_mask[1]], axis=0)

    out_i, in_i = iota((span, span), 0), iota((span, span), 1)

    def permutation(hit):
        return hit.astype(F32).astype(BF16)

    band0, band1 = band[:span], band[span:]
    band1_swapped = jnp.concatenate([band1[frames:], band1[:frames]], axis=0)
    flip = permutation(in_i + out_i == span - 1)
    band0_rev = mm(flip, band0).astype(BF16)
    band1_rev = mm(flip, band1_swapped).astype(BF16)

    row2 = iota((2 * frames, span), 0) & (frames - 1)
    col2 = iota((2 * frames, span), 1)
    forward_mask = (col2 + row2 >= frames - 1) & (col2 + row2 <= span - 2)
    offset = col2 - row2
    back_mask = (offset >= 1) & (offset <= frames)
    back0 = back_mask.astype(F32).astype(BF16)
    back1 = (~back_mask).astype(F32).astype(BF16)

    dq, dk, dv, qp_all, d0_all, d1_all = [], [], [], [], [], []
    for b in range(2):
        before_k = k_prev if b == 0 else k[0]
        before_v = v_prev if b == 0 else v[0]
        kw = jnp.concatenate([k[b], before_k], axis=0)
        vw = jnp.concatenate([v[b], before_v], axis=0)
        qf = q[b].astype(F32)
        qc = stack((qf + bias_c).astype(BF16))
        qp = stack((qf + bias_p).astype(BF16))
        gs = stack(g[b])
        content = mm_nt(qc, kw)
        merged = jnp.where(forward_mask, mm_nt(qp, band0_rev), mm_nt(qp, band1_rev))
        scores = (content + shear(merged, frames)) * factor
        e = jnp.exp(scores - jnp.max(scores, axis=1, keepdims=True))
        gw = mm_nt(gs, vw)
        inverse = 1.0 / jnp.sum(e, axis=1, keepdims=True)
        attention = e * inverse
        delta = jnp.sum(attention * gw, axis=1, keepdims=True)
        ds = (attention * (gw - delta) * factor).astype(BF16)
        placed = shear(mm(ds, flip), frames).astype(BF16)
        d0, d1 = placed * back0, placed * back1
        lhs = jnp.concatenate([ds, d0, d1], axis=1)
        rhs = jnp.concatenate([kw, band0, band1_swapped], axis=0)
        full = mm(lhs, rhs)
        dq.append(jnp.where(lane < DH, full[:frames], full[frames:]).astype(BF16))
        dk.append(mm_tn(ds, qc))
        dv.append(mm_tn(attention.astype(BF16), gs))
        qp_all.append(qp)
        d0_all.append(d0)
        d1_all.append(d1)
    qp_all = jnp.concatenate(qp_all, axis=0)
    g0 = mm_tn(jnp.concatenate(d0_all, axis=0), qp_all).astype(BF16)
    g1 = mm_tn(jnp.concatenate(d1_all, axis=0), qp_all).astype(BF16)
    g_band = jnp.concatenate([g0, g1[frames:], g1[:frames]], axis=0)
    return dq, dk, dv, g_band


def main_body(count, meta, *refs):
    own, sib = refs[0:4], refs[4:8]
    kp0, kp1, vp0, vp1, bias_c, bias_p = refs[8:14]
    bands = refs[14 : 14 + count]
    dq_own, dq_sib, tot_own, tot_sib, back = refs[14 + count : 19 + count]
    g_bands = refs[19 + count : 19 + 2 * count]
    x_scr, band_scr, gband_scr, dq_scr, tot_scr = refs[19 + 2 * count :]
    core = meta[0]
    step = pl.program_id(0)
    for n in range(4):
        x_scr[n, core] = own[n][...]
        x_scr[n, 1 - core] = sib[n][...]
    for n in range(count):

        @pl.when(step == n)
        def _():
            band_scr[...] = bands[n][...]

    pairs = [[x_scr[n, 0], x_scr[n, 1]] for n in range(4)]
    dq, dk, dv, g_band = unit(
        *pairs,
        kp0[...] + kp1[...],
        vp0[...] + vp1[...],
        band_scr[...],
        bias_c[...],
        bias_p[...],
    )
    frames = dq[0].shape[0]
    for b in range(2):
        dq_scr[b] = dq[b]
        for n, term in enumerate((dk, dv)):
            own_term = term[b][:frames]
            if b == 0:
                own_term = own_term + term[1][frames:].astype(BF16).astype(F32)
                back[n] = term[0][frames:].astype(BF16)
            tot_scr[b, n] = own_term
    dq_own[...] = dq_scr[core]
    dq_sib[...] = dq_scr[1 - core]
    tot_own[...] = tot_scr[core]
    tot_sib[...] = tot_scr[1 - core]
    gband_scr[...] = g_band
    for n in range(count):

        @pl.when(step == n)
        def _():
            g_bands[n][...] = gband_scr[...]


def main_call(meta, own, sib, prevs, biases, bands, frames, half):
    count = len(bands)
    rows = bands[0].shape[0]
    wide = pl.BlockSpec((frames, W), lambda s, m: (0, m[1] + (m[2] ^ s)))
    narrow = pl.BlockSpec((frames, W), lambda s, m: (0, m[2] ^ s))
    double = pl.BlockSpec((2, frames, W), lambda s, m: (0, 0, m[2] ^ s))
    bias = pl.BlockSpec((1, W), lambda s, m: (0, m[1] + (m[2] ^ s)))
    whole = pl.BlockSpec((rows, W), lambda s, m: (0, 0))
    return pl.pallas_call(
        functools.partial(main_body, count),
        grid_spec=pltpu.PrefetchScalarGridSpec(
            num_scalar_prefetch=1,
            grid=(count,),
            in_specs=[wide] * 8 + [narrow] * 4 + [bias] * 2 + [whole] * count,
            out_specs=[narrow, narrow, double, double, double] + [whole] * count,
            scratch_shapes=[
                pltpu.VMEM((4, 2, frames, W), BF16),
                pltpu.VMEM((rows, W), BF16),
                pltpu.VMEM((rows, W), BF16),
                pltpu.VMEM((2, frames, W), BF16),
                pltpu.VMEM((2, 2, frames, W), F32),
            ],
        ),
        out_shape=[
            jax.ShapeDtypeStruct((frames, half), BF16),
            jax.ShapeDtypeStruct((frames, half), BF16),
            jax.ShapeDtypeStruct((2, frames, half), F32),
            jax.ShapeDtypeStruct((2, frames, half), F32),
            jax.ShapeDtypeStruct((2, frames, half), BF16),
        ]
        + [jax.ShapeDtypeStruct((rows, W), BF16)] * count,
        compiler_params=pltpu.CompilerParams(vmem_limit_bytes=48 * 2**20),
        name="attention_backward",
    )(meta, *own, *sib, *prevs, *biases, *bands)


def sum_split_body(parts, pieces, meta, *refs):
    total = refs[0][...].astype(F32)
    for n in range(1, parts):
        total = total + refs[n][...].astype(F32)
    scr = refs[-1]
    scr[...] = total
    outs = refs[parts:-1]
    rows = outs[0].shape[0]
    for n in range(pieces):
        at = lax.rem(meta[3] + n, pieces) * rows
        outs[n][...] = scr[pl.ds(pl.multiple_of(at, rows), rows)].astype(outs[n].dtype)


def sum_split(meta, terms, pieces, dtypes):
    rows = terms[0].shape[0]
    return pl.pallas_call(
        functools.partial(sum_split_body, len(terms), pieces),
        in_specs=[pl.BlockSpec(memory_space=pltpu.SMEM)] + [pl.BlockSpec()] * len(terms),
        out_shape=[jax.ShapeDtypeStruct((rows // pieces, W), d) for d in dtypes],
        scratch_shapes=[pltpu.VMEM((rows, W), F32)],
        name="band_sum",
    )(meta, *terms)


def sum_plane_body(parts, meta, *refs):
    total = refs[0][...].astype(F32)
    for n in range(1, parts):
        total = total + refs[n][...].astype(F32)
    own, same, cross, scr = refs[parts:]
    scr[...] = total
    rows = own.shape[0]
    mine = scr[pl.ds(pl.multiple_of(meta[0] * rows, rows), rows)]
    own[...] = mine
    same[...] = mine.astype(BF16)
    cross[...] = scr[pl.ds(pl.multiple_of((1 - meta[0]) * rows, rows), rows)].astype(BF16)


def sum_plane(meta, terms):
    rows = terms[0].shape[0] // 2
    return pl.pallas_call(
        functools.partial(sum_plane_body, len(terms)),
        in_specs=[pl.BlockSpec(memory_space=pltpu.SMEM)] + [pl.BlockSpec()] * len(terms),
        out_shape=[jax.ShapeDtypeStruct((rows, W), d) for d in (F32, BF16, BF16)],
        scratch_shapes=[pltpu.VMEM((2 * rows, W), F32)],
        name="plane_sum",
    )(meta, *terms)


def rows_final_body(meta, dq_own, dq_sib, tot_own, tot_sib, back0, back1, dq, dk, dv):
    core = meta[0]
    half = dq_own.shape[1]
    mine = pl.ds(pl.multiple_of(core * half, half), half)
    other = pl.ds(pl.multiple_of((1 - core) * half, half), half)
    dq[:, mine] = dq_own[...]
    dq[:, other] = dq_sib[...]
    for n, out in enumerate((dk, dv)):
        back = jnp.concatenate([back0[n], back1[n]], axis=1).astype(F32)
        for part, (columns, which) in enumerate(((mine, tot_own), (other, tot_sib))):
            at = core if part == 0 else 1 - core
            back_part = jnp.where(at == 0, back[:, :half], back[:, half:])
            out[:, columns] = (which[n] + back_part).astype(BF16)


def rows_final(meta, *arrays):
    frames, half = arrays[0].shape
    return pl.pallas_call(
        rows_final_body,
        in_specs=[pl.BlockSpec(memory_space=pltpu.SMEM)] + [pl.BlockSpec()] * len(arrays),
        out_shape=[jax.ShapeDtypeStruct((frames, 2 * half), BF16)] * 3,
        name="rows_final",
    )(meta, *arrays)


def band_final_body(groups, meta, *refs):
    out = refs[-1]
    core, low = meta[0], meta[2]
    half = out.shape[1] // 2
    for n in range(2 * groups):
        k, other = n // 2, n % 2
        side = (core if other == 0 else 1 - core) * half
        at = side + (low ^ k) * W
        out[:, pl.ds(pl.multiple_of(at, W), W)] = refs[n][...].astype(F32)


def band_final(meta, pieces, width):
    return pl.pallas_call(
        functools.partial(band_final_body, len(pieces) // 2),
        in_specs=[pl.BlockSpec(memory_space=pltpu.SMEM)] + [pl.BlockSpec()] * len(pieces),
        out_shape=jax.ShapeDtypeStruct((pieces[0].shape[0], width), F32),
        name="band_final",
    )(meta, *pieces)


def local(query_rows, key_rows, value_rows, grad_out, pos_keys, bias_content, bias_position):
    n_dp, n_blk = lax.axis_size("dp"), lax.axis_size("blk")
    n_z = n_blk // 2
    frames, width = query_rows.shape[1], query_rows.shape[2]
    half = width // 2
    groups = half // W
    share = pos_keys.shape[0]
    dp, blk = lax.axis_index("dp"), lax.axis_index("blk")
    core, z, low = blk % 2, blk // 2, dp % groups
    meta = jnp.stack([core, core * groups, low, z]).astype(jnp.int32)

    def blk_permute(x, pairs):
        return lax.ppermute(x, "blk", pairs)

    def to_sibling(x):
        return blk_permute(x, [(s, s ^ 1) for s in range(n_blk)])

    def to_z(x, steps):
        return blk_permute(x, [(s, (s + 2 * steps) % n_blk) for s in range(n_blk)])

    def plane_permute(x, k, cross):
        pairs = []
        for d in range(n_dp):
            for s in range(n_blk):
                pairs.append((d * n_blk + s, (d ^ k) * n_blk + (s ^ cross)))
        return lax.ppermute(x, ("dp", "blk"), pairs)

    own = [x[0] for x in (query_rows, key_rows, value_rows, grad_out)]

    columns = lax.dynamic_slice_in_dim(pos_keys.reshape(share, 2, half), low * W, W, 2)
    columns = jnp.broadcast_to(columns.transpose(1, 0, 2)[None], (n_z, 2, share, W))
    band = lax.all_to_all(columns.reshape(n_blk, share, W), "blk", 0, 0, tiled=True)
    band = band.reshape(n_blk * share, W)

    sib = [to_sibling(x) for x in own]
    odd = [s for s in range(n_blk) if s % 2]
    prevs = []
    for x in own[1:3]:
        for side in range(2):
            pairs = [(s, (s + 1 + side) % n_blk) for s in odd]
            prevs.append(blk_permute(x[:, side * half : (side + 1) * half], pairs))
    bands = [band] + [plane_permute(band, k, 0) for k in range(1, groups)]
    biases = [bias_content.reshape(1, width), bias_position.reshape(1, width)]

    dq_own, dq_sib, tot_own, tot_sib, back, *g_bands = main_call(
        meta, own, sib, prevs, biases, bands, frames, half
    )

    terms = [g_bands[0]] + [plane_permute(g_bands[k], k, 0) for k in range(1, groups)]
    dq_sib, tot_sib = to_sibling(dq_sib), to_sibling(tot_sib)
    back0 = blk_permute(back, [(s, (s - 1) % n_blk) for s in range(0, n_blk, 2)])
    back1 = blk_permute(back, [(s, (s - 2) % n_blk) for s in odd])

    step = groups
    while step < n_dp:
        merged = sum((t.astype(F32) for t in terms), 0.0).astype(BF16)
        terms = [merged, plane_permute(merged, step, 0)]
        step *= 2
    pieces = sum_split(meta, terms, n_z, [F32] + [BF16] * (n_z - 1))
    pieces = [pieces[0]] + [to_z(pieces[k], k) for k in range(1, n_z)]
    mine, same, cross = sum_plane(meta, pieces)
    found = []
    for k in range(groups):
        found.append(mine if k == 0 else plane_permute(same, k, 0))
        found.append(plane_permute(cross, k, 1))
    grad_pos = band_final(meta, found, width)
    dq, dk, dv = rows_final(meta, dq_own, dq_sib, tot_own, tot_sib, back0, back1)
    return dq[None], dk[None], dv[None], grad_pos


def solution(mesh):
    placed = (
        P("dp", "blk", None),
        P("dp", "blk", None),
        P("dp", "blk", None),
        P("dp", "blk", None),
        P("blk", None),
        P(),
        P(),
    )
    return jax.shard_map(
        local,
        mesh=mesh,
        in_specs=placed,
        out_specs=(
            P("dp", "blk", None),
            P("dp", "blk", None),
            P("dp", "blk", None),
            P("blk", None),
        ),
        check_vma=False,
    )
```

```python
import functools

import jax
import jax.numpy as jnp
from jax import lax
from jax.experimental import pallas as pl
from jax.experimental.pallas import tpu as pltpu
from jax.sharding import Mesh
from jax.sharding import PartitionSpec as P

DH = 64
W = 128
GROUPS = 4
F32 = jnp.float32
BF16 = jnp.bfloat16
VMEM = pl.BlockSpec(memory_space=pltpu.VMEM)


def mm(a, b):
    return jnp.dot(a, b, preferred_element_type=F32)


def mm_nt(a, b):
    return lax.dot_general(a, b, (((1,), (1,)), ((), ())), preferred_element_type=F32)


def iota(shape, axis):
    return lax.broadcasted_iota(jnp.int32, shape, axis)


def as_bf16(hit):
    return hit.astype(F32).astype(BF16)


def shear(x, frames):
    rows = [
        pltpu.roll(x[r : r + frames], frames + 1, 1, stride=1, stride_axis=0)
        for r in range(0, x.shape[0], frames)
    ]
    return jnp.concatenate(rows, axis=0)


def columns(start, size):
    return pl.ds(pl.multiple_of(start, W), size)


class Masks:
    def __init__(self, frames):
        span = 2 * frames
        lane = iota((frames, W), 1)
        sub = iota((W, frames), 0)
        self.first = lane < DH
        self.lanes = [as_bf16(lane < DH), as_bf16(lane >= DH)]
        self.subs = [as_bf16(sub < DH), as_bf16(sub >= DH)]
        self.flip = as_bf16(iota((span, span), 0) + iota((span, span), 1) == span - 1)
        row = iota((span, span), 0) & (frames - 1)
        col = iota((span, span), 1)
        self.forward = (col + row >= frames - 1) & (col + row <= span - 2)
        back = (col - row >= 1) & (col - row <= frames)
        self.back = [as_bf16(back), as_bf16(~back)]

    def stack(self, x):
        return jnp.concatenate([x * self.lanes[0], x * self.lanes[1]], axis=0)

    def stack_t(self, x):
        x = x.T
        return jnp.concatenate([x * self.subs[0], x * self.subs[1]], axis=1)


def unit(masks, q, k, v, g, k_prev, v_prev, band, bias_c, bias_p):
    frames = q[0].shape[0]
    span = 2 * frames
    factor = DH**-0.5
    band0, band1 = band[:span], band[span:]
    band1_swapped = jnp.concatenate([band1[frames:], band1[:frames]], axis=0)
    band0_rev = mm(masks.flip, band0).astype(BF16)
    band1_rev = mm(masks.flip, band1_swapped).astype(BF16)

    dq, dk, dv, qp_t, d0_all, d1_all = [], [], [], [], [], []
    for b in range(2):
        before_k = k_prev if b == 0 else k[0]
        before_v = v_prev if b == 0 else v[0]
        kw = jnp.concatenate([k[b], before_k], axis=0)
        vw = jnp.concatenate([v[b], before_v], axis=0)
        qf = q[b].astype(F32)
        qc = (qf + bias_c).astype(BF16)
        qp = (qf + bias_p).astype(BF16)
        qp_stack = masks.stack(qp)
        content = mm_nt(masks.stack(qc), kw)
        merged = jnp.where(masks.forward, mm_nt(qp_stack, band0_rev), mm_nt(qp_stack, band1_rev))
        scores = (content + shear(merged, frames)) * factor
        e = jnp.exp(scores - jnp.max(scores, axis=1, keepdims=True))
        gw = mm_nt(masks.stack(g[b]), vw)
        attention = e * (1.0 / jnp.sum(e, axis=1, keepdims=True))
        delta = jnp.sum(attention * gw, axis=1, keepdims=True)
        ds = (attention * (gw - delta) * factor).astype(BF16)
        placed = shear(mm(ds, masks.flip), frames).astype(BF16)
        d0, d1 = placed * masks.back[0], placed * masks.back[1]
        lhs = jnp.concatenate([ds, d0, d1], axis=1)
        rhs = jnp.concatenate([kw, band0, band1_swapped], axis=0)
        full = mm(lhs, rhs)
        dq.append(jnp.where(masks.first, full[:frames], full[frames:]).astype(BF16))
        dk.append(mm(masks.stack_t(qc), ds))
        dv.append(mm(masks.stack_t(g[b]), attention.astype(BF16)))
        qp_t.append(masks.stack_t(qp))
        d0_all.append(d0)
        d1_all.append(d1)
    qp_t = jnp.concatenate(qp_t, axis=1)
    g0 = mm(qp_t, jnp.concatenate(d0_all, axis=0)).astype(BF16)
    g1 = mm(qp_t, jnp.concatenate(d1_all, axis=0)).astype(BF16)
    g_band = jnp.concatenate([g0, g1[:, frames:], g1[:, :frames]], axis=1)
    return dq, dk, dv, g_band


def main_body(*refs):
    own = refs[0:4]
    sib, prev0, prev1, bias_c, bias_p, bands = refs[4:10]
    out_own, out_sib, back, g_bands, x_scr, out_scr = refs[10:]
    core = lax.axis_index("core")
    frames, half = back.shape[1:]
    masks = Masks(frames)
    for group in range(half // W):
        at = group * W
        here = columns(core * half + at, W)
        for n in range(4):
            x_scr[group, n, core] = own[n][:, here]
            x_scr[group, n, 1 - core] = sib[n, :, at : at + W]
        dq, dk, dv, g_bands[group] = unit(
            masks,
            *[[x_scr[group, n, 0], x_scr[group, n, 1]] for n in range(4)],
            prev0[0, :, at : at + W] + prev1[0, :, at : at + W],
            prev0[1, :, at : at + W] + prev1[1, :, at : at + W],
            bands[group],
            bias_c[:, here],
            bias_p[:, here],
        )
        for b in range(2):
            out_scr[group, b, 0] = dq[b].astype(F32)
            for n, term in enumerate((dk, dv)):
                total = term[b][:, :frames].T
                if b == 0:
                    total = total + term[1][:, frames:].astype(BF16).T.astype(F32)
                    back[n, :, at : at + W] = term[0][:, frames:].astype(BF16).T
                out_scr[group, b, 1 + n] = total
        out_own[:, :, at : at + W] = out_scr[group, core]
        out_sib[:, :, at : at + W] = out_scr[group, 1 - core]


def main_call(own, sib, prevs, biases, bands):
    frames, half = sib.shape[1:]
    groups, rows = bands.shape[:2]
    return pl.pallas_call(
        main_body,
        in_specs=[VMEM] * 10,
        out_specs=[VMEM] * 4,
        out_shape=[
            jax.ShapeDtypeStruct((3, frames, half), F32),
            jax.ShapeDtypeStruct((3, frames, half), F32),
            jax.ShapeDtypeStruct((2, frames, half), BF16),
            jax.ShapeDtypeStruct((groups, W, rows), BF16),
        ],
        scratch_shapes=[
            pltpu.VMEM((groups, 4, 2, frames, W), BF16),
            pltpu.VMEM((groups, 2, 3, frames, W), F32),
        ],
        compiler_params=pltpu.CompilerParams(vmem_limit_bytes=40 * 2**20),
        name="attention_backward",
    )(*own, sib, *prevs, *biases, bands)


def prep_body(q, k, v, g, sib, prev0, prev1):
    half = sib.shape[2]
    core = lax.axis_index("core")
    there = columns((1 - core) * half, half)
    for n, x in enumerate((q, k, v, g)):
        sib[n] = x[:, there]
    for n, x in enumerate((k, v)):
        prev0[n] = x[:, :half]
        prev1[n] = x[:, half:]


def prep(own):
    frames, width = own[0].shape
    return pl.pallas_call(
        prep_body,
        in_specs=[VMEM] * 4,
        out_specs=[VMEM] * 3,
        out_shape=[jax.ShapeDtypeStruct((n, frames, width // 2), BF16) for n in (4, 2, 2)],
        name="prepare",
    )(*own)


def summed(ref):
    total = ref[0].astype(F32)
    for n in range(1, ref.shape[0]):
        total = total + ref[n].astype(F32)
    return total


def band_sum_body(terms, out):
    pieces, rows = out.shape[:2]
    out[...] = summed(terms).T.reshape(pieces, rows, W).astype(BF16)


def band_sum(terms, pieces):
    rows = terms.shape[2]
    return pl.pallas_call(
        band_sum_body,
        in_specs=[VMEM],
        out_specs=VMEM,
        out_shape=jax.ShapeDtypeStruct((pieces, rows // pieces, W), BF16),
        name="band_sum",
    )(terms)


def plane_sum_body(terms, out):
    total = summed(terms).astype(BF16)
    rows = out.shape[1]
    for n in range(out.shape[0]):
        out[n] = total[(n % 2) * rows : (n % 2 + 1) * rows]


def plane_sum(terms):
    return pl.pallas_call(
        plane_sum_body,
        in_specs=[VMEM],
        out_specs=VMEM,
        out_shape=jax.ShapeDtypeStruct((2 * GROUPS, terms.shape[1] // 2, W), BF16),
        name="plane_sum",
    )(terms)


def rows_final_body(own, sib, back0, back1, dq, dk, dv):
    core = lax.axis_index("core")
    half = own.shape[2]
    mine, other = columns(core * half, half), columns((1 - core) * half, half)
    dq[:, mine] = own[0].astype(BF16)
    dq[:, other] = sib[0].astype(BF16)
    for n, out in enumerate((dk, dv)):
        back = [back0[n].astype(F32), back1[n].astype(F32)]
        out[:, mine] = (own[1 + n] + jnp.where(core == 0, back[0], back[1])).astype(BF16)
        out[:, other] = (sib[1 + n] + jnp.where(core == 0, back[1], back[0])).astype(BF16)


def rows_final(*arrays):
    frames, half = arrays[0].shape[1:]
    return pl.pallas_call(
        rows_final_body,
        in_specs=[VMEM] * 4,
        out_specs=[VMEM] * 3,
        out_shape=[jax.ShapeDtypeStruct((frames, 2 * half), BF16)] * 3,
        name="rows_final",
    )(*arrays)


def band_final_body(pieces, out):
    half = out.shape[1] // 2
    for n in range(pieces.shape[0]):
        at = (n % 2) * half + (n // 2) * W
        out[:, at : at + W] = pieces[n].astype(F32)


def band_final(pieces, width):
    return pl.pallas_call(
        band_final_body,
        in_specs=[VMEM],
        out_specs=VMEM,
        out_shape=jax.ShapeDtypeStruct((pieces.shape[1], width), F32),
        name="band_final",
    )(pieces)


def local(query_rows, key_rows, value_rows, grad_out, pos_keys, bias_content, bias_position):
    n_high, n_z = lax.axis_size("dh"), lax.axis_size("z")
    width = query_rows.shape[2]
    half = width // 2
    share = pos_keys.shape[0]
    chain = ("z", "core")
    n_blk = 2 * n_z

    def exchange(x, axes):
        return lax.all_to_all(x, axes, 0, 0, tiled=True)

    def to_sibling(x):
        return lax.ppermute(x, "core", [(0, 1), (1, 0)])

    low = lax.axis_index("dl")
    mine = lax.dynamic_slice_in_dim(pos_keys.reshape(share, 2, half), low * W, W, 2)
    mine = jnp.broadcast_to(mine.transpose(1, 0, 2)[None], (n_z, 2, share, W))
    band = exchange(mine.reshape(n_blk, share, W), chain).reshape(n_blk * share, W)

    own = [x[0] for x in (query_rows, key_rows, value_rows, grad_out)]
    sib, prev0, prev1 = prep(own)
    odd = range(1, n_blk, 2)
    prev0 = lax.ppermute(prev0, chain, [(s, (s + 1) % n_blk) for s in odd])
    prev1 = lax.ppermute(prev1, chain, [(s, (s + 2) % n_blk) for s in odd])
    sib = to_sibling(sib)
    bands = exchange(jnp.broadcast_to(band[None], (GROUPS, *band.shape)), "dl")
    biases = [bias_content.reshape(1, width), bias_position.reshape(1, width)]

    out_own, out_sib, back, g_bands = main_call(own, sib, (prev0, prev1), biases, bands)

    terms = exchange(g_bands, "dl")
    out_sib = to_sibling(out_sib)
    back0 = lax.ppermute(back, chain, [(s, (s - 1) % n_blk) for s in range(0, n_blk, 2)])
    back1 = lax.ppermute(back, chain, [(s, (s - 2) % n_blk) for s in odd])

    step = 1
    while step < n_high:
        merged = jnp.sum(terms.astype(F32), axis=0).astype(BF16)
        other = lax.ppermute(merged, "dh", [(s, s ^ step) for s in range(n_high)])
        terms = jnp.stack([merged, other])
        step *= 2
    pieces = exchange(band_sum(terms, n_z), "z")
    pieces = exchange(plane_sum(pieces), ("dl", "core"))
    dq, dk, dv = rows_final(out_own, out_sib, back0, back1)
    grad_pos = band_final(pieces, width)
    return dq[None], dk[None], dv[None], grad_pos


def solution(mesh):
    n_dp, n_blk = mesh.shape["dp"], mesh.shape["blk"]
    fine = Mesh(
        mesh.devices.reshape(n_dp // GROUPS, GROUPS, n_blk // 2, 2), ("dh", "dl", "z", "core")
    )
    rows = P(("dh", "dl"), ("z", "core"), None)
    band = P(("z", "core"), None)
    return jax.shard_map(
        local,
        mesh=fine,
        in_specs=(rows, rows, rows, rows, band, P(), P()),
        out_specs=(rows, rows, rows, band),
        check_vma=False,
    )
```

```python
import functools

import jax
import jax.numpy as jnp
from jax import lax
from jax.experimental import pallas as pl
from jax.experimental.pallas import tpu as pltpu
from jax.sharding import Mesh
from jax.sharding import PartitionSpec as P

DH = 64
W = 128
PLANE = 4
MIB = 2**20
F32 = jnp.float32
BF16 = jnp.bfloat16


def mm(a, b):
    return jnp.dot(a, b, preferred_element_type=F32)


def mm_nt(a, b):
    return lax.dot_general(a, b, (((1,), (1,)), ((), ())), preferred_element_type=F32)


def iota(shape, axis):
    return lax.broadcasted_iota(jnp.int32, shape, axis)


def as_bf16(hit):
    return hit.astype(F32).astype(BF16)


def shear(x, frames):
    rows = [
        pltpu.roll(x[r : r + frames], frames + 1, 1, stride=1, stride_axis=0)
        for r in range(0, x.shape[0], frames)
    ]
    return jnp.concatenate(rows, axis=0)


def columns(start, size):
    return pl.ds(pl.multiple_of(start, W), size)


class Masks:
    def __init__(self, frames):
        span = 2 * frames
        lane = iota((frames, W), 1)
        sub = iota((W, frames), 0)
        self.first = lane < DH
        self.lanes = [as_bf16(lane < DH), as_bf16(lane >= DH)]
        self.subs = [as_bf16(sub < DH), as_bf16(sub >= DH)]
        self.flip = as_bf16(iota((span, span), 0) + iota((span, span), 1) == span - 1)
        row = iota((span, span), 0) & (frames - 1)
        col = iota((span, span), 1)
        self.forward = (col + row >= frames - 1) & (col + row <= span - 2)
        back = (col - row >= 1) & (col - row <= frames)
        self.back = [as_bf16(back), as_bf16(~back)]

    def stack(self, x):
        return jnp.concatenate([x * self.lanes[0], x * self.lanes[1]], axis=0)

    def stack_t(self, x):
        x = x.T
        return jnp.concatenate([x * self.subs[0], x * self.subs[1]], axis=1)


def unit(masks, q, k, v, g, k_prev, v_prev, band, bias_c, bias_p):
    frames = q[0].shape[0]
    span = 2 * frames
    factor = DH**-0.5
    band0, band1 = band[:span], band[span:]
    band1_swapped = jnp.concatenate([band1[frames:], band1[:frames]], axis=0)
    band0_rev = mm(masks.flip, band0).astype(BF16)
    band1_rev = mm(masks.flip, band1_swapped).astype(BF16)

    dq, dk, dv, qp_t, d0_all, d1_all = [], [], [], [], [], []
    for b in range(2):
        before_k = k_prev if b == 0 else k[0]
        before_v = v_prev if b == 0 else v[0]
        kw = jnp.concatenate([k[b], before_k], axis=0)
        vw = jnp.concatenate([v[b], before_v], axis=0)
        qf = q[b].astype(F32)
        qc = (qf + bias_c).astype(BF16)
        qp = (qf + bias_p).astype(BF16)
        qp_stack = masks.stack(qp)
        content = mm_nt(masks.stack(qc), kw)
        merged = jnp.where(masks.forward, mm_nt(qp_stack, band0_rev), mm_nt(qp_stack, band1_rev))
        scores = (content + shear(merged, frames)) * factor
        e = jnp.exp(scores - jnp.max(scores, axis=1, keepdims=True))
        gw = mm_nt(masks.stack(g[b]), vw)
        attention = e * (1.0 / jnp.sum(e, axis=1, keepdims=True))
        delta = jnp.sum(attention * gw, axis=1, keepdims=True)
        ds = (attention * (gw - delta) * factor).astype(BF16)
        placed = shear(mm(ds, masks.flip), frames).astype(BF16)
        d0, d1 = placed * masks.back[0], placed * masks.back[1]
        lhs = jnp.concatenate([ds, d0, d1], axis=1)
        rhs = jnp.concatenate([kw, band0, band1_swapped], axis=0)
        full = mm(lhs, rhs)
        dq.append(jnp.where(masks.first, full[:frames], full[frames:]).astype(BF16))
        dk.append(mm(masks.stack_t(qc), ds))
        dv.append(mm(masks.stack_t(g[b]), attention.astype(BF16)))
        qp_t.append(masks.stack_t(qp))
        d0_all.append(d0)
        d1_all.append(d1)
    qp_t = jnp.concatenate(qp_t, axis=1)
    g0 = mm(qp_t, jnp.concatenate(d0_all, axis=0)).astype(BF16)
    g1 = mm(qp_t, jnp.concatenate(d1_all, axis=0)).astype(BF16)
    g_band = jnp.concatenate([g0, g1[:, frames:], g1[:, :frames]], axis=1)
    return dq, dk, dv, g_band


def call(body, name, out_shape, scratch=(), limit=8):
    return pl.pallas_call(
        body,
        out_shape=out_shape,
        scratch_shapes=list(scratch),
        compiler_params=pltpu.CompilerParams(vmem_limit_bytes=limit * MIB),
        name=name,
    )


def shape(dims, dtype):
    return jax.ShapeDtypeStruct(tuple(dims), dtype)


def pair_of():
    low = lax.axis_index("dl")
    return (low & 1) ^ (low >> 1)


def main_body(steps, *refs):
    own = refs[0:4]
    sib, prev0, prev1, bias_c, bias_p = refs[4:9]
    bands = refs[9:13]
    out_own, out_sib, back = refs[13:16]
    g_parts = refs[16 : 16 + steps]
    x_scr, p_scr, band_scr, out_scr, back_scr, g_scr = refs[16 + steps :]
    core, z, pair = lax.axis_index("core"), lax.axis_index("z"), pair_of()
    frames, half = back.shape[1:]
    span = half // 2
    share = band_scr.shape[3]
    masks = Masks(frames)
    for slot in range(2):
        for j in range(span // W):
            n_group = slot * (span // W) + j
            inside = (pair ^ slot) * span + j * W
            here = columns(core * half + inside, W)
            mine = columns(inside, W)
            for n in range(4):
                x_scr[n_group, n, core] = own[n][:, here]
                x_scr[n_group, n, 1 - core] = sib[n, :, mine]
            for n in range(2):
                p_scr[n_group, n] = prev0[n, :, mine] + prev1[n, :, mine]
            for n in range(2):
                part = bands[2 * slot + n][:, j * W : (j + 1) * W].reshape(steps, share, W)
                band_scr[n_group, :, core if n == 0 else 1 - core] = part
            dq, dk, dv, g_band = unit(
                masks,
                *[[x_scr[n_group, n, 0], x_scr[n_group, n, 1]] for n in range(4)],
                p_scr[n_group, 0],
                p_scr[n_group, 1],
                band_scr[n_group].reshape(steps * 2 * share, W),
                bias_c[:, here],
                bias_p[:, here],
            )
            for b in range(2):
                out_scr[n_group, b, 0] = dq[b].astype(F32)
                for n, term in enumerate((dk, dv)):
                    total = term[b][:, :frames].T
                    if b == 0:
                        total = total + term[1][:, frames:].astype(BF16).T.astype(F32)
                        back_scr[n] = term[0][:, frames:].astype(BF16).T
                    out_scr[n_group, b, 1 + n] = total
            for n in range(3):
                out_own[n, :, mine] = out_scr[n_group, core, n]
                out_sib[n, :, mine] = out_scr[n_group, 1 - core, n]
            for n in range(2):
                back[n, :, mine] = back_scr[n]
            for n in range(steps):
                g_scr[n_group, n] = g_band[:, n * 2 * share : (n + 1) * 2 * share]
            for n in range(steps):
                g_parts[n][mine, :] = g_scr[n_group, lax.rem(z + n, steps)]


def main_call(own, sib, prevs, biases, bands, steps):
    frames, half = sib.shape[1:]
    share = bands[0].shape[0] // steps
    groups = half // W
    return call(
        functools.partial(main_body, steps),
        "attention_backward",
        [
            shape((3, frames, half), F32),
            shape((3, frames, half), F32),
            shape((2, frames, half), BF16),
        ]
        + [shape((half, 2 * share), BF16)] * steps,
        [
            pltpu.VMEM((groups, 4, 2, frames, W), BF16),
            pltpu.VMEM((groups, 2, frames, W), BF16),
            pltpu.VMEM((groups, steps, 2, share, W), BF16),
            pltpu.VMEM((groups, 2, 3, frames, W), F32),
            pltpu.VMEM((2, frames, W), BF16),
            pltpu.VMEM((groups, steps, W, 2 * share), BF16),
        ],
        limit=24,
    )(*own, sib, *prevs, *biases, *bands)


def band_cut_body(table, out):
    half = table.shape[1] // 2
    span = half // 2
    pair = pair_of()
    for n in range(2):
        out[:, n * span : (n + 1) * span] = table[:, columns(n * half + pair * span, span)]


def band_cut(table):
    rows, width = table.shape
    return call(band_cut_body, "band_cut", shape((rows, width // 2), BF16))(table)


def band_pack_body(steps, *refs):
    own, sib = refs[steps:]
    core, z = lax.axis_index("core"), lax.axis_index("z")
    span = own.shape[2]
    for n in range(steps):
        at = lax.rem(z - n + steps, steps)
        own[at] = refs[n][:, columns(core * span, span)]
        sib[at] = refs[n][:, columns((1 - core) * span, span)]


def band_pack(parts):
    rows, width = parts[0].shape
    steps = len(parts)
    out = call(
        functools.partial(band_pack_body, steps),
        "band_pack",
        [shape((steps, rows, width // 2), BF16)] * 2,
    )(*parts)
    return [x.reshape(steps * rows, width // 2) for x in out]


def prep_body(q, k, v, g, sib, prev0, prev1):
    half = sib.shape[2]
    there = columns((1 - lax.axis_index("core")) * half, half)
    for n, x in enumerate((q, k, v, g)):
        sib[n] = x[:, there]
    for n, x in enumerate((k, v)):
        prev0[n] = x[:, :half]
        prev1[n] = x[:, half:]


def prep(own):
    frames, width = own[0].shape
    outs = [shape((n, frames, width // 2), BF16) for n in (4, 2, 2)]
    return call(prep_body, "prepare", outs)(*own)


def summed(refs):
    total = refs[0][...].astype(F32)
    for ref in refs[1:]:
        total = total + ref[...].astype(F32)
    return total


def z_sum_body(*refs):
    refs[-1][...] = summed(refs[:-1]).astype(BF16)


def z_sum(parts):
    return call(z_sum_body, "z_sum", shape(parts[0].shape, BF16))(*parts)


def plane_sum_body(*refs):
    mine, other, scr = refs[-3:]
    rows = mine.shape[0]
    core = lax.axis_index("core")
    scr[...] = summed(refs[:-3]).T.reshape(scr.shape)
    mine[...] = scr[core]
    other[...] = scr[1 - core]


def plane_sum(parts):
    half, rows = parts[0].shape
    return call(
        plane_sum_body,
        "plane_sum",
        [shape((rows // 2, half), F32)] * 2,
        [pltpu.VMEM((2, rows // 2, half), F32)],
    )(*parts)


def rows_final_body(own, sib, back0, back1, dq, dk, dv):
    core = lax.axis_index("core")
    half = own.shape[2]
    mine, other = columns(core * half, half), columns((1 - core) * half, half)
    dq[:, mine] = own[0].astype(BF16)
    dq[:, other] = sib[0].astype(BF16)
    for n, out in enumerate((dk, dv)):
        back = [back0[n].astype(F32), back1[n].astype(F32)]
        out[:, mine] = (own[1 + n] + jnp.where(core == 0, back[0], back[1])).astype(BF16)
        out[:, other] = (sib[1 + n] + jnp.where(core == 0, back[1], back[0])).astype(BF16)


def rows_final(*arrays):
    frames, half = arrays[0].shape[1:]
    return call(rows_final_body, "rows_final", [shape((frames, 2 * half), BF16)] * 3)(*arrays)


def band_final_body(mine, other, out):
    core = lax.axis_index("core")
    half = mine.shape[1]
    out[:, columns(core * half, half)] = mine[...]
    out[:, columns((1 - core) * half, half)] = other[...]


def band_final(mine, other):
    rows, half = mine.shape
    return call(band_final_body, "band_final", shape((rows, 2 * half), F32))(mine, other)


def local(query_rows, key_rows, value_rows, grad_out, pos_keys, bias_content, bias_position):
    n_high, n_z = lax.axis_size("dh"), lax.axis_size("z")
    width = query_rows.shape[2]
    n_blk = 2 * n_z
    chain = ("z", "core")

    def along_z(x, steps):
        return lax.ppermute(x, "z", [(s, (s + steps) % n_z) for s in range(n_z)])

    def to_sibling(x):
        return lax.ppermute(x, "core", [(0, 1), (1, 0)])

    def in_plane(x, flip, cross=0):
        pairs = [
            (2 * d + c, 2 * (d ^ flip) + (c ^ cross)) for d in range(PLANE) for c in range(2)
        ]
        return lax.ppermute(x, ("dl", "core"), pairs)

    cut = band_cut(pos_keys)
    cuts = [cut] + [along_z(cut, k) for k in range(1, n_z)]
    own = [x[0] for x in (query_rows, key_rows, value_rows, grad_out)]
    sib, prev0, prev1 = prep(own)
    sib = to_sibling(sib)
    odd = range(1, n_blk, 2)
    prev0 = lax.ppermute(prev0, chain, [(s, (s + 1) % n_blk) for s in odd])
    prev1 = lax.ppermute(prev1, chain, [(s, (s + 2) % n_blk) for s in odd])
    band_own, band_sib = band_pack(cuts)
    bands = [band_own, to_sibling(band_sib), in_plane(band_own, 1), in_plane(band_sib, 2, 1)]
    biases = [bias_content.reshape(1, width), bias_position.reshape(1, width)]

    out_own, out_sib, back, *g_parts = main_call(own, sib, (prev0, prev1), biases, bands, n_z)

    parts = [g_parts[0]] + [along_z(g_parts[k], k) for k in range(1, n_z)]
    out_sib = to_sibling(out_sib)
    back0 = lax.ppermute(back, chain, [(s, (s - 1) % n_blk) for s in range(0, n_blk, 2)])
    back1 = lax.ppermute(back, chain, [(s, (s - 2) % n_blk) for s in odd])

    total = z_sum(parts)
    step = 1
    while step < n_high:
        pairs = [(s, s ^ step) for s in range(n_high)]
        total = z_sum([total, lax.ppermute(total, "dh", pairs)])
        step *= 2
    mine, other = plane_sum([total] + [in_plane(total, k) for k in range(1, PLANE)])
    other = to_sibling(other)
    dq, dk, dv = rows_final(out_own, out_sib, back0, back1)
    grad_pos = band_final(mine, other)
    return dq[None], dk[None], dv[None], grad_pos


def solution(mesh):
    n_dp, n_blk = mesh.shape["dp"], mesh.shape["blk"]
    fine = Mesh(mesh.devices.reshape(n_dp // PLANE, PLANE, n_blk // 2, 2), ("dh", "dl", "z", "core"))
    rows = P(("dh", "dl"), ("z", "core"), None)
    band = P(("z", "core"), None)
    return jax.shard_map(
        local,
        mesh=fine,
        in_specs=(rows, rows, rows, rows, band, P(), P()),
        out_specs=(rows, rows, rows, band),
        check_vma=False,
    )
```

```python
import functools

import jax
import jax.numpy as jnp
from jax import lax
from jax.experimental import pallas as pl
from jax.experimental.pallas import tpu as pltpu
from jax.sharding import Mesh
from jax.sharding import PartitionSpec as P

DH = 64
W = 128
PLANE = 4
MIB = 2**20
F32 = jnp.float32
BF16 = jnp.bfloat16


def mm(a, b):
    return jnp.dot(a, b, preferred_element_type=F32)


def mm_nt(a, b):
    return lax.dot_general(a, b, (((1,), (1,)), ((), ())), preferred_element_type=F32)


def iota(shape, axis):
    return lax.broadcasted_iota(jnp.int32, shape, axis)


def as_bf16(hit):
    return hit.astype(F32).astype(BF16)


def shear(x, frames):
    rows = [
        pltpu.roll(x[r : r + frames], frames + 1, 1, stride=1, stride_axis=0)
        for r in range(0, x.shape[0], frames)
    ]
    return jnp.concatenate(rows, axis=0)


def columns(start, size):
    return pl.ds(pl.multiple_of(start, W), size)


class Masks:
    def __init__(self, frames):
        span = 2 * frames
        lane = iota((frames, W), 1)
        sub = iota((W, frames), 0)
        self.first = lane < DH
        self.lanes = [as_bf16(lane < DH), as_bf16(lane >= DH)]
        self.subs = [as_bf16(sub < DH), as_bf16(sub >= DH)]
        self.flip = as_bf16(iota((span, span), 0) + iota((span, span), 1) == span - 1)
        row = iota((span, span), 0) & (frames - 1)
        col = iota((span, span), 1)
        self.forward = (col + row >= frames - 1) & (col + row <= span - 2)
        back = (col - row >= 1) & (col - row <= frames)
        self.back = [as_bf16(back), as_bf16(~back)]

    def stack(self, x):
        return jnp.concatenate([x * self.lanes[0], x * self.lanes[1]], axis=0)

    def stack_t(self, x):
        x = x.T
        return jnp.concatenate([x * self.subs[0], x * self.subs[1]], axis=1)


def unit(masks, q, k, v, g, k_prev, v_prev, band, bias_c, bias_p):
    frames = q[0].shape[0]
    span = 2 * frames
    factor = DH**-0.5
    band0, band1 = band[:span], band[span:]
    band1_swapped = jnp.concatenate([band1[frames:], band1[:frames]], axis=0)
    band0_rev = mm(masks.flip, band0).astype(BF16)
    band1_rev = mm(masks.flip, band1_swapped).astype(BF16)

    dq, dk, dv, qp_t, d0_all, d1_all = [], [], [], [], [], []
    for b in range(2):
        before_k = k_prev if b == 0 else k[0]
        before_v = v_prev if b == 0 else v[0]
        kw = jnp.concatenate([k[b], before_k], axis=0)
        vw = jnp.concatenate([v[b], before_v], axis=0)
        qf = q[b].astype(F32)
        qc = (qf + bias_c).astype(BF16)
        qp = (qf + bias_p).astype(BF16)
        qp_stack = masks.stack(qp)
        content = mm_nt(masks.stack(qc), kw)
        merged = jnp.where(masks.forward, mm_nt(qp_stack, band0_rev), mm_nt(qp_stack, band1_rev))
        scores = (content + shear(merged, frames)) * factor
        e = jnp.exp(scores - jnp.max(scores, axis=1, keepdims=True))
        gw = mm_nt(masks.stack(g[b]), vw)
        attention = e * (1.0 / jnp.sum(e, axis=1, keepdims=True))
        delta = jnp.sum(attention * gw, axis=1, keepdims=True)
        ds = (attention * (gw - delta) * factor).astype(BF16)
        placed = shear(mm(ds, masks.flip), frames).astype(BF16)
        d0, d1 = placed * masks.back[0], placed * masks.back[1]
        lhs = jnp.concatenate([ds, d0, d1], axis=1)
        rhs = jnp.concatenate([kw, band0, band1_swapped], axis=0)
        full = mm(lhs, rhs)
        dq.append(jnp.where(masks.first, full[:frames], full[frames:]).astype(BF16))
        dk.append(mm(masks.stack_t(qc), ds))
        dv.append(mm(masks.stack_t(g[b]), attention.astype(BF16)))
        qp_t.append(masks.stack_t(qp))
        d0_all.append(d0)
        d1_all.append(d1)
    qp_t = jnp.concatenate(qp_t, axis=1)
    g0 = mm(qp_t, jnp.concatenate(d0_all, axis=0)).astype(BF16)
    g1 = mm(qp_t, jnp.concatenate(d1_all, axis=0)).astype(BF16)
    g_band = jnp.concatenate([g0, g1[:, frames:], g1[:, :frames]], axis=1)
    return dq, dk, dv, g_band


def call(body, name, out_shape, scratch=(), limit=8, **options):
    return pl.pallas_call(
        body,
        out_shape=out_shape,
        scratch_shapes=list(scratch),
        compiler_params=pltpu.CompilerParams(vmem_limit_bytes=limit * MIB),
        name=name,
        **options,
    )


def shape(dims, dtype):
    return jax.ShapeDtypeStruct(tuple(dims), dtype)


def pair_of():
    low = lax.axis_index("dl")
    return (low & 1) ^ (low >> 1)


def main_body(steps, slot, *refs):
    own = refs[0:4]
    sib, prev0, prev1, bias_c, bias_p = refs[4:9]
    bands = refs[9:11]
    carried, refs = refs[11 : 11 + 3 * slot], refs[11 + 3 * slot :]
    out_own, out_sib, back = refs[:3]
    g_outs = refs[3:-5]
    x_scr, p_scr, band_scr, out_scr, back_scr = refs[-5:]
    core, pair = lax.axis_index("core"), pair_of()
    frames, half = back.shape[1:]
    span = half // 2
    share = band_scr.shape[3]
    masks = Masks(frames)
    done = columns((pair ^ 1 ^ slot) * span, span)
    for source, target in zip(carried, (out_own, out_sib, back)):
        target[:, :, done] = source[:, :, done]
    for j in range(span // W):
        inside = (pair ^ slot) * span + j * W
        here = columns(core * half + inside, W)
        mine = columns(inside, W)
        for n in range(4):
            x_scr[j, n, core] = own[n][:, here]
            x_scr[j, n, 1 - core] = sib[n, :, mine]
        for n in range(2):
            p_scr[j, n] = prev0[n, :, mine] + prev1[n, :, mine]
        for n in range(2):
            part = bands[n][:, j * W : (j + 1) * W].reshape(steps, share, W)
            band_scr[j, :, core if n == 0 else 1 - core] = part
        dq, dk, dv, g_band = unit(
            masks,
            *[[x_scr[j, n, 0], x_scr[j, n, 1]] for n in range(4)],
            p_scr[j, 0],
            p_scr[j, 1],
            band_scr[j].reshape(steps * 2 * share, W),
            bias_c[:, here],
            bias_p[:, here],
        )
        for b in range(2):
            out_scr[j, b, 0] = dq[b].astype(F32)
            for n, term in enumerate((dk, dv)):
                total = term[b][:, :frames].T
                if b == 0:
                    total = total + term[1][:, frames:].astype(BF16).T.astype(F32)
                    back_scr[n] = term[0][:, frames:].astype(BF16).T
                out_scr[j, b, 1 + n] = total
        for n in range(3):
            out_own[n, :, mine] = out_scr[j, core, n]
            out_sib[n, :, mine] = out_scr[j, 1 - core, n]
        for n in range(2):
            back[n, :, mine] = back_scr[n]
        g_outs[j][...] = g_band.astype(g_outs[j].dtype)


def main_call(slot, own, sib, prevs, biases, bands, steps, carried=()):
    frames, half = sib.shape[1:]
    share = bands[0].shape[0] // steps
    groups = half // W // 2
    rows = 2 * share * steps
    return call(
        functools.partial(main_body, steps, slot),
        "attention_backward",
        [
            shape((3, frames, half), F32),
            shape((3, frames, half), F32),
            shape((2, frames, half), BF16),
        ]
        + [shape((W, rows), F32 if slot else BF16)] * groups,
        [
            pltpu.VMEM((groups, 4, 2, frames, W), BF16),
            pltpu.VMEM((groups, 2, frames, W), BF16),
            pltpu.VMEM((groups, steps, 2, share, W), BF16),
            pltpu.VMEM((groups, 2, 3, frames, W), F32),
            pltpu.VMEM((2, frames, W), BF16),
        ],
        limit=24,
    )(*own, sib, *prevs, *biases, *bands, *carried)


def copies(sem, pairs):
    started = [pltpu.make_async_copy(a, b, sem.at[n]) for n, (a, b) in enumerate(pairs)]
    for copy in started:
        copy.start()
    for copy in started:
        copy.wait()


HBM = pl.BlockSpec(memory_space=pltpu.HBM)


def band_cut_body(table, out, sem):
    half = table.shape[1] // 2
    span = half // 2
    pair = pair_of()
    copies(
        sem,
        [
            (table.at[:, columns(n * half + pair * span, span)], out.at[:, n * span : (n + 1) * span])
            for n in range(2)
        ],
    )


def band_cut(table):
    rows, width = table.shape
    out = shape((rows, width // 2), BF16)
    return call(
        band_cut_body, "band_cut", out, [pltpu.SemaphoreType.DMA((2,))], in_specs=[HBM]
    )(table)


def band_pack_body(steps, *refs):
    own, sib = refs[steps:]
    core, z = lax.axis_index("core"), lax.axis_index("z")
    span = own.shape[2]
    for n in range(steps):
        at = lax.rem(z - n + steps, steps)
        own[at] = refs[n][:, columns(core * span, span)]
        sib[at] = refs[n][:, columns((1 - core) * span, span)]


def band_pack(parts):
    rows, width = parts[0].shape
    steps = len(parts)
    out = call(
        functools.partial(band_pack_body, steps),
        "band_pack",
        [shape((steps, rows, width // 2), BF16)] * 2,
    )(*parts)
    return [x.reshape(steps * rows, width // 2) for x in out]


def prep_body(q, k, v, g, cut, sib, prev0, prev1, sem):
    half = sib.shape[2]
    there = columns((1 - lax.axis_index("core")) * half, half)
    pairs = [(x.at[:, there], sib.at[n]) for n, x in enumerate((q, k, v, g))]
    for n, x in enumerate((k, v)):
        pairs.append((x.at[:, :half], prev0.at[n]))
        pairs.append((x.at[:, half:], prev1.at[n]))
    copies(sem, pairs)


def prep(own, cut):
    frames, width = own[0].shape
    outs = [shape((n, frames, width // 2), BF16) for n in (4, 2, 2)]
    scratch = [pltpu.SemaphoreType.DMA((8,))]
    return call(prep_body, "prepare", outs, scratch, in_specs=[HBM] * 4 + [pl.BlockSpec()])(*own, cut)


def summed(refs):
    total = refs[0][...].astype(F32)
    for ref in refs[1:]:
        total = total + ref[...].astype(F32)
    return total


def pair_sum_body(steps, own0, own1, from_x, from_y, *refs):
    scr = refs[-1]
    z = lax.axis_index("z")
    rows = scr.shape[2]
    for n, (a, b) in enumerate(((own0, from_x), (own1, from_y))):
        total = (a[...] + b[...].astype(F32)).astype(BF16)
        for m in range(steps):
            scr[m, n * W : (n + 1) * W] = total[:, m * rows : (m + 1) * rows]
    for m in range(steps):
        refs[m][...] = scr[lax.rem(z + m, steps)]


def pair_sum(own, received, steps):
    rows = own[0].shape[1] // steps
    return call(
        functools.partial(pair_sum_body, steps),
        "pair_sum",
        [shape((2 * W, rows), BF16)] * steps,
        [pltpu.VMEM((steps, 2 * W, rows), BF16)],
    )(*own, *received)


def z_sum_body(*refs):
    refs[-1][...] = summed(refs[:-1]).astype(BF16)


def z_sum(parts):
    return call(z_sum_body, "z_sum", shape(parts[0].shape, BF16))(*parts)


def plane_sum_body(own, diagonal, from_x, from_y, mine, other, scr):
    core, pair = lax.axis_index("core"), pair_of()
    rows, half = mine.shape
    span = half // 2
    for n, terms in enumerate(((from_x, from_y), (own, diagonal))):
        total = summed(terms).T.reshape(2, rows, span)
        scr[:, :, columns((pair ^ n) * span, span)] = total
    mine[...] = scr[core]
    other[...] = scr[1 - core]


def plane_sum(parts):
    span, rows = parts[0].shape
    return call(
        plane_sum_body,
        "plane_sum",
        [shape((rows // 2, 2 * span), F32)] * 2,
        [pltpu.VMEM((2, rows // 2, 2 * span), F32)],
    )(*parts)


def rows_final_body(own, sib, back0, back1, dq, dk, dv):
    core = lax.axis_index("core")
    half = own.shape[2]
    mine, other = columns(core * half, half), columns((1 - core) * half, half)
    dq[:, mine] = own[0].astype(BF16)
    dq[:, other] = sib[0].astype(BF16)
    for n, out in enumerate((dk, dv)):
        back = [back0[n].astype(F32), back1[n].astype(F32)]
        out[:, mine] = (own[1 + n] + jnp.where(core == 0, back[0], back[1])).astype(BF16)
        out[:, other] = (sib[1 + n] + jnp.where(core == 0, back[1], back[0])).astype(BF16)


def rows_final(*arrays):
    frames, half = arrays[0].shape[1:]
    return call(rows_final_body, "rows_final", [shape((frames, 2 * half), BF16)] * 3)(*arrays)


def band_final_body(mine, other, out):
    core = lax.axis_index("core")
    half = mine.shape[1]
    out[:, columns(core * half, half)] = mine[...]
    out[:, columns((1 - core) * half, half)] = other[...]


def band_final(mine, other):
    rows, half = mine.shape
    return call(band_final_body, "band_final", shape((rows, 2 * half), F32))(mine, other)


def local(query_rows, key_rows, value_rows, grad_out, pos_keys, bias_content, bias_position):
    n_high, n_z = lax.axis_size("dh"), lax.axis_size("z")
    width = query_rows.shape[2]
    n_blk = 2 * n_z
    chain = ("z", "core")

    def along_z(x, steps):
        return lax.ppermute(x, "z", [(s, (s + steps) % n_z) for s in range(n_z)])

    def to_sibling(x):
        return lax.ppermute(x, "core", [(0, 1), (1, 0)])

    def in_plane(x, flip, cross=0):
        pairs = [
            (2 * d + c, 2 * (d ^ flip) + (c ^ cross)) for d in range(PLANE) for c in range(2)
        ]
        return lax.ppermute(x, ("dl", "core"), pairs)

    cut = band_cut(pos_keys)
    cuts = [cut] + [along_z(cut, k) for k in range(1, n_z)]
    own = [x[0] for x in (query_rows, key_rows, value_rows, grad_out)]
    sib, prev0, prev1 = prep(own, cut)
    sib = to_sibling(sib)
    odd = range(1, n_blk, 2)
    prev0 = lax.ppermute(prev0, chain, [(s, (s + 1) % n_blk) for s in odd])
    prev1 = lax.ppermute(prev1, chain, [(s, (s + 2) % n_blk) for s in odd])
    band_own, band_sib = band_pack(cuts)
    first_bands = [band_own, to_sibling(band_sib)]
    second_bands = [in_plane(band_own, 1), in_plane(band_sib, 2, 1)]
    biases = [bias_content.reshape(1, width), bias_position.reshape(1, width)]

    inputs = (own, sib, (prev0, prev1), biases)
    *carried, g_x, g_y = main_call(0, *inputs, first_bands, n_z)
    received = [in_plane(g_x, 1), in_plane(g_y, 2)]
    out_own, out_sib, back, *g_own = main_call(1, *inputs, second_bands, n_z, carried)

    parts = pair_sum(g_own, received, n_z)
    parts = [parts[0]] + [along_z(parts[k], k) for k in range(1, n_z)]
    out_sib = to_sibling(out_sib)
    back0 = lax.ppermute(back, chain, [(s, (s - 1) % n_blk) for s in range(0, n_blk, 2)])
    back1 = lax.ppermute(back, chain, [(s, (s - 2) % n_blk) for s in odd])

    total = z_sum(parts)
    step = 1
    while step < n_high:
        pairs = [(s, s ^ step) for s in range(n_high)]
        total = z_sum([total, lax.ppermute(total, "dh", pairs)])
        step *= 2
    mine, other = plane_sum([total] + [in_plane(total, k) for k in (3, 1, 2)])
    other = to_sibling(other)
    dq, dk, dv = rows_final(out_own, out_sib, back0, back1)
    grad_pos = band_final(mine, other)
    return dq[None], dk[None], dv[None], grad_pos


def solution(mesh):
    n_dp, n_blk = mesh.shape["dp"], mesh.shape["blk"]
    fine = Mesh(mesh.devices.reshape(n_dp // PLANE, PLANE, n_blk // 2, 2), ("dh", "dl", "z", "core"))
    rows = P(("dh", "dl"), ("z", "core"), None)
    band = P(("z", "core"), None)
    return jax.shard_map(
        local,
        mesh=fine,
        in_specs=(rows, rows, rows, rows, band, P(), P()),
        out_specs=(rows, rows, rows, band),
        check_vma=False,
    )
```

```python
import functools

import jax
import jax.numpy as jnp
from jax import lax
from jax.experimental import pallas as pl
from jax.experimental.pallas import tpu as pltpu
from jax.sharding import Mesh
from jax.sharding import PartitionSpec as P

DH = 64
W = 128
PLANE = 4
MIB = 2**20
F32 = jnp.float32
BF16 = jnp.bfloat16


def mm(a, b):
    return jnp.dot(a, b, preferred_element_type=F32)


def mm_nt(a, b):
    return lax.dot_general(a, b, (((1,), (1,)), ((), ())), preferred_element_type=F32)


def iota(shape, axis):
    return lax.broadcasted_iota(jnp.int32, shape, axis)


def as_bf16(hit):
    return hit.astype(F32).astype(BF16)


def shear(x, frames):
    rows = [
        pltpu.roll(x[r : r + frames], frames + 1, 1, stride=1, stride_axis=0)
        for r in range(0, x.shape[0], frames)
    ]
    return jnp.concatenate(rows, axis=0)


def columns(start, size):
    return pl.ds(pl.multiple_of(start, W), size)


class Masks:
    def __init__(self, frames):
        span = 2 * frames
        lane = iota((frames, W), 1)
        sub = iota((W, frames), 0)
        self.first = lane < DH
        self.lanes = [as_bf16(lane < DH), as_bf16(lane >= DH)]
        self.subs = [as_bf16(sub < DH), as_bf16(sub >= DH)]
        self.flip = as_bf16(iota((span, span), 0) + iota((span, span), 1) == span - 1)
        row = iota((span, span), 0) & (frames - 1)
        col = iota((span, span), 1)
        self.forward = (col + row >= frames - 1) & (col + row <= span - 2)
        back = (col - row >= 1) & (col - row <= frames)
        self.back = [as_bf16(back), as_bf16(~back)]

    def stack(self, x):
        return jnp.concatenate([x * self.lanes[0], x * self.lanes[1]], axis=0)

    def stack_t(self, x):
        x = x.T
        return jnp.concatenate([x * self.subs[0], x * self.subs[1]], axis=1)


def unit(masks, q, k, v, g, k_before, v_before, tables, bias_c, bias_p):
    frames = q.shape[0]
    factor = DH**-0.5
    band0, band1, band0_rev, band1_rev = tables
    kw = jnp.concatenate([k, k_before], axis=0)
    vw = jnp.concatenate([v, v_before], axis=0)
    qf = q.astype(F32)
    qc = (qf + bias_c).astype(BF16)
    qp = (qf + bias_p).astype(BF16)
    qp_stack = masks.stack(qp)
    content = mm_nt(masks.stack(qc), kw)
    merged = jnp.where(masks.forward, mm_nt(qp_stack, band0_rev), mm_nt(qp_stack, band1_rev))
    scores = (content + shear(merged, frames)) * factor
    e = jnp.exp(scores - jnp.max(scores, axis=1, keepdims=True))
    gw = mm_nt(masks.stack(g), vw)
    attention = e * (1.0 / jnp.sum(e, axis=1, keepdims=True))
    delta = jnp.sum(attention * gw, axis=1, keepdims=True)
    ds = (attention * (gw - delta) * factor).astype(BF16)
    placed = shear(mm(ds, masks.flip), frames).astype(BF16)
    d0, d1 = placed * masks.back[0], placed * masks.back[1]
    lhs = jnp.concatenate([ds, d0, d1], axis=1)
    rhs = jnp.concatenate([kw, band0, band1], axis=0)
    full = mm(lhs, rhs)
    dq = jnp.where(masks.first, full[:frames], full[frames:]).astype(BF16).astype(F32)
    dk = mm(masks.stack_t(qc), ds)
    dv = mm(masks.stack_t(g), attention.astype(BF16))
    qp_t = masks.stack_t(qp)
    g1 = mm(qp_t, d1)
    g_band = jnp.concatenate([mm(qp_t, d0), g1[:, frames:], g1[:, :frames]], axis=1)
    return dq, dk, dv, g_band


def call(body, name, out_shape, scratch=(), limit=8, **options):
    return pl.pallas_call(
        body,
        out_shape=out_shape,
        scratch_shapes=list(scratch),
        compiler_params=pltpu.CompilerParams(vmem_limit_bytes=limit * MIB),
        name=name,
        **options,
    )


def shape(dims, dtype):
    return jax.ShapeDtypeStruct(tuple(dims), dtype)


def pair_of():
    low = lax.axis_index("dl")
    return (low & 1) ^ (low >> 1)


def place(own, sib, scr, slot):
    core = lax.axis_index("core")
    span = scr.shape[3]
    here = columns((2 * core + (pair_of() ^ slot)) * span, span)
    for n, (a, b) in enumerate(zip(own, sib)):
        scr[n, core] = a[:, here]
        scr[n, 1 - core] = b[:, here]
    return here


def odd_body(steps, slot, *refs):
    own, sib, (bias_c, bias_p), bands = refs[0:4], refs[4:8], refs[8:10], refs[10:12]
    out, carry, g_out, tables, scr, band_scr = refs[12:]
    core = lax.axis_index("core")
    frames, span = scr.shape[2:]
    share = band_scr.shape[2]
    here = place(own, sib, scr, slot)
    bias_c, bias_p = bias_c[:, here], bias_p[:, here]
    band_scr[:, core] = bands[0][...].reshape(steps, share, span)
    band_scr[:, 1 - core] = bands[1][...].reshape(steps, share, span)
    band = band_scr[...].reshape(steps * 2 * share, span)
    masks = Masks(frames)
    band0, band1 = band[: 2 * frames], band[2 * frames :]
    band1 = jnp.concatenate([band1[frames:], band1[:frames]], axis=0)
    tables[0] = band0
    tables[1] = band1
    tables[2] = mm(masks.flip, band0).astype(BF16)
    tables[3] = mm(masks.flip, band1).astype(BF16)
    for j in range(span // W):
        at = slice(j * W, (j + 1) * W)
        dq, dk, dv, g_band = unit(
            masks,
            *[scr[n, 1, :, at] for n in range(4)],
            scr[1, 0, :, at],
            scr[2, 0, :, at],
            [tables[n, :, at] for n in range(4)],
            bias_c[:, at],
            bias_p[:, at],
        )
        out[0, :, at] = dq
        for n, term in enumerate((dk, dv)):
            out[1 + n, :, at] = term[:, :frames].T
            carry[n, :, at] = term[:, frames:].astype(BF16).T
        g_out[j] = g_band


def even_body(slot, *refs):
    own, sib, (bias_c, bias_p) = refs[0:4], refs[4:8], refs[8:10]
    prev, tables, carry, g_odd, back_done = refs[10:15]
    out, back = refs[15:17]
    g_outs, scr, back_scr = refs[17:-2], refs[-2], refs[-1]
    frames, span = scr.shape[2:]
    here = place(own, sib, scr, slot)
    bias_c, bias_p = bias_c[:, here], bias_p[:, here]
    inside = columns((pair_of() ^ slot) * span, span)
    done = columns((pair_of() ^ 1 ^ slot) * span, span)
    masks = Masks(frames)
    for j in range(span // W):
        at = slice(j * W, (j + 1) * W)
        mine = columns((pair_of() ^ slot) * span + j * W, W)
        dq, dk, dv, g_band = unit(
            masks,
            *[scr[n, 0, :, at] for n in range(4)],
            prev[0, :, mine],
            prev[1, :, mine],
            [tables[n, :, at] for n in range(4)],
            bias_c[:, at],
            bias_p[:, at],
        )
        out[0, :, at] = dq
        for n, term in enumerate((dk, dv)):
            out[1 + n, :, at] = term[:, :frames].T + carry[n, :, at].astype(F32)
            back_scr[n, :, at] = term[:, frames:].astype(BF16).T
        g_outs[j][...] = (g_odd[j] + g_band).astype(g_outs[j].dtype)
    back[:, :, inside] = back_scr[...]
    back[:, :, done] = back_done[:, :, done]


def cost(groups, frames):
    return pl.CostEstimate(
        flops=2 * groups * 20 * frames * (2 * frames) ** 2,
        bytes_accessed=64 * groups * frames * W,
        transcendentals=groups * 4 * frames * frames,
    )


def odd_call(slot, own, sib, biases, bands, steps):
    frames = own[0].shape[0]
    rows, span = bands[0].shape
    groups = span // W
    return call(
        functools.partial(odd_body, steps, slot),
        "odd_block",
        [
            shape((3, frames, span), F32),
            shape((2, frames, span), BF16),
            shape((groups, W, 2 * rows), F32),
            shape((4, rows, span), BF16),
        ],
        [
            pltpu.VMEM((4, 2, frames, span), BF16),
            pltpu.VMEM((steps, 2, rows // steps, span), BF16),
        ],
        limit=16,
        cost_estimate=cost(groups, frames),
    )(*own, *sib, *biases, *bands)


def even_call(slot, own, sib, biases, prev, odd, back):
    frames = own[0].shape[0]
    _, carry, g_odd, tables = odd
    groups, _, rows = g_odd.shape
    span = groups * W
    return call(
        functools.partial(even_body, slot),
        "even_block",
        [shape((3, frames, span), F32), shape((2, frames, 2 * span), BF16)]
        + [shape((W, rows), F32 if slot else BF16)] * groups,
        [pltpu.VMEM((4, 2, frames, span), BF16), pltpu.VMEM((2, frames, span), BF16)],
        limit=16,
        cost_estimate=cost(groups, frames),
    )(*own, *sib, *biases, prev, tables, carry, g_odd, back)


def band_cut_body(table, out):
    half = table.shape[1] // 2
    span = half // 2
    pair = pair_of()
    for n in range(2):
        out[:, n * span : (n + 1) * span] = table[:, columns(n * half + pair * span, span)]


def band_cut(table):
    rows, width = table.shape
    return call(band_cut_body, "band_cut", shape((rows, width // 2), BF16))(table)


def band_pack_body(steps, *refs):
    own, sib = refs[steps:]
    core, z = lax.axis_index("core"), lax.axis_index("z")
    span = own.shape[2]
    for n in range(steps):
        at = z ^ n
        own[at] = refs[n][:, columns(core * span, span)]
        sib[at] = refs[n][:, columns((1 - core) * span, span)]


def band_pack(parts):
    rows, width = parts[0].shape
    steps = len(parts)
    out = call(
        functools.partial(band_pack_body, steps),
        "band_pack",
        [shape((steps, rows, width // 2), BF16)] * 2,
    )(*parts)
    return [x.reshape(steps * rows, width // 2) for x in out]


def odd_rows_body(k, v, k_sib, v_sib, out):
    half = out.shape[2]
    core = lax.axis_index("core")
    for which, pair in enumerate(((k_sib, v_sib), (k, v))):

        @pl.when(core == which)
        def _():
            for n, x in enumerate(pair):
                out[n] = x[:, which * half : (which + 1) * half]


def odd_rows(*arrays):
    frames, width = arrays[0].shape
    return call(odd_rows_body, "odd_rows", shape((2, frames, width // 2), BF16))(*arrays)


def summed(refs):
    total = refs[0][...].astype(F32)
    for ref in refs[1:]:
        total = total + ref[...].astype(F32)
    return total


def pair_sum_body(steps, own0, own1, from_x, from_y, *refs):
    scr = refs[-1]
    z = lax.axis_index("z")
    rows = scr.shape[2]
    for n, (a, b) in enumerate(((own0, from_x), (own1, from_y))):
        total = (a[...] + b[...].astype(F32)).astype(BF16)
        for m in range(steps):
            scr[m, n * W : (n + 1) * W] = total[:, m * rows : (m + 1) * rows]
    for m in range(steps):
        refs[m][...] = scr[z ^ m]


def pair_sum(own, received, steps):
    rows = own[0].shape[1] // steps
    return call(
        functools.partial(pair_sum_body, steps),
        "pair_sum",
        [shape((2 * W, rows), BF16)] * steps,
        [pltpu.VMEM((steps, 2 * W, rows), BF16)],
    )(*own, *received)


def z_sum_body(*refs):
    refs[-1][...] = summed(refs[:-1]).astype(BF16)


def z_sum(parts):
    return call(z_sum_body, "z_sum", shape(parts[0].shape, BF16))(*parts)


def plane_sum_body(own, diagonal, from_x, from_y, mine, other, scr):
    core, pair = lax.axis_index("core"), pair_of()
    rows, half = mine.shape
    span = half // 2
    for n, terms in enumerate(((from_x, from_y), (own, diagonal))):
        total = summed(terms).T.reshape(2, rows, span)
        scr[:, :, columns((pair ^ n) * span, span)] = total
    mine[...] = scr[core]
    other[...] = scr[1 - core]


def plane_sum(parts):
    span, rows = parts[0].shape
    return call(
        plane_sum_body,
        "plane_sum",
        [shape((rows // 2, 2 * span), F32)] * 2,
        [pltpu.VMEM((2, rows // 2, 2 * span), F32)],
    )(*parts)


def fold_body(odd0, odd1, even0, even1, back, out):
    core, pair = lax.axis_index("core"), pair_of()
    span = odd0.shape[2]
    for which, blocks in enumerate(((odd0, odd1), (even0, even1))):

        @pl.when(core == which)
        def _():
            for slot, x in enumerate(blocks):
                here = columns((pair ^ slot) * span, span)
                out[0, :, here] = x[0]
                for n in range(2):
                    total = x[1 + n]
                    if which == 0:
                        total = total + back[n, :, here].astype(F32)
                    out[1 + n, :, here] = total


def fold(odd, even, back):
    return call(fold_body, "fold", shape((3, *back.shape[1:]), F32))(*odd, *even, back)


def rows_final_body(odd0, odd1, even0, even1, back, sib, dq, dk, dv):
    core, pair = lax.axis_index("core"), pair_of()
    span = odd0.shape[2]
    other = columns((1 - core) * 2 * span, 2 * span)
    dq[:, other] = sib[0].astype(BF16)
    dk[:, other] = sib[1].astype(BF16)
    dv[:, other] = sib[2].astype(BF16)
    for which, blocks in enumerate(((even0, even1), (odd0, odd1))):

        @pl.when(core == which)
        def _():
            for slot, x in enumerate(blocks):
                inside = columns((pair ^ slot) * span, span)
                mine = columns((2 * which + (pair ^ slot)) * span, span)
                dq[:, mine] = x[0].astype(BF16)
                for n, out in enumerate((dk, dv)):
                    total = x[1 + n]
                    if which == 1:
                        total = total + back[n, :, inside].astype(F32)
                    out[:, mine] = total.astype(BF16)


def rows_final(odd, even, back, sib):
    frames, half = back.shape[1:]
    outs = [shape((frames, 2 * half), BF16)] * 3
    return call(rows_final_body, "rows_final", outs)(*odd, *even, back, sib)


def band_final_body(mine, other, out):
    core = lax.axis_index("core")
    half = mine.shape[1]
    out[:, columns(core * half, half)] = mine[...]
    out[:, columns((1 - core) * half, half)] = other[...]


def band_final(mine, other):
    rows, half = mine.shape
    return call(band_final_body, "band_final", shape((rows, 2 * half), F32))(mine, other)


def local(query_rows, key_rows, value_rows, grad_out, pos_keys, bias_content, bias_position):
    n_high, n_z = lax.axis_size("dh"), lax.axis_size("z")
    width = query_rows.shape[2]

    def along_z(x, flip):
        return lax.ppermute(x, "z", [(s, s ^ flip) for s in range(n_z)])

    def around_z(x, steps):
        return lax.ppermute(x, "z", [(s, (s + steps) % n_z) for s in range(n_z)])

    def to_sibling(x):
        return lax.ppermute(x, "core", [(0, 1), (1, 0)])

    def in_plane(x, flip, cross=0):
        pairs = [
            (2 * d + c, 2 * (d ^ flip) + (c ^ cross)) for d in range(PLANE) for c in range(2)
        ]
        return lax.ppermute(x, ("dl", "core"), pairs)

    cut = band_cut(pos_keys)
    cuts = [cut] + [along_z(cut, k) for k in range(1, n_z)]
    own = [x[0] for x in (query_rows, key_rows, value_rows, grad_out)]
    sib = [to_sibling(x) for x in own]
    prev = around_z(odd_rows(*own[1:3], *sib[1:3]), 1)
    band_own, band_sib = band_pack(cuts)
    first_bands = [band_own, to_sibling(band_sib)]
    second_bands = [in_plane(band_own, 1), in_plane(band_sib, 2, 1)]
    biases = [bias_content.reshape(1, width), bias_position.reshape(1, width)]

    inputs = (own, sib, biases)
    first = odd_call(0, *inputs, first_bands, n_z)
    second = odd_call(1, *inputs, second_bands, n_z)
    first, second = lax.optimization_barrier((first, second))
    even0, back, g_x, g_y = even_call(0, *inputs, prev, first, prev)
    received = [in_plane(g_x, 1), in_plane(g_y, 2)]
    even1, back, *g_own = even_call(1, *inputs, prev, second, back)
    odd, even = (first[0], second[0]), (even0, even1)

    parts, back = lax.optimization_barrier((pair_sum(g_own, received, n_z), back))
    parts = [parts[0]] + [along_z(parts[k], k) for k in range(1, n_z)]
    back = around_z(back, -1)
    total = z_sum(parts)
    step = 1
    while step < n_high:
        pairs = [(s, s ^ step) for s in range(n_high)]
        total = z_sum([total, lax.ppermute(total, "dh", pairs)])
        step *= 2
    planes = [in_plane(total, k) for k in (3, 1, 2)]
    *planes, back = lax.optimization_barrier((*planes, back))
    out_sib = to_sibling(fold(odd, even, back))
    mine, other = plane_sum([total, *planes])
    other = to_sibling(other)
    rows = rows_final(odd, even, back, out_sib)
    *rows, mine, other = lax.optimization_barrier((*rows, mine, other))
    return *[x[None] for x in rows], band_final(mine, other)


def solution(mesh):
    n_dp, n_blk = mesh.shape["dp"], mesh.shape["blk"]
    fine = Mesh(mesh.devices.reshape(n_dp // PLANE, PLANE, n_blk // 2, 2), ("dh", "dl", "z", "core"))
    rows = P(("dh", "dl"), ("z", "core"), None)
    band = P(("z", "core"), None)
    return jax.shard_map(
        local,
        mesh=fine,
        in_specs=(rows, rows, rows, rows, band, P(), P()),
        out_specs=(rows, rows, rows, band),
        check_vma=False,
    )
```

```python
import functools

import jax
import jax.numpy as jnp
from jax import lax
from jax.experimental import pallas as pl
from jax.experimental.pallas import tpu as pltpu
from jax.sharding import Mesh
from jax.sharding import PartitionSpec as P

DH = 64
W = 128
PLANE = 4
MIB = 2**20
F32 = jnp.float32
BF16 = jnp.bfloat16


def mm(a, b):
    return jnp.dot(a, b, preferred_element_type=F32)


def mm_nt(a, b):
    return lax.dot_general(a, b, (((1,), (1,)), ((), ())), preferred_element_type=F32)


def iota(shape, axis):
    return lax.broadcasted_iota(jnp.int32, shape, axis)


def as_bf16(hit):
    return hit.astype(F32).astype(BF16)


def shear(x, frames):
    rows = [
        pltpu.roll(x[r : r + frames], frames + 1, 1, stride=1, stride_axis=0)
        for r in range(0, x.shape[0], frames)
    ]
    return jnp.concatenate(rows, axis=0)


def columns(start, size):
    return pl.ds(pl.multiple_of(start, W), size)


class Masks:
    def __init__(self, frames):
        span = 2 * frames
        lane = iota((frames, W), 1)
        sub = iota((W, frames), 0)
        self.first = lane < DH
        self.lanes = [as_bf16(lane < DH), as_bf16(lane >= DH)]
        self.subs = [as_bf16(sub < DH), as_bf16(sub >= DH)]
        self.flip = as_bf16(iota((span, span), 0) + iota((span, span), 1) == span - 1)
        row = iota((span, span), 0) & (frames - 1)
        col = iota((span, span), 1)
        self.forward = (col + row >= frames - 1) & (col + row <= span - 2)
        back = (col - row >= 1) & (col - row <= frames)
        self.back = [as_bf16(back), as_bf16(~back)]

    def stack(self, x):
        return jnp.concatenate([x * self.lanes[0], x * self.lanes[1]], axis=0)

    def stack_t(self, x):
        x = x.T
        return jnp.concatenate([x * self.subs[0], x * self.subs[1]], axis=1)


def unit(masks, q, k, v, g, k_before, v_before, tables, bias_c, bias_p):
    frames = q.shape[0]
    factor = DH**-0.5
    band0, band1, band0_rev, band1_rev = tables
    kw = jnp.concatenate([k, k_before], axis=0)
    vw = jnp.concatenate([v, v_before], axis=0)
    qf = q.astype(F32)
    qc = (qf + bias_c).astype(BF16)
    qp = (qf + bias_p).astype(BF16)
    qp_stack = masks.stack(qp)
    content = mm_nt(masks.stack(qc), kw)
    merged = jnp.where(masks.forward, mm_nt(qp_stack, band0_rev), mm_nt(qp_stack, band1_rev))
    scores = (content + shear(merged, frames)) * factor
    e = jnp.exp(scores - jnp.max(scores, axis=1, keepdims=True))
    gw = mm_nt(masks.stack(g), vw)
    attention = e * (1.0 / jnp.sum(e, axis=1, keepdims=True))
    delta = jnp.sum(attention * gw, axis=1, keepdims=True)
    ds = (attention * (gw - delta) * factor).astype(BF16)
    placed = shear(mm(ds, masks.flip), frames).astype(BF16)
    d0, d1 = placed * masks.back[0], placed * masks.back[1]
    lhs = jnp.concatenate([ds, d0, d1], axis=1)
    rhs = jnp.concatenate([kw, band0, band1], axis=0)
    full = mm(lhs, rhs)
    dq = jnp.where(masks.first, full[:frames], full[frames:]).astype(BF16).astype(F32)
    dk = mm(masks.stack_t(qc), ds)
    dv = mm(masks.stack_t(g), attention.astype(BF16))
    qp_t = masks.stack_t(qp)
    g1 = mm(qp_t, d1)
    g_band = jnp.concatenate([mm(qp_t, d0), g1[:, frames:], g1[:, :frames]], axis=1)
    return dq, dk, dv, g_band


def call(body, name, out_shape, scratch=(), limit=8, **options):
    return pl.pallas_call(
        body,
        out_shape=out_shape,
        scratch_shapes=list(scratch),
        compiler_params=pltpu.CompilerParams(vmem_limit_bytes=limit * MIB),
        name=name,
        **options,
    )


def shape(dims, dtype):
    return jax.ShapeDtypeStruct(tuple(dims), dtype)


def pair_of():
    low = lax.axis_index("dl")
    return (low & 1) ^ (low >> 1)


def place(own, sib, scr, slot):
    core = lax.axis_index("core")
    span = scr.shape[3]
    here = columns((2 * core + (pair_of() ^ slot)) * span, span)
    for n, (a, b) in enumerate(zip(own, sib)):
        scr[n, core] = a[:, here]
        scr[n, 1 - core] = b[:, here]
    return here


def odd_body(steps, slot, *refs):
    own, sib, (bias_c, bias_p), bands = refs[0:4], refs[4:8], refs[8:10], refs[10:12]
    out, carry, g_out, tables, scr, band_scr = refs[12:]
    core = lax.axis_index("core")
    frames, span = scr.shape[2:]
    share = band_scr.shape[2]
    here = place(own, sib, scr, slot)
    bias_c, bias_p = bias_c[:, here], bias_p[:, here]
    band_scr[:, core] = bands[0][...].reshape(steps, share, span)
    band_scr[:, 1 - core] = bands[1][...].reshape(steps, share, span)
    band = band_scr[...].reshape(steps * 2 * share, span)
    masks = Masks(frames)
    band0, band1 = band[: 2 * frames], band[2 * frames :]
    band1 = jnp.concatenate([band1[frames:], band1[:frames]], axis=0)
    tables[0] = band0
    tables[1] = band1
    tables[2] = mm(masks.flip, band0).astype(BF16)
    tables[3] = mm(masks.flip, band1).astype(BF16)
    for j in range(span // W):
        at = slice(j * W, (j + 1) * W)
        dq, dk, dv, g_band = unit(
            masks,
            *[scr[n, 1, :, at] for n in range(4)],
            scr[1, 0, :, at],
            scr[2, 0, :, at],
            [tables[n, :, at] for n in range(4)],
            bias_c[:, at],
            bias_p[:, at],
        )
        out[0, :, at] = dq
        for n, term in enumerate((dk, dv)):
            out[1 + n, :, at] = term[:, :frames].T
            carry[n, :, at] = term[:, frames:].astype(BF16).T
        g_out[j] = g_band


def even_body(slot, *refs):
    own, sib, (bias_c, bias_p) = refs[0:4], refs[4:8], refs[8:10]
    prev, tables, carry, g_odd, back_done = refs[10:15]
    out, back = refs[15:17]
    g_outs, scr, back_scr = refs[17:-2], refs[-2], refs[-1]
    frames, span = scr.shape[2:]
    here = place(own, sib, scr, slot)
    bias_c, bias_p = bias_c[:, here], bias_p[:, here]
    inside = columns((pair_of() ^ slot) * span, span)
    done = columns((pair_of() ^ 1 ^ slot) * span, span)
    masks = Masks(frames)
    for j in range(span // W):
        at = slice(j * W, (j + 1) * W)
        mine = columns((pair_of() ^ slot) * span + j * W, W)
        dq, dk, dv, g_band = unit(
            masks,
            *[scr[n, 0, :, at] for n in range(4)],
            prev[0, :, mine],
            prev[1, :, mine],
            [tables[n, :, at] for n in range(4)],
            bias_c[:, at],
            bias_p[:, at],
        )
        out[0, :, at] = dq
        for n, term in enumerate((dk, dv)):
            out[1 + n, :, at] = term[:, :frames].T + carry[n, :, at].astype(F32)
            back_scr[n, :, at] = term[:, frames:].astype(BF16).T
        g_outs[j][...] = (g_odd[j] + g_band).astype(g_outs[j].dtype)
    back[:, :, inside] = back_scr[...]
    back[:, :, done] = back_done[:, :, done]


def cost(groups, frames):
    return pl.CostEstimate(
        flops=2 * groups * 20 * frames * (2 * frames) ** 2,
        bytes_accessed=64 * groups * frames * W,
        transcendentals=groups * 4 * frames * frames,
    )


def odd_call(slot, own, sib, biases, bands, steps):
    frames = own[0].shape[0]
    rows, span = bands[0].shape
    groups = span // W
    return call(
        functools.partial(odd_body, steps, slot),
        "odd_block",
        [
            shape((3, frames, span), F32),
            shape((2, frames, span), BF16),
            shape((groups, W, 2 * rows), F32),
            shape((4, rows, span), BF16),
        ],
        [
            pltpu.VMEM((4, 2, frames, span), BF16),
            pltpu.VMEM((steps, 2, rows // steps, span), BF16),
        ],
        limit=16,
        cost_estimate=cost(groups, frames),
    )(*own, *sib, *biases, *bands)


def even_call(slot, own, sib, biases, prev, odd, back):
    frames = own[0].shape[0]
    _, carry, g_odd, tables = odd
    groups, _, rows = g_odd.shape
    span = groups * W
    return call(
        functools.partial(even_body, slot),
        "even_block",
        [shape((3, frames, span), F32), shape((2, frames, 2 * span), BF16)]
        + [shape((W, rows), F32 if slot else BF16)] * groups,
        [pltpu.VMEM((4, 2, frames, span), BF16), pltpu.VMEM((2, frames, span), BF16)],
        limit=16,
        cost_estimate=cost(groups, frames),
    )(*own, *sib, *biases, prev, tables, carry, g_odd, back)


def band_cut_body(table, out):
    half = table.shape[1] // 2
    span = half // 2
    pair = pair_of()
    for n in range(2):
        out[:, n * span : (n + 1) * span] = table[:, columns(n * half + pair * span, span)]


def band_cut(table):
    rows, width = table.shape
    return call(band_cut_body, "band_cut", shape((rows, width // 2), BF16))(table)


def band_pack_body(steps, *refs):
    own, sib = refs[steps:]
    core, z = lax.axis_index("core"), lax.axis_index("z")
    span = own.shape[2]
    for n in range(steps):
        at = z ^ n
        own[at] = refs[n][:, columns(core * span, span)]
        sib[at] = refs[n][:, columns((1 - core) * span, span)]


def band_pack(parts):
    rows, width = parts[0].shape
    steps = len(parts)
    out = call(
        functools.partial(band_pack_body, steps),
        "band_pack",
        [shape((steps, rows, width // 2), BF16)] * 2,
    )(*parts)
    return [x.reshape(steps * rows, width // 2) for x in out]


def odd_rows_body(k, v, k_sib, v_sib, out):
    half = out.shape[2]
    core = lax.axis_index("core")
    for which, pair in enumerate(((k_sib, v_sib), (k, v))):

        @pl.when(core == which)
        def _():
            for n, x in enumerate(pair):
                out[n] = x[:, which * half : (which + 1) * half]


def odd_rows(*arrays):
    frames, width = arrays[0].shape
    return call(odd_rows_body, "odd_rows", shape((2, frames, width // 2), BF16))(*arrays)


def summed(refs):
    total = refs[0][...].astype(F32)
    for ref in refs[1:]:
        total = total + ref[...].astype(F32)
    return total


def pair_sum_body(steps, own0, own1, from_x, from_y, *refs):
    scr = refs[-1]
    z = lax.axis_index("z")
    rows = scr.shape[2]
    for n, (a, b) in enumerate(((own0, from_x), (own1, from_y))):
        total = (a[...] + b[...].astype(F32)).astype(BF16)
        for m in range(steps):
            scr[m, n * W : (n + 1) * W] = total[:, m * rows : (m + 1) * rows]
    for m in range(steps):
        refs[m][...] = scr[z ^ m]


def pair_sum(own, received, steps):
    rows = own[0].shape[1] // steps
    return call(
        functools.partial(pair_sum_body, steps),
        "pair_sum",
        [shape((2 * W, rows), BF16)] * steps,
        [pltpu.VMEM((steps, 2 * W, rows), BF16)],
    )(*own, *received)


def z_sum_body(*refs):
    refs[-1][...] = summed(refs[:-1]).astype(BF16)


def z_sum(parts):
    return call(z_sum_body, "z_sum", shape(parts[0].shape, BF16))(*parts)


def plane_sum_body(own, diagonal, from_x, from_y, back, mine, other, scr):
    core, pair = lax.axis_index("core"), pair_of()
    rows, half = mine.shape
    span = half // 2
    for n, terms in enumerate(((from_x, from_y), (own, diagonal))):
        total = summed(terms).T.reshape(2, rows, span)
        scr[:, :, columns((pair ^ n) * span, span)] = total
    mine[...] = scr[core]
    other[:rows] = scr[1 - core]
    frames = back.shape[1]
    for n in range(2):
        other[rows + n * frames : rows + (n + 1) * frames] = back[n].astype(F32)


def plane_sum(parts, back):
    span, rows = parts[0].shape
    _, frames, half = back.shape
    return call(
        plane_sum_body,
        "plane_sum",
        [shape((rows // 2, half), F32), shape((rows // 2 + 2 * frames, half), F32)],
        [pltpu.VMEM((2, rows // 2, half), F32)],
    )(*parts, back)


def fold_body(odd0, odd1, even0, even1, out):
    core, pair = lax.axis_index("core"), pair_of()
    span = odd0.shape[2]
    for which, blocks in enumerate(((odd0, odd1), (even0, even1))):

        @pl.when(core == which)
        def _():
            for slot, x in enumerate(blocks):
                here = columns((pair ^ slot) * span, span)
                out[:, :, here] = x[...]


def fold(odd, even):
    _, frames, span = odd[0].shape
    return call(fold_body, "fold", shape((3, frames, 2 * span), F32))(*odd, *even)


def final_body(odd0, odd1, even0, even1, back, sib, band_mine, swapped, dq, dk, dv, band):
    core, pair = lax.axis_index("core"), pair_of()
    span, half = odd0.shape[2], band_mine.shape[1]
    rows, frames = band.shape[0], dq.shape[0]
    own, other = columns(core * half, half), columns((1 - core) * half, half)
    band[:, own] = band_mine[...]
    band[:, other] = swapped[:rows]
    dq[:, other] = sib[0].astype(BF16)
    for n, out in enumerate((dk, dv)):
        further = swapped[rows + n * frames : rows + (n + 1) * frames]
        out[:, other] = (sib[1 + n] + jnp.where(core == 1, further, 0.0)).astype(BF16)
    for which, blocks in enumerate(((even0, even1), (odd0, odd1))):

        @pl.when(core == which)
        def _():
            for slot, x in enumerate(blocks):
                inside = columns((pair ^ slot) * span, span)
                mine = columns((2 * which + (pair ^ slot)) * span, span)
                dq[:, mine] = x[0].astype(BF16)
                for n, out in enumerate((dk, dv)):
                    total = x[1 + n]
                    if which == 1:
                        total = total + back[n, :, inside].astype(F32)
                    out[:, mine] = total.astype(BF16)


def final(odd, even, back, sib, band_mine, swapped):
    rows, half = band_mine.shape
    outs = [shape((back.shape[1], 2 * half), BF16)] * 3 + [shape((rows, 2 * half), F32)]
    return call(final_body, "final", outs)(*odd, *even, back, sib, band_mine, swapped)


def local(query_rows, key_rows, value_rows, grad_out, pos_keys, bias_content, bias_position):
    n_high, n_z = lax.axis_size("dh"), lax.axis_size("z")
    width = query_rows.shape[2]

    def along_z(x, flip):
        return lax.ppermute(x, "z", [(s, s ^ flip) for s in range(n_z)])

    def around_z(x, steps):
        return lax.ppermute(x, "z", [(s, (s + steps) % n_z) for s in range(n_z)])

    def to_sibling(x):
        return lax.ppermute(x, "core", [(0, 1), (1, 0)])

    def in_plane(x, flip, cross=0):
        pairs = [
            (2 * d + c, 2 * (d ^ flip) + (c ^ cross)) for d in range(PLANE) for c in range(2)
        ]
        return lax.ppermute(x, ("dl", "core"), pairs)

    cut = band_cut(pos_keys)
    cuts = [cut] + [along_z(cut, k) for k in range(1, n_z)]
    own = [x[0] for x in (query_rows, key_rows, value_rows, grad_out)]
    sib = [to_sibling(x) for x in own]
    prev = around_z(odd_rows(*own[1:3], *sib[1:3]), 1)
    band_own, band_sib = band_pack(cuts)
    first_bands = [band_own, to_sibling(band_sib)]
    second_bands = [in_plane(band_own, 1), in_plane(band_sib, 2, 1)]
    biases = [bias_content.reshape(1, width), bias_position.reshape(1, width)]

    inputs = (own, sib, biases)
    first = odd_call(0, *inputs, first_bands, n_z)
    second = odd_call(1, *inputs, second_bands, n_z)
    first, second = lax.optimization_barrier((first, second))
    even0, back, g_x, g_y = even_call(0, *inputs, prev, first, prev)
    received = [in_plane(g_x, 1), in_plane(g_y, 2)]
    even1, back, *g_own = even_call(1, *inputs, prev, second, back)


    parts = pair_sum(g_own, received, n_z)
    *parts, odd0, even0 = lax.optimization_barrier((*parts, first[0], even0))
    odd, even = (odd0, second[0]), (even0, even1)
    out_sib = to_sibling(fold(odd, even))
    parts = [parts[0]] + [along_z(parts[k], k) for k in range(1, n_z)]
    *parts, back = lax.optimization_barrier((*parts, back))
    back = around_z(back, -1)
    total = z_sum(parts)
    step = 1
    while step < n_high:
        pairs = [(s, s ^ step) for s in range(n_high)]
        total = z_sum([total, lax.ppermute(total, "dh", pairs)])
        step *= 2
    planes = [in_plane(total, k) for k in (3, 1, 2)]
    mine, other = plane_sum([total, *planes], back)
    *rows, grad_pos = final(odd, even, back, out_sib, mine, to_sibling(other))
    return *[x[None] for x in rows], grad_pos


def solution(mesh):
    n_dp, n_blk = mesh.shape["dp"], mesh.shape["blk"]
    fine = Mesh(mesh.devices.reshape(n_dp // PLANE, PLANE, n_blk // 2, 2), ("dh", "dl", "z", "core"))
    rows = P(("dh", "dl"), ("z", "core"), None)
    band = P(("z", "core"), None)
    return jax.shard_map(
        local,
        mesh=fine,
        in_specs=(rows, rows, rows, rows, band, P(), P()),
        out_specs=(rows, rows, rows, band),
        check_vma=False,
    )
```

```python
import functools

import jax
import jax.numpy as jnp
from jax import lax
from jax.experimental import pallas as pl
from jax.experimental.pallas import tpu as pltpu
from jax.sharding import Mesh
from jax.sharding import PartitionSpec as P

DH = 64
W = 128
PLANE = 4
MIB = 2**20
F32 = jnp.float32
BF16 = jnp.bfloat16


def mm(a, b):
    return jnp.dot(a, b, preferred_element_type=F32)


def mm_nt(a, b):
    return lax.dot_general(a, b, (((1,), (1,)), ((), ())), preferred_element_type=F32)


def iota(shape, axis):
    return lax.broadcasted_iota(jnp.int32, shape, axis)


def as_bf16(hit):
    return hit.astype(F32).astype(BF16)


def shear(x, frames):
    rows = [
        pltpu.roll(x[r : r + frames], frames + 1, 1, stride=1, stride_axis=0)
        for r in range(0, x.shape[0], frames)
    ]
    return jnp.concatenate(rows, axis=0)


def columns(start, size):
    return pl.ds(pl.multiple_of(start, W), size)


class Masks:
    def __init__(self, frames):
        span = 2 * frames
        lane = iota((frames, W), 1)
        sub = iota((W, frames), 0)
        self.first = lane < DH
        self.lanes = [as_bf16(lane < DH), as_bf16(lane >= DH)]
        self.subs = [as_bf16(sub < DH), as_bf16(sub >= DH)]
        self.flip = as_bf16(iota((span, span), 0) + iota((span, span), 1) == span - 1)
        row = iota((span, span), 0) & (frames - 1)
        col = iota((span, span), 1)
        self.forward = (col + row >= frames - 1) & (col + row <= span - 2)
        back = (col - row >= 1) & (col - row <= frames)
        self.back = [as_bf16(back), as_bf16(~back)]

    def stack(self, x):
        return jnp.concatenate([x * self.lanes[0], x * self.lanes[1]], axis=0)

    def stack_t(self, x):
        x = x.T
        return jnp.concatenate([x * self.subs[0], x * self.subs[1]], axis=1)


def unit(masks, q, k, v, g, k_before, v_before, tables, bias_c, bias_p):
    frames = q.shape[0]
    factor = DH**-0.5
    band0, band1, band0_rev, band1_rev = tables
    kw = jnp.concatenate([k, k_before], axis=0)
    vw = jnp.concatenate([v, v_before], axis=0)
    qf = q.astype(F32)
    qc = (qf + bias_c).astype(BF16)
    qp = (qf + bias_p).astype(BF16)
    qp_stack = masks.stack(qp)
    content = mm_nt(masks.stack(qc), kw)
    merged = jnp.where(masks.forward, mm_nt(qp_stack, band0_rev), mm_nt(qp_stack, band1_rev))
    scores = (content + shear(merged, frames)) * factor
    e = jnp.exp(scores - jnp.max(scores, axis=1, keepdims=True))
    gw = mm_nt(masks.stack(g), vw)
    attention = e * (1.0 / jnp.sum(e, axis=1, keepdims=True))
    delta = jnp.sum(attention * gw, axis=1, keepdims=True)
    ds = (attention * (gw - delta) * factor).astype(BF16)
    placed = shear(mm(ds, masks.flip), frames).astype(BF16)
    d0, d1 = placed * masks.back[0], placed * masks.back[1]
    lhs = jnp.concatenate([ds, d0, d1], axis=1)
    rhs = jnp.concatenate([kw, band0, band1], axis=0)
    full = mm(lhs, rhs)
    dq = jnp.where(masks.first, full[:frames], full[frames:]).astype(BF16).astype(F32)
    dk = mm(masks.stack_t(qc), ds)
    dv = mm(masks.stack_t(g), attention.astype(BF16))
    qp_t = masks.stack_t(qp)
    g1 = mm(qp_t, d1)
    g_band = jnp.concatenate([mm(qp_t, d0), g1[:, frames:], g1[:, :frames]], axis=1)
    return dq, dk, dv, g_band


def call(body, name, out_shape, scratch=(), limit=8, **options):
    return pl.pallas_call(
        body,
        out_shape=out_shape,
        scratch_shapes=list(scratch),
        compiler_params=pltpu.CompilerParams(vmem_limit_bytes=limit * MIB),
        name=name,
        **options,
    )


def shape(dims, dtype):
    return jax.ShapeDtypeStruct(tuple(dims), dtype)


def pair_of():
    low = lax.axis_index("dl")
    return (low & 1) ^ (low >> 1)


def place(own, sib, scr, slot):
    core = lax.axis_index("core")
    span = scr.shape[3]
    here = columns((2 * core + (pair_of() ^ slot)) * span, span)
    for n, (a, b) in enumerate(zip(own, sib)):
        scr[n, core] = a[:, here]
        scr[n, 1 - core] = b[:, here]
    return here


def odd_body(steps, slot, *refs):
    own, sib, (bias_c, bias_p), bands = refs[0:4], refs[4:8], refs[8:10], refs[10:12]
    out, carry, g_out, tables, scr, band_scr = refs[12:]
    core = lax.axis_index("core")
    frames, span = scr.shape[2:]
    share = band_scr.shape[2]
    here = place(own, sib, scr, slot)
    bias_c, bias_p = bias_c[:, here], bias_p[:, here]
    band_scr[:, core] = bands[0][...].reshape(steps, share, span)
    band_scr[:, 1 - core] = bands[1][...].reshape(steps, share, span)
    band = band_scr[...].reshape(steps * 2 * share, span)
    masks = Masks(frames)
    band0, band1 = band[: 2 * frames], band[2 * frames :]
    band1 = jnp.concatenate([band1[frames:], band1[:frames]], axis=0)
    tables[0] = band0
    tables[1] = band1
    tables[2] = mm(masks.flip, band0).astype(BF16)
    tables[3] = mm(masks.flip, band1).astype(BF16)
    for j in range(span // W):
        at = slice(j * W, (j + 1) * W)
        dq, dk, dv, g_band = unit(
            masks,
            *[scr[n, 1, :, at] for n in range(4)],
            scr[1, 0, :, at],
            scr[2, 0, :, at],
            [tables[n, :, at] for n in range(4)],
            bias_c[:, at],
            bias_p[:, at],
        )
        out[0, :, at] = dq
        for n, term in enumerate((dk, dv)):
            out[1 + n, :, at] = term[:, :frames].T
            carry[n, :, at] = term[:, frames:].astype(BF16).T
        g_out[j] = g_band


def even_body(slot, *refs):
    own, sib, (bias_c, bias_p) = refs[0:4], refs[4:8], refs[8:10]
    prev, tables, carry, g_odd, back_done = refs[10:15]
    out, back = refs[15:17]
    g_outs, scr, back_scr = refs[17:-2], refs[-2], refs[-1]
    frames, span = scr.shape[2:]
    here = place(own, sib, scr, slot)
    bias_c, bias_p = bias_c[:, here], bias_p[:, here]
    inside = columns((pair_of() ^ slot) * span, span)
    done = columns((pair_of() ^ 1 ^ slot) * span, span)
    masks = Masks(frames)
    for j in range(span // W):
        at = slice(j * W, (j + 1) * W)
        mine = columns((pair_of() ^ slot) * span + j * W, W)
        dq, dk, dv, g_band = unit(
            masks,
            *[scr[n, 0, :, at] for n in range(4)],
            prev[0, :, mine],
            prev[1, :, mine],
            [tables[n, :, at] for n in range(4)],
            bias_c[:, at],
            bias_p[:, at],
        )
        out[0, :, at] = dq
        for n, term in enumerate((dk, dv)):
            out[1 + n, :, at] = term[:, :frames].T + carry[n, :, at].astype(F32)
            back_scr[n, :, at] = term[:, frames:].astype(BF16).T
        g_outs[j][...] = (g_odd[j] + g_band).astype(g_outs[j].dtype)
    back[:, :, inside] = back_scr[...]
    back[:, :, done] = back_done[:, :, done]


def cost(groups, frames):
    return pl.CostEstimate(
        flops=2 * groups * 20 * frames * (2 * frames) ** 2,
        bytes_accessed=64 * groups * frames * W,
        transcendentals=groups * 4 * frames * frames,
    )


def odd_call(slot, own, sib, biases, bands, steps):
    frames = own[0].shape[0]
    rows, span = bands[0].shape
    groups = span // W
    return call(
        functools.partial(odd_body, steps, slot),
        "odd_block",
        [
            shape((3, frames, span), F32),
            shape((2, frames, span), BF16),
            shape((groups, W, 2 * rows), F32),
            shape((4, rows, span), BF16),
        ],
        [
            pltpu.VMEM((4, 2, frames, span), BF16),
            pltpu.VMEM((steps, 2, rows // steps, span), BF16),
        ],
        limit=16,
        cost_estimate=cost(groups, frames),
    )(*own, *sib, *biases, *bands)


def even_call(slot, own, sib, biases, prev, odd, back):
    frames = own[0].shape[0]
    _, carry, g_odd, tables = odd
    groups, _, rows = g_odd.shape
    span = groups * W
    return call(
        functools.partial(even_body, slot),
        "even_block",
        [shape((3, frames, span), F32), shape((2, frames, 2 * span), BF16)]
        + [shape((W, rows), F32 if slot else BF16)] * groups,
        [pltpu.VMEM((4, 2, frames, span), BF16), pltpu.VMEM((2, frames, span), BF16)],
        limit=16,
        cost_estimate=cost(groups, frames),
    )(*own, *sib, *biases, prev, tables, carry, g_odd, back)


def band_cut_body(table, out):
    half = table.shape[1] // 2
    span = half // 2
    pair = pair_of()
    for n in range(2):
        out[:, n * span : (n + 1) * span] = table[:, columns(n * half + pair * span, span)]


def band_cut(table):
    rows, width = table.shape
    return call(band_cut_body, "band_cut", shape((rows, width // 2), BF16))(table)


def band_pack_body(steps, *refs):
    own, sib = refs[steps:]
    core, z = lax.axis_index("core"), lax.axis_index("z")
    span = own.shape[2]
    for n in range(steps):
        at = z ^ n
        own[at] = refs[n][:, columns(core * span, span)]
        sib[at] = refs[n][:, columns((1 - core) * span, span)]


def band_pack(parts):
    rows, width = parts[0].shape
    steps = len(parts)
    out = call(
        functools.partial(band_pack_body, steps),
        "band_pack",
        [shape((steps, rows, width // 2), BF16)] * 2,
    )(*parts)
    return [x.reshape(steps * rows, width // 2) for x in out]


def odd_rows_body(k, v, k_sib, v_sib, out):
    half = out.shape[2]
    core = lax.axis_index("core")
    for which, pair in enumerate(((k_sib, v_sib), (k, v))):

        @pl.when(core == which)
        def _():
            for n, x in enumerate(pair):
                out[n] = x[:, which * half : (which + 1) * half]


def odd_rows(*arrays):
    frames, width = arrays[0].shape
    return call(odd_rows_body, "odd_rows", shape((2, frames, width // 2), BF16))(*arrays)


def summed(refs):
    total = refs[0][...].astype(F32)
    for ref in refs[1:]:
        total = total + ref[...].astype(F32)
    return total


def pair_sum_body(steps, own0, own1, from_x, from_y, *refs):
    scr = refs[-1]
    z = lax.axis_index("z")
    rows = scr.shape[2]
    for n, (a, b) in enumerate(((own0, from_x), (own1, from_y))):
        total = (a[...] + b[...].astype(F32)).astype(BF16)
        for m in range(steps):
            scr[m, n * W : (n + 1) * W] = total[:, m * rows : (m + 1) * rows]
    for m in range(steps):
        refs[m][...] = scr[z ^ m]


def pair_sum(own, received, steps):
    rows = own[0].shape[1] // steps
    return call(
        functools.partial(pair_sum_body, steps),
        "pair_sum",
        [shape((2 * W, rows), BF16)] * steps,
        [pltpu.VMEM((steps, 2 * W, rows), BF16)],
    )(*own, *received)


def z_sum_body(*refs):
    refs[-1][...] = summed(refs[:-1]).astype(BF16)


def z_sum(parts):
    return call(z_sum_body, "z_sum", shape(parts[0].shape, BF16))(*parts)


def plane_sum_body(own, diagonal, from_x, from_y, mine, other, scr):
    core, pair = lax.axis_index("core"), pair_of()
    rows, half = mine.shape
    span = half // 2
    for n, terms in enumerate(((from_x, from_y), (own, diagonal))):
        total = summed(terms).T.reshape(2, rows, span)
        scr[:, :, columns((pair ^ n) * span, span)] = total
    mine[...] = scr[core]
    other[...] = scr[1 - core]


def plane_sum(parts):
    span, rows = parts[0].shape
    half = 2 * span
    return call(
        plane_sum_body,
        "plane_sum",
        [shape((rows // 2, half), F32)] * 2,
        [pltpu.VMEM((2, rows // 2, half), F32)],
    )(*parts)


def fold_body(odd0, odd1, even0, even1, out):
    core, pair = lax.axis_index("core"), pair_of()
    span = odd0.shape[2]
    for which, blocks in enumerate(((odd0, odd1), (even0, even1))):

        @pl.when(core == which)
        def _():
            for slot, x in enumerate(blocks):
                here = columns((pair ^ slot) * span, span)
                out[:, :, here] = x[...]


def fold(odd, even):
    _, frames, span = odd[0].shape
    return call(fold_body, "fold", shape((3, frames, 2 * span), F32))(*odd, *even)


def rows_final_body(odd0, odd1, even0, even1, back, sib, back_sib, dq, dk, dv):
    core, pair = lax.axis_index("core"), pair_of()
    span = odd0.shape[2]
    other = columns((1 - core) * 2 * span, 2 * span)
    dq[:, other] = sib[0].astype(BF16)
    for n, out in enumerate((dk, dv)):
        further = jnp.where(core == 1, back_sib[n].astype(F32), 0.0)
        out[:, other] = (sib[1 + n] + further).astype(BF16)
    for which, blocks in enumerate(((even0, even1), (odd0, odd1))):

        @pl.when(core == which)
        def _():
            for slot, x in enumerate(blocks):
                inside = columns((pair ^ slot) * span, span)
                mine = columns((2 * which + (pair ^ slot)) * span, span)
                dq[:, mine] = x[0].astype(BF16)
                for n, out in enumerate((dk, dv)):
                    total = x[1 + n]
                    if which == 1:
                        total = total + back[n, :, inside].astype(F32)
                    out[:, mine] = total.astype(BF16)


def rows_final(odd, even, back, sib, back_sib):
    frames, half = back.shape[1:]
    outs = [shape((frames, 2 * half), BF16)] * 3
    return call(rows_final_body, "rows_final", outs)(*odd, *even, back, sib, back_sib)


def band_final_body(mine, other, out):
    core = lax.axis_index("core")
    half = mine.shape[1]
    out[:, columns(core * half, half)] = mine[...]
    out[:, columns((1 - core) * half, half)] = other[...]


def band_final(mine, other):
    rows, half = mine.shape
    return call(band_final_body, "band_final", shape((rows, 2 * half), F32))(mine, other)


def local(query_rows, key_rows, value_rows, grad_out, pos_keys, bias_content, bias_position):
    n_high, n_z = lax.axis_size("dh"), lax.axis_size("z")
    width = query_rows.shape[2]

    def along_z(x, flip):
        return lax.ppermute(x, "z", [(s, s ^ flip) for s in range(n_z)])

    def around_z(x, steps):
        return lax.ppermute(x, "z", [(s, (s + steps) % n_z) for s in range(n_z)])

    def to_sibling(x):
        return lax.ppermute(x, "core", [(0, 1), (1, 0)])

    def in_plane(x, flip, cross=0):
        pairs = [
            (2 * d + c, 2 * (d ^ flip) + (c ^ cross)) for d in range(PLANE) for c in range(2)
        ]
        return lax.ppermute(x, ("dl", "core"), pairs)

    cut = band_cut(pos_keys)
    cuts = [cut] + [along_z(cut, k) for k in range(1, n_z)]
    own = [x[0] for x in (query_rows, key_rows, value_rows, grad_out)]
    sib = [to_sibling(x) for x in own]
    prev = around_z(odd_rows(*own[1:3], *sib[1:3]), 1)
    band_own, band_sib = band_pack(cuts)
    first_bands = [band_own, to_sibling(band_sib)]
    second_bands = [in_plane(band_own, 1), in_plane(band_sib, 2, 1)]
    biases = [bias_content.reshape(1, width), bias_position.reshape(1, width)]

    inputs = (own, sib, biases)
    first = odd_call(0, *inputs, first_bands, n_z)
    second = odd_call(1, *inputs, second_bands, n_z)
    first, second = lax.optimization_barrier((first, second))
    even0, back, g_x, g_y = even_call(0, *inputs, prev, first, prev)
    received = [in_plane(g_x, 1), in_plane(g_y, 2)]
    even1, back, *g_own = even_call(1, *inputs, prev, second, back)


    parts = pair_sum(g_own, received, n_z)
    parts = [along_z(parts[k], k) for k in range(n_z - 1, 0, -1)] + [parts[0]]
    *parts, back, odd0, even0 = lax.optimization_barrier((*parts, back, first[0], even0))
    odd, even = (odd0, second[0]), (even0, even1)
    back = around_z(back, -1)
    out_sib = to_sibling(fold(odd, even))
    total = z_sum(parts)
    step = 1
    while step < n_high:
        pairs = [(s, s ^ step) for s in range(n_high)]
        total = z_sum([total, lax.ppermute(total, "dh", pairs)])
        step *= 2
    planes = [in_plane(total, k) for k in (3, 1, 2)]
    *planes, back = lax.optimization_barrier((*planes, back))
    back_sib = to_sibling(back)
    mine, other = plane_sum([total, *planes])
    other = to_sibling(other)
    rows = rows_final(odd, even, back, out_sib, back_sib)
    *rows, mine, other = lax.optimization_barrier((*rows, mine, other))
    return *[x[None] for x in rows], band_final(mine, other)


def solution(mesh):
    n_dp, n_blk = mesh.shape["dp"], mesh.shape["blk"]
    fine = Mesh(mesh.devices.reshape(n_dp // PLANE, PLANE, n_blk // 2, 2), ("dh", "dl", "z", "core"))
    rows = P(("dh", "dl"), ("z", "core"), None)
    band = P(("z", "core"), None)
    return jax.shard_map(
        local,
        mesh=fine,
        in_specs=(rows, rows, rows, rows, band, P(), P()),
        out_specs=(rows, rows, rows, band),
        check_vma=False,
    )
```

```python
import functools

import jax
import jax.numpy as jnp
from jax import lax
from jax.experimental import pallas as pl
from jax.experimental.pallas import tpu as pltpu
from jax.sharding import Mesh
from jax.sharding import PartitionSpec as P

DH = 64
W = 128
PLANE = 4
MIB = 2**20
F32 = jnp.float32
BF16 = jnp.bfloat16


def mm(a, b):
    return jnp.dot(a, b, preferred_element_type=F32)


def mm_nt(a, b):
    return lax.dot_general(a, b, (((1,), (1,)), ((), ())), preferred_element_type=F32)


def iota(shape, axis):
    return lax.broadcasted_iota(jnp.int32, shape, axis)


def as_bf16(hit):
    return hit.astype(F32).astype(BF16)


def shear(x, frames):
    rows = [
        pltpu.roll(x[r : r + frames], frames + 1, 1, stride=1, stride_axis=0)
        for r in range(0, x.shape[0], frames)
    ]
    return jnp.concatenate(rows, axis=0)


def columns(start, size):
    return pl.ds(pl.multiple_of(start, W), size)


class Masks:
    def __init__(self, frames):
        span = 2 * frames
        lane = iota((frames, W), 1)
        sub = iota((W, frames), 0)
        self.first = lane < DH
        self.lanes = [as_bf16(lane < DH), as_bf16(lane >= DH)]
        self.subs = [as_bf16(sub < DH), as_bf16(sub >= DH)]
        self.flip = as_bf16(iota((span, span), 0) + iota((span, span), 1) == span - 1)
        row = iota((span, span), 0) & (frames - 1)
        col = iota((span, span), 1)
        self.forward = (col + row >= frames - 1) & (col + row <= span - 2)
        back = (col - row >= 1) & (col - row <= frames)
        self.back = [as_bf16(back), as_bf16(~back)]

    def stack(self, x):
        return jnp.concatenate([x * self.lanes[0], x * self.lanes[1]], axis=0)

    def stack_t(self, x):
        x = x.T
        return jnp.concatenate([x * self.subs[0], x * self.subs[1]], axis=1)


def unit(masks, q, k, v, g, k_before, v_before, tables, bias_c, bias_p):
    frames = q.shape[0]
    factor = DH**-0.5
    band0, band1, band0_rev, band1_rev = tables
    kw = jnp.concatenate([k, k_before], axis=0)
    vw = jnp.concatenate([v, v_before], axis=0)
    qf = q.astype(F32)
    qc = (qf + bias_c).astype(BF16)
    qp = (qf + bias_p).astype(BF16)
    qp_stack = masks.stack(qp)
    content = mm_nt(masks.stack(qc), kw)
    merged = jnp.where(masks.forward, mm_nt(qp_stack, band0_rev), mm_nt(qp_stack, band1_rev))
    scores = (content + shear(merged, frames)) * factor
    e = jnp.exp(scores - jnp.max(scores, axis=1, keepdims=True))
    gw = mm_nt(masks.stack(g), vw)
    attention = e * (1.0 / jnp.sum(e, axis=1, keepdims=True))
    delta = jnp.sum(attention * gw, axis=1, keepdims=True)
    ds = (attention * (gw - delta) * factor).astype(BF16)
    placed = shear(mm(ds, masks.flip), frames).astype(BF16)
    d0, d1 = placed * masks.back[0], placed * masks.back[1]
    lhs = jnp.concatenate([ds, d0, d1], axis=1)
    rhs = jnp.concatenate([kw, band0, band1], axis=0)
    full = mm(lhs, rhs)
    dq = jnp.where(masks.first, full[:frames], full[frames:]).astype(BF16).astype(F32)
    dk = mm(masks.stack_t(qc), ds)
    dv = mm(masks.stack_t(g), attention.astype(BF16))
    qp_t = masks.stack_t(qp)
    g1 = mm(qp_t, d1)
    g_band = jnp.concatenate([mm(qp_t, d0), g1[:, frames:], g1[:, :frames]], axis=1)
    return dq, dk, dv, g_band


def call(body, name, out_shape, scratch=(), limit=8, **options):
    return pl.pallas_call(
        body,
        out_shape=out_shape,
        scratch_shapes=list(scratch),
        compiler_params=pltpu.CompilerParams(vmem_limit_bytes=limit * MIB),
        name=name,
        **options,
    )


def shape(dims, dtype):
    return jax.ShapeDtypeStruct(tuple(dims), dtype)


def pair_of():
    low = lax.axis_index("dl")
    return (low & 1) ^ (low >> 1)


def place(own, sib, scr, slot):
    core = lax.axis_index("core")
    span = scr.shape[3]
    here = columns((2 * core + (pair_of() ^ slot)) * span, span)
    for n, (a, b) in enumerate(zip(own, sib)):
        scr[n, core] = a[:, here]
        scr[n, 1 - core] = b[:, here]
    return here


def tables_body(steps, part0, part1, out, scr):
    core = lax.axis_index("core")
    share, span = scr.shape[2:]
    scr[:, core] = part0[...].reshape(steps, share, span)
    scr[:, 1 - core] = part1[...].reshape(steps, share, span)
    band = scr[...].reshape(steps * 2 * share, span)
    frames = band.shape[0] // 4
    flip = as_bf16(iota((2 * frames,) * 2, 0) + iota((2 * frames,) * 2, 1) == 2 * frames - 1)
    band0, band1 = band[: 2 * frames], band[2 * frames :]
    band1 = jnp.concatenate([band1[frames:], band1[:frames]], axis=0)
    out[0] = band0
    out[1] = band1
    out[2] = mm(flip, band0).astype(BF16)
    out[3] = mm(flip, band1).astype(BF16)


def band_tables(parts, steps):
    rows, span = parts[0].shape
    return call(
        functools.partial(tables_body, steps),
        "band_tables",
        shape((4, rows, span), BF16),
        [pltpu.VMEM((steps, 2, rows // steps, span), BF16)],
    )(*parts)


def odd_body(slot, *refs):
    own, sib, (bias_c, bias_p), tables = refs[0:4], refs[4:8], refs[8:10], refs[10]
    even, g_even = refs[11 : 11 + 2 * slot] or (None, None)
    out, crossing = refs[11 + 2 * slot : 13 + 2 * slot]
    g_outs, scr = refs[13 + 2 * slot : -1], refs[-1]
    frames, span = scr.shape[2:]
    here = place(own, sib, scr, slot)
    bias_c, bias_p = bias_c[:, here], bias_p[:, here]
    masks = Masks(frames)
    for j in range(span // W):
        at = slice(j * W, (j + 1) * W)
        dq, dk, dv, g_band = unit(
            masks,
            *[scr[n, 1, :, at] for n in range(4)],
            scr[1, 0, :, at],
            scr[2, 0, :, at],
            [tables[n, :, at] for n in range(4)],
            bias_c[:, at],
            bias_p[:, at],
        )
        out[0, :, at] = dq
        if slot:
            crossing[0, :, at] = even[0, :, at]
            g_band = g_band + g_even[j]
        for n, term in enumerate((dk, dv)):
            out[1 + n, :, at] = term[:, :frames].T
            carry = term[:, frames:].astype(BF16).T
            if slot:
                crossing[1 + n, :, at] = even[1 + n, :, at] + carry.astype(F32)
            else:
                crossing[n, :, at] = carry
        if slot:
            g_outs[j][...] = g_band
        else:
            g_outs[0][j] = g_band


def even_body(slot, *refs):
    own, sib, (bias_c, bias_p), tables, prev = refs[0:4], refs[4:8], refs[8:10], refs[10], refs[11]
    given, refs = refs[12 : 14 - slot], refs[14 - slot :]
    out, back, scr, back_scr = *refs[:2], *refs[-2:]
    g_outs = refs[2:-2]
    frames, span = scr.shape[2:]
    here = place(own, sib, scr, slot)
    bias_c, bias_p = bias_c[:, here], bias_p[:, here]
    inside = columns((pair_of() ^ slot) * span, span)
    masks = Masks(frames)
    for j in range(span // W):
        at = slice(j * W, (j + 1) * W)
        mine = columns((pair_of() ^ slot) * span + j * W, W)
        dq, dk, dv, g_band = unit(
            masks,
            *[scr[n, 0, :, at] for n in range(4)],
            prev[0, :, mine],
            prev[1, :, mine],
            [tables[n, :, at] for n in range(4)],
            bias_c[:, at],
            bias_p[:, at],
        )
        out[0, :, at] = dq
        for n, term in enumerate((dk, dv)):
            total = term[:, :frames].T
            if not slot:
                total = total + given[0][n, :, at].astype(F32)
            out[1 + n, :, at] = total
            back_scr[n, :, at] = term[:, frames:].astype(BF16).T
        if slot:
            g_outs[0][j] = g_band
        else:
            g_outs[j][...] = (given[1][j] + g_band).astype(BF16)
    back[:, :, inside] = back_scr[...]
    if slot:
        done = columns((pair_of() ^ 1 ^ slot) * span, span)
        back[:, :, done] = given[0][:, :, done]


def cost(groups, frames, share=1):
    return pl.CostEstimate(
        flops=2 * groups * 20 * frames * (2 * frames) ** 2 // share,
        bytes_accessed=64 * groups * frames * W // share,
        transcendentals=groups * 4 * frames * frames // share,
    )


def odd_call(slot, own, sib, biases, tables, given=()):
    frames = own[0].shape[0]
    _, rows, span = tables.shape
    groups = span // W
    g_shapes = [shape((W, 2 * rows), F32)] * groups if slot else [shape((groups, W, 2 * rows), F32)]
    crossing = shape((3, frames, span), F32) if slot else shape((2, frames, span), BF16)
    return call(
        functools.partial(odd_body, slot),
        "odd_block",
        [shape((3, frames, span), F32), crossing] + g_shapes,
        [pltpu.VMEM((4, 2, frames, span), BF16)],
        limit=16,
        cost_estimate=cost(groups, frames, 8 if slot else 1),
    )(*own, *sib, *biases, tables, *given)


def even_call(slot, own, sib, biases, tables, prev, given):
    frames = own[0].shape[0]
    _, rows, span = tables.shape
    groups = span // W
    g_shapes = [shape((groups, W, 2 * rows), F32)] if slot else [shape((W, 2 * rows), BF16)] * groups
    return call(
        functools.partial(even_body, slot),
        "even_block",
        [shape((3, frames, span), F32), shape((2, frames, 2 * span), BF16)] + g_shapes,
        [pltpu.VMEM((4, 2, frames, span), BF16), pltpu.VMEM((2, frames, span), BF16)],
        limit=16,
        cost_estimate=cost(groups, frames),
    )(*own, *sib, *biases, tables, prev, *given)


def band_cut_body(table, out):
    half = table.shape[1] // 2
    span = half // 2
    pair = pair_of()
    for n in range(2):
        out[:, n * span : (n + 1) * span] = table[:, columns(n * half + pair * span, span)]


def band_cut(table):
    rows, width = table.shape
    return call(band_cut_body, "band_cut", shape((rows, width // 2), BF16))(table)


def band_pack_body(steps, *refs):
    own, sib = refs[steps:]
    core, z = lax.axis_index("core"), lax.axis_index("z")
    span = own.shape[2]
    for n in range(steps):
        at = z ^ n
        own[at] = refs[n][:, columns(core * span, span)]
        sib[at] = refs[n][:, columns((1 - core) * span, span)]


def band_pack(parts):
    rows, width = parts[0].shape
    steps = len(parts)
    out = call(
        functools.partial(band_pack_body, steps),
        "band_pack",
        [shape((steps, rows, width // 2), BF16)] * 2,
    )(*parts)
    return [x.reshape(steps * rows, width // 2) for x in out]


def odd_rows_body(k, v, k_sib, v_sib, out):
    half = out.shape[2]
    core = lax.axis_index("core")
    for which, pair in enumerate(((k_sib, v_sib), (k, v))):

        @pl.when(core == which)
        def _():
            for n, x in enumerate(pair):
                out[n] = x[:, which * half : (which + 1) * half]


def odd_rows(*arrays):
    frames, width = arrays[0].shape
    return call(odd_rows_body, "odd_rows", shape((2, frames, width // 2), BF16))(*arrays)


def summed(refs):
    total = refs[0][...].astype(F32)
    for ref in refs[1:]:
        total = total + ref[...].astype(F32)
    return total


def pair_sum_body(steps, own0, own1, from_x, from_y, *refs):
    scr = refs[-1]
    z = lax.axis_index("z")
    rows = scr.shape[2]
    for n, (a, b) in enumerate(((own0, from_x), (own1, from_y))):
        total = (a[...] + b[...].astype(F32)).astype(BF16)
        for m in range(steps):
            scr[m, n * W : (n + 1) * W] = total[:, m * rows : (m + 1) * rows]
    for m in range(steps):
        refs[m][...] = scr[z ^ m]


def pair_sum(own, received, steps):
    rows = own[0].shape[1] // steps
    return call(
        functools.partial(pair_sum_body, steps),
        "pair_sum",
        [shape((2 * W, rows), BF16)] * steps,
        [pltpu.VMEM((steps, 2 * W, rows), BF16)],
    )(*own, *received)


def z_sum_body(*refs):
    refs[-1][...] = summed(refs[:-1]).astype(BF16)


def z_sum(parts):
    return call(z_sum_body, "z_sum", shape(parts[0].shape, BF16))(*parts)


def plane_sum_body(own, diagonal, from_x, from_y, mine, other, scr):
    core, pair = lax.axis_index("core"), pair_of()
    rows, half = mine.shape
    span = half // 2
    for n, terms in enumerate(((from_x, from_y), (own, diagonal))):
        total = summed(terms).T.reshape(2, rows, span)
        scr[:, :, columns((pair ^ n) * span, span)] = total
    mine[...] = scr[core]
    other[...] = scr[1 - core]


def plane_sum(parts):
    span, rows = parts[0].shape
    half = 2 * span
    return call(
        plane_sum_body,
        "plane_sum",
        [shape((rows // 2, half), F32)] * 2,
        [pltpu.VMEM((2, rows // 2, half), F32)],
    )(*parts)


def fold_body(odd0, odd1, even0, even1, out):
    core, pair = lax.axis_index("core"), pair_of()
    span = odd0.shape[2]
    for which, blocks in enumerate(((odd0, odd1), (even0, even1))):

        @pl.when(core == which)
        def _():
            for slot, x in enumerate(blocks):
                here = columns((pair ^ slot) * span, span)
                out[:, :, here] = x[...]


def fold(odd, even):
    _, frames, span = odd[0].shape
    return call(fold_body, "fold", shape((3, frames, 2 * span), F32))(*odd, *even)


def rows_final_body(odd0, odd1, even0, even1, back, sib, back_sib, dq, dk, dv):
    core, pair = lax.axis_index("core"), pair_of()
    span = odd0.shape[2]
    other = columns((1 - core) * 2 * span, 2 * span)
    dq[:, other] = sib[0].astype(BF16)
    for n, out in enumerate((dk, dv)):
        further = jnp.where(core == 1, back_sib[n].astype(F32), 0.0)
        out[:, other] = (sib[1 + n] + further).astype(BF16)
    for which, blocks in enumerate(((even0, even1), (odd0, odd1))):

        @pl.when(core == which)
        def _():
            for slot, x in enumerate(blocks):
                inside = columns((pair ^ slot) * span, span)
                mine = columns((2 * which + (pair ^ slot)) * span, span)
                dq[:, mine] = x[0].astype(BF16)
                for n, out in enumerate((dk, dv)):
                    total = x[1 + n]
                    if which == 1:
                        total = total + back[n, :, inside].astype(F32)
                    out[:, mine] = total.astype(BF16)


def rows_final(odd, even, back, sib, back_sib):
    frames, half = back.shape[1:]
    outs = [shape((frames, 2 * half), BF16)] * 3
    return call(rows_final_body, "rows_final", outs)(*odd, *even, back, sib, back_sib)


def band_final_body(mine, other, out):
    core = lax.axis_index("core")
    half = mine.shape[1]
    out[:, columns(core * half, half)] = mine[...]
    out[:, columns((1 - core) * half, half)] = other[...]


def band_final(mine, other):
    rows, half = mine.shape
    return call(band_final_body, "band_final", shape((rows, 2 * half), F32))(mine, other)


def local(query_rows, key_rows, value_rows, grad_out, pos_keys, bias_content, bias_position):
    n_high, n_z = lax.axis_size("dh"), lax.axis_size("z")
    width = query_rows.shape[2]

    def along_z(x, flip):
        return lax.ppermute(x, "z", [(s, s ^ flip) for s in range(n_z)])

    def around_z(x, steps):
        return lax.ppermute(x, "z", [(s, (s + steps) % n_z) for s in range(n_z)])

    def to_sibling(x):
        return lax.ppermute(x, "core", [(0, 1), (1, 0)])

    def in_plane(x, flip, cross=0):
        pairs = [
            (2 * d + c, 2 * (d ^ flip) + (c ^ cross)) for d in range(PLANE) for c in range(2)
        ]
        return lax.ppermute(x, ("dl", "core"), pairs)

    cut = band_cut(pos_keys)
    cuts = [cut] + [along_z(cut, k) for k in range(1, n_z)]
    own = [x[0] for x in (query_rows, key_rows, value_rows, grad_out)]
    sib = [to_sibling(x) for x in own]
    *cuts, sib_k, sib_v = lax.optimization_barrier((*cuts, *sib[1:3]))
    prev = around_z(odd_rows(*own[1:3], sib_k, sib_v), 1)
    band_own, band_sib = band_pack(cuts)
    first_tables = band_tables([band_own, to_sibling(band_sib)], n_z)
    second_bands = [in_plane(band_own, 1), in_plane(band_sib, 2, 1)]
    biases = [bias_content.reshape(1, width), bias_position.reshape(1, width)]

    inputs = (own, sib, biases)
    odd0, carry, g_first = odd_call(0, *inputs, first_tables)
    even0, back, g_x, g_y = even_call(0, *inputs, first_tables, prev, (carry, g_first))
    received = [in_plane(g_x, 1), in_plane(g_y, 2)]
    *second_bands, even0 = lax.optimization_barrier((*second_bands, even0))
    second_tables = band_tables(second_bands, n_z)
    even1, back, g_second = even_call(1, *inputs, second_tables, prev, (back,))
    back = around_z(back, -1)
    odd1, even1, *g_own = odd_call(1, *inputs, second_tables, (even1, g_second))

    parts = pair_sum(g_own, received, n_z)
    parts = [along_z(parts[k], k) for k in range(n_z - 1, 0, -1)] + [parts[0]]
    *parts, odd0, even0, back = lax.optimization_barrier((*parts, odd0, even0, back))
    odd, even = (odd0, odd1), (even0, even1)
    out_sib = to_sibling(fold(odd, even))
    total = z_sum(parts)
    step = 1
    while step < n_high:
        pairs = [(s, s ^ step) for s in range(n_high)]
        total = z_sum([total, lax.ppermute(total, "dh", pairs)])
        step *= 2
    planes = [in_plane(total, k) for k in (3, 1, 2)]
    back_sib = to_sibling(back)
    mine, other = plane_sum([total, *planes])
    other = to_sibling(other)
    rows = rows_final(odd, even, back, out_sib, back_sib)
    *rows, mine, other = lax.optimization_barrier((*rows, mine, other))
    return *[x[None] for x in rows], band_final(mine, other)


def solution(mesh):
    n_dp, n_blk = mesh.shape["dp"], mesh.shape["blk"]
    fine = Mesh(mesh.devices.reshape(n_dp // PLANE, PLANE, n_blk // 2, 2), ("dh", "dl", "z", "core"))
    rows = P(("dh", "dl"), ("z", "core"), None)
    band = P(("z", "core"), None)
    return jax.shard_map(
        local,
        mesh=fine,
        in_specs=(rows, rows, rows, rows, band, P(), P()),
        out_specs=(rows, rows, rows, band),
        check_vma=False,
    )
```

```python
import functools

import jax
import jax.numpy as jnp
from jax import lax
from jax.experimental import pallas as pl
from jax.experimental.pallas import tpu as pltpu
from jax.sharding import Mesh
from jax.sharding import PartitionSpec as P

DH = 64
W = 128
PLANE = 4
MIB = 2**20
F32 = jnp.float32
BF16 = jnp.bfloat16


def mm(a, b):
    return jnp.dot(a, b, preferred_element_type=F32)


def mm_nt(a, b):
    return lax.dot_general(a, b, (((1,), (1,)), ((), ())), preferred_element_type=F32)


def iota(shape, axis):
    return lax.broadcasted_iota(jnp.int32, shape, axis)


def as_bf16(hit):
    return hit.astype(F32).astype(BF16)


def shear(x, frames):
    rows = [
        pltpu.roll(x[r : r + frames], frames + 1, 1, stride=1, stride_axis=0)
        for r in range(0, x.shape[0], frames)
    ]
    return jnp.concatenate(rows, axis=0)


def columns(start, size):
    return pl.ds(pl.multiple_of(start, W), size)


class Masks:
    def __init__(self, frames):
        span = 2 * frames
        lane = iota((frames, W), 1)
        sub = iota((W, frames), 0)
        self.first = lane < DH
        self.lanes = [as_bf16(lane < DH), as_bf16(lane >= DH)]
        self.subs = [as_bf16(sub < DH), as_bf16(sub >= DH)]
        self.flip = as_bf16(iota((span, span), 0) + iota((span, span), 1) == span - 1)
        row = iota((span, span), 0) & (frames - 1)
        col = iota((span, span), 1)
        self.forward = (col + row >= frames - 1) & (col + row <= span - 2)
        back = (col - row >= 1) & (col - row <= frames)
        self.back = [as_bf16(back), as_bf16(~back)]

    def stack(self, x):
        return jnp.concatenate([x * self.lanes[0], x * self.lanes[1]], axis=0)

    def stack_t(self, x):
        x = x.T
        return jnp.concatenate([x * self.subs[0], x * self.subs[1]], axis=1)


def unit(masks, q, k, v, g, k_before, v_before, tables, bias_c, bias_p):
    frames = q.shape[0]
    factor = DH**-0.5
    band0, band1, band0_rev, band1_rev = tables
    kw = jnp.concatenate([k, k_before], axis=0)
    vw = jnp.concatenate([v, v_before], axis=0)
    qf = q.astype(F32)
    qc = (qf + bias_c).astype(BF16)
    qp = (qf + bias_p).astype(BF16)
    qp_stack = masks.stack(qp)
    content = mm_nt(masks.stack(qc), kw)
    merged = jnp.where(masks.forward, mm_nt(qp_stack, band0_rev), mm_nt(qp_stack, band1_rev))
    scores = (content + shear(merged, frames)) * factor
    e = jnp.exp(scores - jnp.max(scores, axis=1, keepdims=True))
    gw = mm_nt(masks.stack(g), vw)
    attention = e * (1.0 / jnp.sum(e, axis=1, keepdims=True))
    delta = jnp.sum(attention * gw, axis=1, keepdims=True)
    ds = (attention * (gw - delta) * factor).astype(BF16)
    placed = shear(mm(ds, masks.flip), frames).astype(BF16)
    d0, d1 = placed * masks.back[0], placed * masks.back[1]
    lhs = jnp.concatenate([ds, d0, d1], axis=1)
    rhs = jnp.concatenate([kw, band0, band1], axis=0)
    full = mm(lhs, rhs)
    dq = jnp.where(masks.first, full[:frames], full[frames:]).astype(BF16).astype(F32)
    dk = mm(masks.stack_t(qc), ds)
    dv = mm(masks.stack_t(g), attention.astype(BF16))
    qp_t = masks.stack_t(qp)
    g1 = mm(qp_t, d1)
    g_band = jnp.concatenate([mm(qp_t, d0), g1[:, frames:], g1[:, :frames]], axis=1)
    return dq, dk, dv, g_band


def call(body, name, out_shape, scratch=(), limit=8, **options):
    return pl.pallas_call(
        body,
        out_shape=out_shape,
        scratch_shapes=list(scratch),
        compiler_params=pltpu.CompilerParams(vmem_limit_bytes=limit * MIB),
        name=name,
        **options,
    )


def shape(dims, dtype):
    return jax.ShapeDtypeStruct(tuple(dims), dtype)


def pair_of():
    low = lax.axis_index("dl")
    return (low & 1) ^ (low >> 1)


def place(own, sib, scr, slot):
    core = lax.axis_index("core")
    span = scr.shape[3]
    here = columns((2 * core + (pair_of() ^ slot)) * span, span)
    for n, (a, b) in enumerate(zip(own, sib)):
        scr[n, core] = a[:, here]
        scr[n, 1 - core] = b[:, here]
    return here


def odd_body(steps, slot, *refs):
    own, sib, (bias_c, bias_p), bands = refs[0:4], refs[4:8], refs[8:10], refs[10:12]
    out, carry, g_out, tables, scr, band_scr = refs[12:]
    core = lax.axis_index("core")
    frames, span = scr.shape[2:]
    share = band_scr.shape[2]
    here = place(own, sib, scr, slot)
    bias_c, bias_p = bias_c[:, here], bias_p[:, here]
    band_scr[:, core] = bands[0][...].reshape(steps, share, span)
    band_scr[:, 1 - core] = bands[1][...].reshape(steps, share, span)
    band = band_scr[...].reshape(steps * 2 * share, span)
    masks = Masks(frames)
    band0, band1 = band[: 2 * frames], band[2 * frames :]
    band1 = jnp.concatenate([band1[frames:], band1[:frames]], axis=0)
    tables[0] = band0
    tables[1] = band1
    tables[2] = mm(masks.flip, band0).astype(BF16)
    tables[3] = mm(masks.flip, band1).astype(BF16)
    for j in range(span // W):
        at = slice(j * W, (j + 1) * W)
        dq, dk, dv, g_band = unit(
            masks,
            *[scr[n, 1, :, at] for n in range(4)],
            scr[1, 0, :, at],
            scr[2, 0, :, at],
            [tables[n, :, at] for n in range(4)],
            bias_c[:, at],
            bias_p[:, at],
        )
        out[0, :, at] = dq
        for n, term in enumerate((dk, dv)):
            out[1 + n, :, at] = term[:, :frames].T
            carry[n, :, at] = term[:, frames:].astype(BF16).T
        g_out[j] = g_band


def even_body(slot, *refs):
    own, sib, (bias_c, bias_p) = refs[0:4], refs[4:8], refs[8:10]
    prev, tables, carry, g_odd, back_done = refs[10:15]
    out, back = refs[15:17]
    g_outs, scr, back_scr = refs[17:-2], refs[-2], refs[-1]
    frames, span = scr.shape[2:]
    here = place(own, sib, scr, slot)
    bias_c, bias_p = bias_c[:, here], bias_p[:, here]
    inside = columns((pair_of() ^ slot) * span, span)
    done = columns((pair_of() ^ 1 ^ slot) * span, span)
    masks = Masks(frames)
    for j in range(span // W):
        at = slice(j * W, (j + 1) * W)
        mine = columns((pair_of() ^ slot) * span + j * W, W)
        dq, dk, dv, g_band = unit(
            masks,
            *[scr[n, 0, :, at] for n in range(4)],
            prev[0, :, mine],
            prev[1, :, mine],
            [tables[n, :, at] for n in range(4)],
            bias_c[:, at],
            bias_p[:, at],
        )
        out[0, :, at] = dq
        for n, term in enumerate((dk, dv)):
            out[1 + n, :, at] = term[:, :frames].T + carry[n, :, at].astype(F32)
            back_scr[n, :, at] = term[:, frames:].astype(BF16).T
        g_outs[j][...] = (g_odd[j] + g_band).astype(g_outs[j].dtype)
    back[:, :, inside] = back_scr[...]
    back[:, :, done] = back_done[:, :, done]


def cost(groups, frames):
    return pl.CostEstimate(
        flops=2 * groups * 20 * frames * (2 * frames) ** 2,
        bytes_accessed=64 * groups * frames * W,
        transcendentals=groups * 4 * frames * frames,
    )


def odd_call(slot, own, sib, biases, bands, steps):
    frames = own[0].shape[0]
    rows, span = bands[0].shape
    groups = span // W
    return call(
        functools.partial(odd_body, steps, slot),
        "odd_block",
        [
            shape((3, frames, span), F32),
            shape((2, frames, span), BF16),
            shape((groups, W, 2 * rows), F32),
            shape((4, rows, span), BF16),
        ],
        [
            pltpu.VMEM((4, 2, frames, span), BF16),
            pltpu.VMEM((steps, 2, rows // steps, span), BF16),
        ],
        limit=16,
        cost_estimate=cost(groups, frames),
    )(*own, *sib, *biases, *bands)


def even_call(slot, own, sib, biases, prev, odd, back):
    frames = own[0].shape[0]
    _, carry, g_odd, tables = odd
    groups, _, rows = g_odd.shape
    span = groups * W
    return call(
        functools.partial(even_body, slot),
        "even_block",
        [shape((3, frames, span), F32), shape((2, frames, 2 * span), BF16)]
        + [shape((W, rows), F32 if slot else BF16)] * groups,
        [pltpu.VMEM((4, 2, frames, span), BF16), pltpu.VMEM((2, frames, span), BF16)],
        limit=16,
        cost_estimate=cost(groups, frames),
    )(*own, *sib, *biases, prev, tables, carry, g_odd, back)


def band_cut_body(table, out):
    half = table.shape[1] // 2
    span = half // 2
    pair = pair_of()
    for n in range(2):
        out[:, n * span : (n + 1) * span] = table[:, columns(n * half + pair * span, span)]


def band_cut(table):
    rows, width = table.shape
    return call(band_cut_body, "band_cut", shape((rows, width // 2), BF16))(table)


def band_pack_body(steps, *refs):
    own, sib = refs[steps:]
    core, z = lax.axis_index("core"), lax.axis_index("z")
    span = own.shape[2]
    for n in range(steps):
        at = z ^ n
        own[at] = refs[n][:, columns(core * span, span)]
        sib[at] = refs[n][:, columns((1 - core) * span, span)]


def band_pack(parts):
    rows, width = parts[0].shape
    steps = len(parts)
    out = call(
        functools.partial(band_pack_body, steps),
        "band_pack",
        [shape((steps, rows, width // 2), BF16)] * 2,
    )(*parts)
    return [x.reshape(steps * rows, width // 2) for x in out]


def own_half_body(k, v, out):
    half = out.shape[2]
    here = columns(lax.axis_index("core") * half, half)
    out[0] = k[:, here]
    out[1] = v[:, here]


def own_half(k, v):
    frames, width = k.shape
    return call(own_half_body, "own_half", shape((2, frames, width // 2), BF16))(k, v)


def odd_rows_body(own, k_sib, v_sib, out):
    half = out.shape[2]
    core = lax.axis_index("core")

    @pl.when(core == 0)
    def _():
        out[0] = k_sib[:, :half]
        out[1] = v_sib[:, :half]

    @pl.when(core == 1)
    def _():
        out[...] = own[...]


def odd_rows(own, k_sib, v_sib):
    return call(odd_rows_body, "odd_rows", shape(own.shape, BF16))(own, k_sib, v_sib)


def summed(refs):
    total = refs[0][...].astype(F32)
    for ref in refs[1:]:
        total = total + ref[...].astype(F32)
    return total


def pair_sum_body(steps, own0, own1, from_x, from_y, *refs):
    scr = refs[-1]
    z = lax.axis_index("z")
    rows = scr.shape[2]
    for n, (a, b) in enumerate(((own0, from_x), (own1, from_y))):
        total = (a[...] + b[...].astype(F32)).astype(BF16)
        for m in range(steps):
            scr[m, n * W : (n + 1) * W] = total[:, m * rows : (m + 1) * rows]
    for m in range(steps):
        refs[m][...] = scr[z ^ m]


def pair_sum(own, received, steps):
    rows = own[0].shape[1] // steps
    return call(
        functools.partial(pair_sum_body, steps),
        "pair_sum",
        [shape((2 * W, rows), BF16)] * steps,
        [pltpu.VMEM((steps, 2 * W, rows), BF16)],
    )(*own, *received)


def z_sum_body(*refs):
    refs[-1][...] = summed(refs[:-1]).astype(BF16)


def z_sum(parts):
    return call(z_sum_body, "z_sum", shape(parts[0].shape, BF16))(*parts)


def plane_sum_body(own, diagonal, from_x, from_y, mine, other, scr):
    core, pair = lax.axis_index("core"), pair_of()
    rows, half = mine.shape
    span = half // 2
    for n, terms in enumerate(((from_x, from_y), (own, diagonal))):
        total = summed(terms).T.reshape(2, rows, span)
        scr[:, :, columns((pair ^ n) * span, span)] = total
    mine[...] = scr[core]
    other[...] = scr[1 - core]


def plane_sum(parts):
    span, rows = parts[0].shape
    half = 2 * span
    return call(
        plane_sum_body,
        "plane_sum",
        [shape((rows // 2, half), F32)] * 2,
        [pltpu.VMEM((2, rows // 2, half), F32)],
    )(*parts)


def fold_body(odd0, odd1, even0, even1, out):
    core, pair = lax.axis_index("core"), pair_of()
    span = odd0.shape[2]
    for which, blocks in enumerate(((odd0, odd1), (even0, even1))):

        @pl.when(core == which)
        def _():
            for slot, x in enumerate(blocks):
                here = columns((pair ^ slot) * span, span)
                out[:, :, here] = x[...]


def fold(odd, even):
    _, frames, span = odd[0].shape
    return call(fold_body, "fold", shape((3, frames, 2 * span), F32))(*odd, *even)


def rows_final_body(odd0, odd1, even0, even1, back, sib, back_sib, dq, dk, dv):
    core, pair = lax.axis_index("core"), pair_of()
    span = odd0.shape[2]
    other = columns((1 - core) * 2 * span, 2 * span)
    dq[:, other] = sib[0].astype(BF16)
    for n, out in enumerate((dk, dv)):
        further = jnp.where(core == 1, back_sib[n].astype(F32), 0.0)
        out[:, other] = (sib[1 + n] + further).astype(BF16)
    for which, blocks in enumerate(((even0, even1), (odd0, odd1))):

        @pl.when(core == which)
        def _():
            for slot, x in enumerate(blocks):
                inside = columns((pair ^ slot) * span, span)
                mine = columns((2 * which + (pair ^ slot)) * span, span)
                dq[:, mine] = x[0].astype(BF16)
                for n, out in enumerate((dk, dv)):
                    total = x[1 + n]
                    if which == 1:
                        total = total + back[n, :, inside].astype(F32)
                    out[:, mine] = total.astype(BF16)


def rows_final(odd, even, back, sib, back_sib):
    frames, half = back.shape[1:]
    outs = [shape((frames, 2 * half), BF16)] * 3
    return call(rows_final_body, "rows_final", outs)(*odd, *even, back, sib, back_sib)


def band_final_body(mine, other, out):
    core = lax.axis_index("core")
    half = mine.shape[1]
    out[:, columns(core * half, half)] = mine[...]
    out[:, columns((1 - core) * half, half)] = other[...]


def band_final(mine, other):
    rows, half = mine.shape
    return call(band_final_body, "band_final", shape((rows, 2 * half), F32))(mine, other)


def local(query_rows, key_rows, value_rows, grad_out, pos_keys, bias_content, bias_position):
    n_high, n_z = lax.axis_size("dh"), lax.axis_size("z")
    width = query_rows.shape[2]

    def along_z(x, flip):
        return lax.ppermute(x, "z", [(s, s ^ flip) for s in range(n_z)])

    def around_z(x, steps):
        return lax.ppermute(x, "z", [(s, (s + steps) % n_z) for s in range(n_z)])

    def to_sibling(x):
        return lax.ppermute(x, "core", [(0, 1), (1, 0)])

    def in_plane(x, flip, cross=0):
        pairs = [
            (2 * d + c, 2 * (d ^ flip) + (c ^ cross)) for d in range(PLANE) for c in range(2)
        ]
        return lax.ppermute(x, ("dl", "core"), pairs)

    cut = band_cut(pos_keys)
    cuts = [cut] + [along_z(cut, k) for k in range(1, n_z)]
    own = [x[0] for x in (query_rows, key_rows, value_rows, grad_out)]
    sib = [to_sibling(x) for x in own]
    mine = own_half(*own[1:3])
    *cuts, mine = lax.optimization_barrier((*cuts, mine))
    band_own, band_sib = band_pack(cuts)
    prev = around_z(odd_rows(mine, *sib[1:3]), 1)
    first_bands = [band_own, to_sibling(band_sib)]
    second_bands = [in_plane(band_own, 1), in_plane(band_sib, 2, 1)]
    biases = [bias_content.reshape(1, width), bias_position.reshape(1, width)]

    inputs = (own, sib, biases)
    first = odd_call(0, *inputs, first_bands, n_z)
    second = odd_call(1, *inputs, second_bands, n_z)
    first, second = lax.optimization_barrier((first, second))
    even0, back, g_x, g_y = even_call(0, *inputs, prev, first, prev)
    received = [in_plane(g_x, 1), in_plane(g_y, 2)]
    even1, back, *g_own = even_call(1, *inputs, prev, second, back)


    parts = pair_sum(g_own, received, n_z)
    parts = [along_z(parts[k], k) for k in range(n_z - 1, 0, -1)] + [parts[0]]
    *parts, back, odd0, even0 = lax.optimization_barrier((*parts, back, first[0], even0))
    odd, even = (odd0, second[0]), (even0, even1)
    back = around_z(back, -1)
    out_sib = to_sibling(fold(odd, even))
    total = z_sum(parts)
    step = 1
    while step < n_high:
        pairs = [(s, s ^ step) for s in range(n_high)]
        total = z_sum([total, lax.ppermute(total, "dh", pairs)])
        step *= 2
    planes = [in_plane(total, k) for k in (3, 1, 2)]
    *planes, back = lax.optimization_barrier((*planes, back))
    back_sib = to_sibling(back)
    mine, other = plane_sum([total, *planes])
    other = to_sibling(other)
    rows = rows_final(odd, even, back, out_sib, back_sib)
    *rows, mine, other = lax.optimization_barrier((*rows, mine, other))
    return *[x[None] for x in rows], band_final(mine, other)


def solution(mesh):
    n_dp, n_blk = mesh.shape["dp"], mesh.shape["blk"]
    fine = Mesh(mesh.devices.reshape(n_dp // PLANE, PLANE, n_blk // 2, 2), ("dh", "dl", "z", "core"))
    rows = P(("dh", "dl"), ("z", "core"), None)
    band = P(("z", "core"), None)
    return jax.shard_map(
        local,
        mesh=fine,
        in_specs=(rows, rows, rows, rows, band, P(), P()),
        out_specs=(rows, rows, rows, band),
        check_vma=False,
    )
```

```python
import functools

import jax
import jax.numpy as jnp
from jax import lax
from jax.experimental import pallas as pl
from jax.experimental.pallas import tpu as pltpu
from jax.sharding import Mesh
from jax.sharding import PartitionSpec as P

DH = 64
W = 128
PLANE = 4
MIB = 2**20
F32 = jnp.float32
BF16 = jnp.bfloat16


def mm(a, b):
    return jnp.dot(a, b, preferred_element_type=F32)


def mm_nt(a, b):
    return lax.dot_general(a, b, (((1,), (1,)), ((), ())), preferred_element_type=F32)


def iota(shape, axis):
    return lax.broadcasted_iota(jnp.int32, shape, axis)


def as_bf16(hit):
    return hit.astype(F32).astype(BF16)


def shear(x, frames):
    rows = [
        pltpu.roll(x[r : r + frames], frames + 1, 1, stride=1, stride_axis=0)
        for r in range(0, x.shape[0], frames)
    ]
    return jnp.concatenate(rows, axis=0)


def columns(start, size):
    return pl.ds(pl.multiple_of(start, W), size)


class Masks:
    def __init__(self, frames):
        span = 2 * frames
        lane = iota((frames, W), 1)
        sub = iota((W, frames), 0)
        self.first = lane < DH
        scale = jnp.bfloat16(DH**-0.5)
        self.lanes = [as_bf16(lane < DH) * scale, as_bf16(lane >= DH) * scale]
        self.subs = [as_bf16(sub < DH), as_bf16(sub >= DH)]
        self.flip = as_bf16(iota((span, span), 0) + iota((span, span), 1) == span - 1)
        row = iota((span, span), 0) & (frames - 1)
        col = iota((span, span), 1)
        self.forward = (col + row >= frames - 1) & (col + row <= span - 2)
        back = (col - row >= 1) & (col - row <= frames)
        self.back = [as_bf16(back), as_bf16(~back)]

    def stack(self, x):
        return jnp.concatenate([x * self.lanes[0], x * self.lanes[1]], axis=0)

    def stack_t(self, x):
        x = x.T
        return jnp.concatenate([x * self.subs[0], x * self.subs[1]], axis=1)


def unit(masks, q, k, v, g, k_before, v_before, tables, bias_c, bias_p):
    frames = q.shape[0]
    band0, band1, band0_rev, band1_rev = tables
    kw = jnp.concatenate([k, k_before], axis=0)
    vw = jnp.concatenate([v, v_before], axis=0)
    qf = q.astype(F32)
    qc = (qf + bias_c).astype(BF16)
    qp = (qf + bias_p).astype(BF16)
    qp_stack = masks.stack(qp)
    content = mm_nt(masks.stack(qc), kw)
    merged = jnp.where(masks.forward, mm_nt(qp_stack, band0_rev), mm_nt(qp_stack, band1_rev))
    scores = content + shear(merged, frames)
    e = jnp.exp(scores - jnp.max(scores, axis=1, keepdims=True))
    gw = mm_nt(masks.stack(g), vw)
    attention = e * (1.0 / jnp.sum(e, axis=1, keepdims=True))
    delta = jnp.sum(attention * gw, axis=1, keepdims=True)
    ds = (attention * (gw - delta)).astype(BF16)
    placed = shear(mm(ds, masks.flip), frames).astype(BF16)
    d0, d1 = placed * masks.back[0], placed * masks.back[1]
    lhs = jnp.concatenate([ds, d0, d1], axis=1)
    rhs = jnp.concatenate([kw, band0, band1], axis=0)
    full = mm(lhs, rhs)
    dq = jnp.where(masks.first, full[:frames], full[frames:]).astype(BF16).astype(F32)
    dk = mm(masks.stack_t(qc), ds)
    dv = mm(masks.stack_t(g), attention.astype(BF16))
    qp_t = masks.stack_t(qp)
    g1 = mm(qp_t, d1)
    g_band = jnp.concatenate([mm(qp_t, d0), g1[:, frames:], g1[:, :frames]], axis=1)
    return dq, dk, dv, g_band


def call(body, name, out_shape, scratch=(), limit=8, **options):
    return pl.pallas_call(
        body,
        out_shape=out_shape,
        scratch_shapes=list(scratch),
        compiler_params=pltpu.CompilerParams(vmem_limit_bytes=limit * MIB),
        name=name,
        **options,
    )


def shape(dims, dtype):
    return jax.ShapeDtypeStruct(tuple(dims), dtype)


def pair_of():
    low = lax.axis_index("dl")
    return (low & 1) ^ (low >> 1)


def place(own, sib, scr, slot):
    core = lax.axis_index("core")
    span = scr.shape[3]
    here = columns((2 * core + (pair_of() ^ slot)) * span, span)
    for n, (a, b) in enumerate(zip(own, sib)):
        scr[n, core] = a[:, here]
        scr[n, 1 - core] = b[:, here]
    return here


def odd_body(steps, slot, *refs):
    own, sib, (bias_c, bias_p), bands = refs[0:4], refs[4:8], refs[8:10], refs[10:12]
    dq_out, out, carry, g_out, tables, scr, band_scr = refs[12:]
    core = lax.axis_index("core")
    frames, span = scr.shape[2:]
    share = band_scr.shape[2]
    here = place(own, sib, scr, slot)
    bias_c, bias_p = bias_c[:, here], bias_p[:, here]
    band_scr[:, core] = bands[0][...].reshape(steps, share, span)
    band_scr[:, 1 - core] = bands[1][...].reshape(steps, share, span)
    band = band_scr[...].reshape(steps * 2 * share, span)
    masks = Masks(frames)
    band0, band1 = band[: 2 * frames], band[2 * frames :]
    band1 = jnp.concatenate([band1[frames:], band1[:frames]], axis=0)
    tables[0] = band0
    tables[1] = band1
    tables[2] = mm(masks.flip, band0).astype(BF16)
    tables[3] = mm(masks.flip, band1).astype(BF16)
    for j in range(span // W):
        at = slice(j * W, (j + 1) * W)
        dq, dk, dv, g_band = unit(
            masks,
            *[scr[n, 1, :, at] for n in range(4)],
            scr[1, 0, :, at],
            scr[2, 0, :, at],
            [tables[n, :, at] for n in range(4)],
            bias_c[:, at],
            bias_p[:, at],
        )
        dq_out[:, at] = dq
        for n, term in enumerate((dk, dv)):
            out[n, at] = term[:, :frames]
            carry[n, at] = term[:, frames:].astype(BF16)
        g_out[j] = g_band


def even_body(slot, *refs):
    own, sib, (bias_c, bias_p) = refs[0:4], refs[4:8], refs[8:10]
    prev, tables, carry, g_odd = refs[10:14]
    dq_out, out, back = refs[14:17]
    g_outs, scr = refs[17:-1], refs[-1]
    frames, span = scr.shape[2:]
    here = place(own, sib, scr, slot)
    bias_c, bias_p = bias_c[:, here], bias_p[:, here]
    masks = Masks(frames)
    for j in range(span // W):
        at = slice(j * W, (j + 1) * W)
        mine = columns((pair_of() ^ slot) * span + j * W, W)
        dq, dk, dv, g_band = unit(
            masks,
            *[scr[n, 0, :, at] for n in range(4)],
            prev[0, :, mine],
            prev[1, :, mine],
            [tables[n, :, at] for n in range(4)],
            bias_c[:, at],
            bias_p[:, at],
        )
        dq_out[:, at] = dq
        for n, term in enumerate((dk, dv)):
            out[n, at] = term[:, :frames] + carry[n, at].astype(F32)
            back[n, at] = term[:, frames:].astype(BF16)
        g_outs[j][...] = (g_odd[j] + g_band).astype(g_outs[j].dtype)


def cost(groups, frames):
    return pl.CostEstimate(
        flops=2 * groups * 20 * frames * (2 * frames) ** 2,
        bytes_accessed=64 * groups * frames * W,
        transcendentals=groups * 4 * frames * frames,
    )


def odd_call(slot, own, sib, biases, bands, steps):
    frames = own[0].shape[0]
    rows, span = bands[0].shape
    groups = span // W
    return call(
        functools.partial(odd_body, steps, slot),
        "odd_block",
        [
            shape((frames, span), F32),
            shape((2, span, frames), F32),
            shape((2, span, frames), BF16),
            shape((groups, W, 2 * rows), F32),
            shape((4, rows, span), BF16),
        ],
        [
            pltpu.VMEM((4, 2, frames, span), BF16),
            pltpu.VMEM((steps, 2, rows // steps, span), BF16),
        ],
        limit=16,
        cost_estimate=cost(groups, frames),
    )(*own, *sib, *biases, *bands)


def even_call(slot, own, sib, biases, prev, odd):
    frames = own[0].shape[0]
    _, _, carry, g_odd, tables = odd
    groups, _, rows = g_odd.shape
    span = groups * W
    return call(
        functools.partial(even_body, slot),
        "even_block",
        [shape((frames, span), F32), shape((2, span, frames), F32), shape((2, span, frames), BF16)]
        + [shape((W, rows), F32 if slot else BF16)] * groups,
        [pltpu.VMEM((4, 2, frames, span), BF16)],
        limit=16,
        cost_estimate=cost(groups, frames),
    )(*own, *sib, *biases, prev, tables, carry, g_odd)


def band_cut_body(table, out):
    half = table.shape[1] // 2
    span = half // 2
    pair = pair_of()
    for n in range(2):
        out[:, n * span : (n + 1) * span] = table[:, columns(n * half + pair * span, span)]


def band_cut(table):
    rows, width = table.shape
    return call(band_cut_body, "band_cut", shape((rows, width // 2), BF16))(table)


def band_pack_body(steps, *refs):
    own, sib = refs[steps:]
    core, z = lax.axis_index("core"), lax.axis_index("z")
    span = own.shape[2]
    for n in range(steps):
        at = z ^ n
        own[at] = refs[n][:, columns(core * span, span)]
        sib[at] = refs[n][:, columns((1 - core) * span, span)]


def band_pack(parts):
    rows, width = parts[0].shape
    steps = len(parts)
    out = call(
        functools.partial(band_pack_body, steps),
        "band_pack",
        [shape((steps, rows, width // 2), BF16)] * 2,
    )(*parts)
    return [x.reshape(steps * rows, width // 2) for x in out]


def odd_rows_body(k, v, k_sib, v_sib, out):
    half = out.shape[2]
    core = lax.axis_index("core")
    for which, pair in enumerate(((k_sib, v_sib), (k, v))):

        @pl.when(core == which)
        def _():
            for n, x in enumerate(pair):
                out[n] = x[:, which * half : (which + 1) * half]


def odd_rows(*arrays):
    frames, width = arrays[0].shape
    return call(odd_rows_body, "odd_rows", shape((2, frames, width // 2), BF16))(*arrays)


def summed(refs):
    total = refs[0][...].astype(F32)
    for ref in refs[1:]:
        total = total + ref[...].astype(F32)
    return total


def pair_sum_body(steps, own0, own1, from_x, from_y, *refs):
    scr = refs[-1]
    z = lax.axis_index("z")
    rows = scr.shape[2]
    for n, (a, b) in enumerate(((own0, from_x), (own1, from_y))):
        total = (a[...] + b[...].astype(F32)).astype(BF16)
        for m in range(steps):
            scr[m, n * W : (n + 1) * W] = total[:, m * rows : (m + 1) * rows]
    for m in range(steps):
        refs[m][...] = scr[z ^ m]


def pair_sum(own, received, steps):
    rows = own[0].shape[1] // steps
    return call(
        functools.partial(pair_sum_body, steps),
        "pair_sum",
        [shape((2 * W, rows), BF16)] * steps,
        [pltpu.VMEM((steps, 2 * W, rows), BF16)],
    )(*own, *received)


def z_sum_body(*refs):
    refs[-1][...] = summed(refs[:-1]).astype(BF16)


def z_sum(parts):
    return call(z_sum_body, "z_sum", shape(parts[0].shape, BF16))(*parts)


def plane_sum_body(own, diagonal, from_x, from_y, mine, other, scr):
    core, pair = lax.axis_index("core"), pair_of()
    rows, half = mine.shape
    span = half // 2
    for n, terms in enumerate(((from_x, from_y), (own, diagonal))):
        total = summed(terms).T.reshape(2, rows, span)
        scr[:, :, columns((pair ^ n) * span, span)] = total
    mine[...] = scr[core]
    other[...] = scr[1 - core]


def plane_sum(parts):
    span, rows = parts[0].shape
    half = 2 * span
    return call(
        plane_sum_body,
        "plane_sum",
        [shape((rows // 2, half), F32)] * 2,
        [pltpu.VMEM((2, rows // 2, half), F32)],
    )(*parts)


def settle_body(*refs):
    odd, even, given = refs[0:4], refs[4:8], refs[8:10]
    own, sib, back = refs[10:]
    core, pair = lax.axis_index("core"), pair_of()
    span = odd[0].shape[1]
    for slot in range(2):
        here = columns((pair ^ slot) * span, span)
        for n in range(2):
            back[n, :, here] = given[slot][n].T
        for which, (first, second) in enumerate(((own, sib), (sib, own))):

            @pl.when(core == which)
            def _():
                for target, block in ((first, even), (second, odd)):
                    target[0, :, here] = block[2 * slot][...]
                    for n in range(2):
                        target[1 + n, :, here] = block[2 * slot + 1][n].T


def settle(odd, even, back):
    frames, span = odd[0].shape
    outs = [shape((3, frames, 2 * span), F32)] * 2 + [shape((2, frames, 2 * span), BF16)]
    return call(settle_body, "settle", outs)(*odd, *even, *back)


def rows_final_body(own, sib, back, back_sib, dq, dk, dv):
    core = lax.axis_index("core")
    half = own.shape[2]
    mine, other = columns(core * half, half), columns((1 - core) * half, half)
    dq[:, mine] = own[0].astype(BF16)
    dq[:, other] = sib[0].astype(BF16)
    odd = core == 1
    for n, out in enumerate((dk, dv)):
        out[:, mine] = (own[1 + n] + jnp.where(odd, back[n].astype(F32), 0.0)).astype(BF16)
        out[:, other] = (sib[1 + n] + jnp.where(odd, back_sib[n].astype(F32), 0.0)).astype(BF16)


def rows_final(own, sib, back, back_sib):
    frames, half = back.shape[1:]
    outs = [shape((frames, 2 * half), BF16)] * 3
    return call(rows_final_body, "rows_final", outs)(own, sib, back, back_sib)


def band_final_body(mine, other, out):
    core = lax.axis_index("core")
    half = mine.shape[1]
    out[:, columns(core * half, half)] = mine[...]
    out[:, columns((1 - core) * half, half)] = other[...]


def band_final(mine, other):
    rows, half = mine.shape
    return call(band_final_body, "band_final", shape((rows, 2 * half), F32))(mine, other)


def local(query_rows, key_rows, value_rows, grad_out, pos_keys, bias_content, bias_position):
    n_high, n_z = lax.axis_size("dh"), lax.axis_size("z")
    width = query_rows.shape[2]

    def along_z(x, flip):
        return lax.ppermute(x, "z", [(s, s ^ flip) for s in range(n_z)])

    def around_z(x, steps):
        return lax.ppermute(x, "z", [(s, (s + steps) % n_z) for s in range(n_z)])

    def to_sibling(x):
        return lax.ppermute(x, "core", [(0, 1), (1, 0)])

    def in_plane(x, flip, cross=0):
        pairs = [
            (2 * d + c, 2 * (d ^ flip) + (c ^ cross)) for d in range(PLANE) for c in range(2)
        ]
        return lax.ppermute(x, ("dl", "core"), pairs)

    cut = band_cut(pos_keys)
    cuts = [cut] + [along_z(cut, k) for k in range(1, n_z)]
    own = [x[0] for x in (query_rows, key_rows, value_rows, grad_out)]
    sib = [to_sibling(x) for x in own]
    prev = around_z(odd_rows(*own[1:3], *sib[1:3]), 1)
    band_own, band_sib = band_pack(cuts)
    first_bands = [band_own, to_sibling(band_sib)]
    second_bands = [in_plane(band_own, 1), in_plane(band_sib, 2, 1)]
    biases = [bias_content.reshape(1, width), bias_position.reshape(1, width)]

    inputs = (own, sib, biases)
    first = odd_call(0, *inputs, first_bands, n_z)
    second = odd_call(1, *inputs, second_bands, n_z)
    first, second = lax.optimization_barrier((first, second))
    even0 = even_call(0, *inputs, prev, first)
    received = [in_plane(even0[3], 1), in_plane(even0[4], 2)]
    even1 = even_call(1, *inputs, prev, second)
    g_own = even1[3:]

    *parts, turn = lax.optimization_barrier((*pair_sum(g_own, received, n_z), even0[2]))
    parts = [along_z(parts[k], k) for k in range(n_z - 1, 0, -1)] + [parts[0]]
    odd, even = (*first[:2], *second[:2]), (*even0[:2], *even1[:2])
    out_own, out_sib, back = settle(odd, even, (turn, even1[2]))
    *parts, back, out_sib = lax.optimization_barrier((*parts, back, out_sib))
    back = around_z(back, -1)
    out_sib = to_sibling(out_sib)
    total = z_sum(parts)
    step = 1
    while step < n_high:
        pairs = [(s, s ^ step) for s in range(n_high)]
        total = z_sum([total, lax.ppermute(total, "dh", pairs)])
        step *= 2
    planes = [in_plane(total, k) for k in (3, 1, 2)]
    *planes, back = lax.optimization_barrier((*planes, back))
    back_sib = to_sibling(back)
    mine, other = plane_sum([total, *planes])
    other = to_sibling(other)
    rows = rows_final(out_own, out_sib, back, back_sib)
    *rows, mine, other = lax.optimization_barrier((*rows, mine, other))
    return *[x[None] for x in rows], band_final(mine, other)


def solution(mesh):
    n_dp, n_blk = mesh.shape["dp"], mesh.shape["blk"]
    fine = Mesh(mesh.devices.reshape(n_dp // PLANE, PLANE, n_blk // 2, 2), ("dh", "dl", "z", "core"))
    rows = P(("dh", "dl"), ("z", "core"), None)
    band = P(("z", "core"), None)
    return jax.shard_map(
        local,
        mesh=fine,
        in_specs=(rows, rows, rows, rows, band, P(), P()),
        out_specs=(rows, rows, rows, band),
        check_vma=False,
    )
```

```python
import functools

import jax
import jax.numpy as jnp
from jax import lax
from jax.experimental import pallas as pl
from jax.experimental.pallas import tpu as pltpu
from jax.sharding import Mesh
from jax.sharding import PartitionSpec as P

DH = 64
W = 128
PLANE = 4
MIB = 2**20
F32 = jnp.float32
BF16 = jnp.bfloat16


def mm(a, b):
    return jnp.dot(a, b, preferred_element_type=F32)


def mm_nt(a, b):
    return lax.dot_general(a, b, (((1,), (1,)), ((), ())), preferred_element_type=F32)


def iota(shape, axis):
    return lax.broadcasted_iota(jnp.int32, shape, axis)


def as_bf16(hit):
    return hit.astype(F32).astype(BF16)


CHUNK = 32


def shear(x, frames, row):
    return pltpu.roll(x, frames + 1 + row, 1, stride=1, stride_axis=0)


def columns(start, size):
    return pl.ds(pl.multiple_of(start, W), size)


class Masks:
    def __init__(self, frames):
        span = 2 * frames
        lane = iota((frames, W), 1)
        sub = iota((W, frames), 0)
        self.first = lane < DH
        scale = jnp.bfloat16(DH**-0.5)
        self.lanes = [as_bf16(lane < DH) * scale, as_bf16(lane >= DH) * scale]
        self.subs = [as_bf16(sub < DH), as_bf16(sub >= DH)]
        self.flip = as_bf16(iota((span, span), 0) + iota((span, span), 1) == span - 1)
        row, col = iota((frames, frames), 0), iota((frames, frames), 1)
        self.forward = col + row >= frames - 1
        self.back = [as_bf16(col > row), as_bf16(col <= row)]

    def stack(self, x):
        return jnp.concatenate([x * self.lanes[0], x * self.lanes[1]], axis=0)

    def stack_t(self, x):
        x = x.T
        return jnp.concatenate([x * self.subs[0], x * self.subs[1]], axis=1)


def unit(masks, q, k, v, g, k_before, v_before, tables, bias_c, bias_p):
    frames = q.shape[0]
    band0, band1, band0_rev, band1_rev = tables
    kw = jnp.concatenate([k, k_before], axis=0)
    vw = jnp.concatenate([v, v_before], axis=0)
    qf = q.astype(F32)
    qc = (qf + bias_c).astype(BF16)
    qp = (qf + bias_p).astype(BF16)
    qp_stack = masks.stack(qp)
    content = mm_nt(masks.stack(qc), kw)
    near, far = mm_nt(qp_stack, band0_rev), mm_nt(qp_stack, band1_rev)
    gw = mm_nt(masks.stack(g), vw)
    ds, attention_b = [], []
    for start in range(0, 2 * frames, CHUNK):
        rows, first = slice(start, start + CHUNK), start % frames
        own = masks.forward[first : first + CHUNK]
        merged = [
            jnp.where(own, near[rows, :frames], far[rows, :frames]),
            jnp.where(own, far[rows, frames:], near[rows, frames:]),
        ]
        scores = content[rows] + shear(jnp.concatenate(merged, axis=1), frames, first)
        e = jnp.exp(scores - jnp.max(scores, axis=1, keepdims=True))
        inverse = 1.0 / jnp.sum(e, axis=1, keepdims=True)
        delta = jnp.sum(e * gw[rows], axis=1, keepdims=True) * inverse
        attention = e * inverse
        attention_b.append(attention.astype(BF16))
        ds.append((attention * (gw[rows] - delta)).astype(BF16))
    ds, attention_b = jnp.concatenate(ds, axis=0), jnp.concatenate(attention_b, axis=0)
    flipped = mm(ds, masks.flip)
    d0, d1 = [], []
    for start in range(0, 2 * frames, CHUNK):
        first = start % frames
        placed = shear(flipped[start : start + CHUNK], frames, first).astype(BF16)
        left, right = placed[:, :frames], placed[:, frames:]
        mask = [m[first : first + CHUNK] for m in masks.back]
        d0.append(jnp.concatenate([left * mask[0], right * mask[1]], axis=1))
        d1.append(jnp.concatenate([left * mask[1], right * mask[0]], axis=1))
    d0, d1 = jnp.concatenate(d0, axis=0), jnp.concatenate(d1, axis=0)
    lhs = jnp.concatenate([ds, d0, d1], axis=1)
    rhs = jnp.concatenate([kw, band0, band1], axis=0)
    full = mm(lhs, rhs)
    dq = jnp.where(masks.first, full[:frames], full[frames:]).astype(BF16).astype(F32)
    dk = mm(masks.stack_t(qc), ds)
    dv = mm(masks.stack_t(g), attention_b)
    qp_t = masks.stack_t(qp)
    g1 = mm(qp_t, d1)
    g_band = jnp.concatenate([mm(qp_t, d0), g1[:, frames:], g1[:, :frames]], axis=1)
    return dq, dk, dv, g_band


def call(body, name, out_shape, scratch=(), limit=8, **options):
    return pl.pallas_call(
        body,
        out_shape=out_shape,
        scratch_shapes=list(scratch),
        compiler_params=pltpu.CompilerParams(vmem_limit_bytes=limit * MIB),
        name=name,
        **options,
    )


def shape(dims, dtype):
    return jax.ShapeDtypeStruct(tuple(dims), dtype)


def pair_of():
    low = lax.axis_index("dl")
    return (low & 1) ^ (low >> 1)


def place(own, sib, scr, slot):
    core = lax.axis_index("core")
    span = scr.shape[3]
    here = columns((2 * core + (pair_of() ^ slot)) * span, span)
    for n, (a, b) in enumerate(zip(own, sib)):
        scr[n, core] = a[:, here]
        scr[n, 1 - core] = b[:, here]
    return here


def odd_body(steps, slot, *refs):
    own, sib, (bias_c, bias_p), bands = refs[0:4], refs[4:8], refs[8:10], refs[10:12]
    dq_out, out, carry, g_out, tables, scr, band_scr = refs[12:]
    core = lax.axis_index("core")
    frames, span = scr.shape[2:]
    share = band_scr.shape[2]
    here = place(own, sib, scr, slot)
    bias_c, bias_p = bias_c[:, here], bias_p[:, here]
    band_scr[:, core] = bands[0][...].reshape(steps, share, span)
    band_scr[:, 1 - core] = bands[1][...].reshape(steps, share, span)
    band = band_scr[...].reshape(steps * 2 * share, span)
    masks = Masks(frames)
    band0, band1 = band[: 2 * frames], band[2 * frames :]
    band1 = jnp.concatenate([band1[frames:], band1[:frames]], axis=0)
    tables[0] = band0
    tables[1] = band1
    tables[2] = mm(masks.flip, band0).astype(BF16)
    tables[3] = mm(masks.flip, band1).astype(BF16)
    for j in range(span // W):
        at = slice(j * W, (j + 1) * W)
        dq, dk, dv, g_band = unit(
            masks,
            *[scr[n, 1, :, at] for n in range(4)],
            scr[1, 0, :, at],
            scr[2, 0, :, at],
            [tables[n, :, at] for n in range(4)],
            bias_c[:, at],
            bias_p[:, at],
        )
        dq_out[:, at] = dq
        for n, term in enumerate((dk, dv)):
            out[n, at] = term[:, :frames]
            carry[n, at] = term[:, frames:].astype(BF16)
        g_out[j] = g_band


def even_body(slot, *refs):
    own, sib, (bias_c, bias_p) = refs[0:4], refs[4:8], refs[8:10]
    prev, tables, carry, g_odd = refs[10:14]
    dq_out, out, back = refs[14:17]
    g_outs, scr = refs[17:-1], refs[-1]
    frames, span = scr.shape[2:]
    here = place(own, sib, scr, slot)
    bias_c, bias_p = bias_c[:, here], bias_p[:, here]
    masks = Masks(frames)
    for j in range(span // W):
        at = slice(j * W, (j + 1) * W)
        mine = columns((pair_of() ^ slot) * span + j * W, W)
        dq, dk, dv, g_band = unit(
            masks,
            *[scr[n, 0, :, at] for n in range(4)],
            prev[0, :, mine],
            prev[1, :, mine],
            [tables[n, :, at] for n in range(4)],
            bias_c[:, at],
            bias_p[:, at],
        )
        dq_out[:, at] = dq
        for n, term in enumerate((dk, dv)):
            out[n, at] = term[:, :frames] + carry[n, at].astype(F32)
            back[n, at] = term[:, frames:].astype(BF16)
        g_outs[j][...] = (g_odd[j] + g_band).astype(g_outs[j].dtype)


def cost(groups, frames):
    return pl.CostEstimate(
        flops=2 * groups * 20 * frames * (2 * frames) ** 2,
        bytes_accessed=64 * groups * frames * W,
        transcendentals=groups * 4 * frames * frames,
    )


def odd_call(slot, own, sib, biases, bands, steps):
    frames = own[0].shape[0]
    rows, span = bands[0].shape
    groups = span // W
    return call(
        functools.partial(odd_body, steps, slot),
        "odd_block",
        [
            shape((frames, span), F32),
            shape((2, span, frames), F32),
            shape((2, span, frames), BF16),
            shape((groups, W, 2 * rows), F32),
            shape((4, rows, span), BF16),
        ],
        [
            pltpu.VMEM((4, 2, frames, span), BF16),
            pltpu.VMEM((steps, 2, rows // steps, span), BF16),
        ],
        limit=16,
        cost_estimate=cost(groups, frames),
    )(*own, *sib, *biases, *bands)


def even_call(slot, own, sib, biases, prev, odd):
    frames = own[0].shape[0]
    _, _, carry, g_odd, tables = odd
    groups, _, rows = g_odd.shape
    span = groups * W
    return call(
        functools.partial(even_body, slot),
        "even_block",
        [shape((frames, span), F32), shape((2, span, frames), F32), shape((2, span, frames), BF16)]
        + [shape((W, rows), F32 if slot else BF16)] * groups,
        [pltpu.VMEM((4, 2, frames, span), BF16)],
        limit=16,
        cost_estimate=cost(groups, frames),
    )(*own, *sib, *biases, prev, tables, carry, g_odd)


def band_cut_body(table, out):
    half = table.shape[1] // 2
    span = half // 2
    pair = pair_of()
    for n in range(2):
        out[:, n * span : (n + 1) * span] = table[:, columns(n * half + pair * span, span)]


def band_cut(table):
    rows, width = table.shape
    return call(band_cut_body, "band_cut", shape((rows, width // 2), BF16))(table)


def band_pack_body(steps, *refs):
    own, sib = refs[steps:]
    core, z = lax.axis_index("core"), lax.axis_index("z")
    span = own.shape[2]
    for n in range(steps):
        at = z ^ n
        own[at] = refs[n][:, columns(core * span, span)]
        sib[at] = refs[n][:, columns((1 - core) * span, span)]


def band_pack(parts):
    rows, width = parts[0].shape
    steps = len(parts)
    out = call(
        functools.partial(band_pack_body, steps),
        "band_pack",
        [shape((steps, rows, width // 2), BF16)] * 2,
    )(*parts)
    return [x.reshape(steps * rows, width // 2) for x in out]


def odd_rows_body(k, v, k_sib, v_sib, out):
    half = out.shape[2]
    core = lax.axis_index("core")
    for which, pair in enumerate(((k_sib, v_sib), (k, v))):

        @pl.when(core == which)
        def _():
            for n, x in enumerate(pair):
                out[n] = x[:, which * half : (which + 1) * half]


def odd_rows(*arrays):
    frames, width = arrays[0].shape
    return call(odd_rows_body, "odd_rows", shape((2, frames, width // 2), BF16))(*arrays)


def summed(refs):
    total = refs[0][...].astype(F32)
    for ref in refs[1:]:
        total = total + ref[...].astype(F32)
    return total


def pair_sum_body(steps, own0, own1, from_x, from_y, *refs):
    scr = refs[-1]
    z = lax.axis_index("z")
    rows = scr.shape[2]
    for n, (a, b) in enumerate(((own0, from_x), (own1, from_y))):
        total = (a[...] + b[...].astype(F32)).astype(BF16)
        for m in range(steps):
            scr[m, n * W : (n + 1) * W] = total[:, m * rows : (m + 1) * rows]
    for m in range(steps):
        refs[m][...] = scr[z ^ m]


def pair_sum(own, received, steps):
    rows = own[0].shape[1] // steps
    return call(
        functools.partial(pair_sum_body, steps),
        "pair_sum",
        [shape((2 * W, rows), BF16)] * steps,
        [pltpu.VMEM((steps, 2 * W, rows), BF16)],
    )(*own, *received)


def z_sum_body(*refs):
    refs[-1][...] = summed(refs[:-1]).astype(BF16)


def z_sum(parts):
    return call(z_sum_body, "z_sum", shape(parts[0].shape, BF16))(*parts)


def plane_sum_body(own, diagonal, from_x, from_y, mine, other, scr):
    core, pair = lax.axis_index("core"), pair_of()
    rows, half = mine.shape
    span = half // 2
    for n, terms in enumerate(((from_x, from_y), (own, diagonal))):
        total = summed(terms).T.reshape(2, rows, span)
        scr[:, :, columns((pair ^ n) * span, span)] = total
    mine[...] = scr[core]
    other[...] = scr[1 - core]


def plane_sum(parts):
    span, rows = parts[0].shape
    half = 2 * span
    return call(
        plane_sum_body,
        "plane_sum",
        [shape((rows // 2, half), F32)] * 2,
        [pltpu.VMEM((2, rows // 2, half), F32)],
    )(*parts)


def settle_body(*refs):
    odd, even, given = refs[0:4], refs[4:8], refs[8:10]
    own, sib, back = refs[10:]
    core, pair = lax.axis_index("core"), pair_of()
    span = odd[0].shape[1]
    for slot in range(2):
        here = columns((pair ^ slot) * span, span)
        for n in range(2):
            back[n, :, here] = given[slot][n].T
        for which, (first, second) in enumerate(((own, sib), (sib, own))):

            @pl.when(core == which)
            def _():
                for target, block in ((first, even), (second, odd)):
                    target[0, :, here] = block[2 * slot][...]
                    for n in range(2):
                        target[1 + n, :, here] = block[2 * slot + 1][n].T


def settle(odd, even, back):
    frames, span = odd[0].shape
    outs = [shape((3, frames, 2 * span), F32)] * 2 + [shape((2, frames, 2 * span), BF16)]
    return call(settle_body, "settle", outs)(*odd, *even, *back)


def rows_final_body(own, sib, back, back_sib, dq, dk, dv):
    core = lax.axis_index("core")
    half = own.shape[2]
    mine, other = columns(core * half, half), columns((1 - core) * half, half)
    dq[:, mine] = own[0].astype(BF16)
    dq[:, other] = sib[0].astype(BF16)
    odd = core == 1
    for n, out in enumerate((dk, dv)):
        out[:, mine] = (own[1 + n] + jnp.where(odd, back[n].astype(F32), 0.0)).astype(BF16)
        out[:, other] = (sib[1 + n] + jnp.where(odd, back_sib[n].astype(F32), 0.0)).astype(BF16)


def rows_final(own, sib, back, back_sib):
    frames, half = back.shape[1:]
    outs = [shape((frames, 2 * half), BF16)] * 3
    return call(rows_final_body, "rows_final", outs)(own, sib, back, back_sib)


def band_final_body(mine, other, out):
    core = lax.axis_index("core")
    half = mine.shape[1]
    out[:, columns(core * half, half)] = mine[...]
    out[:, columns((1 - core) * half, half)] = other[...]


def band_final(mine, other):
    rows, half = mine.shape
    return call(band_final_body, "band_final", shape((rows, 2 * half), F32))(mine, other)


def local(query_rows, key_rows, value_rows, grad_out, pos_keys, bias_content, bias_position):
    n_high, n_z = lax.axis_size("dh"), lax.axis_size("z")
    width = query_rows.shape[2]

    def along_z(x, flip):
        return lax.ppermute(x, "z", [(s, s ^ flip) for s in range(n_z)])

    def around_z(x, steps):
        return lax.ppermute(x, "z", [(s, (s + steps) % n_z) for s in range(n_z)])

    def to_sibling(x):
        return lax.ppermute(x, "core", [(0, 1), (1, 0)])

    def in_plane(x, flip, cross=0):
        pairs = [
            (2 * d + c, 2 * (d ^ flip) + (c ^ cross)) for d in range(PLANE) for c in range(2)
        ]
        return lax.ppermute(x, ("dl", "core"), pairs)

    cut = band_cut(pos_keys)
    cuts = [cut] + [along_z(cut, k) for k in range(1, n_z)]
    own = [x[0] for x in (query_rows, key_rows, value_rows, grad_out)]
    sib = [to_sibling(x) for x in own]
    prev = around_z(odd_rows(*own[1:3], *sib[1:3]), 1)
    band_own, band_sib = band_pack(cuts)
    first_bands = [band_own, to_sibling(band_sib)]
    second_bands = [in_plane(band_own, 1), in_plane(band_sib, 2, 1)]
    biases = [bias_content.reshape(1, width), bias_position.reshape(1, width)]

    inputs = (own, sib, biases)
    first = odd_call(0, *inputs, first_bands, n_z)
    second = odd_call(1, *inputs, second_bands, n_z)
    first, second = lax.optimization_barrier((first, second))
    even0 = even_call(0, *inputs, prev, first)
    received = [in_plane(even0[3], 1), in_plane(even0[4], 2)]
    even1 = even_call(1, *inputs, prev, second)
    g_own = even1[3:]

    *parts, turn = lax.optimization_barrier((*pair_sum(g_own, received, n_z), even0[2]))
    parts = [along_z(parts[k], k) for k in range(n_z - 1, 0, -1)] + [parts[0]]
    odd, even = (*first[:2], *second[:2]), (*even0[:2], *even1[:2])
    out_own, out_sib, back = settle(odd, even, (turn, even1[2]))
    *parts, back, out_sib = lax.optimization_barrier((*parts, back, out_sib))
    back = around_z(back, -1)
    out_sib = to_sibling(out_sib)
    total = z_sum(parts)
    step = 1
    while step < n_high:
        pairs = [(s, s ^ step) for s in range(n_high)]
        total = z_sum([total, lax.ppermute(total, "dh", pairs)])
        step *= 2
    planes = [in_plane(total, k) for k in (3, 1, 2)]
    *planes, back = lax.optimization_barrier((*planes, back))
    back_sib = to_sibling(back)
    mine, other = plane_sum([total, *planes])
    other = to_sibling(other)
    rows = rows_final(out_own, out_sib, back, back_sib)
    *rows, mine, other = lax.optimization_barrier((*rows, mine, other))
    return *[x[None] for x in rows], band_final(mine, other)


def solution(mesh):
    n_dp, n_blk = mesh.shape["dp"], mesh.shape["blk"]
    fine = Mesh(mesh.devices.reshape(n_dp // PLANE, PLANE, n_blk // 2, 2), ("dh", "dl", "z", "core"))
    rows = P(("dh", "dl"), ("z", "core"), None)
    band = P(("z", "core"), None)
    return jax.shard_map(
        local,
        mesh=fine,
        in_specs=(rows, rows, rows, rows, band, P(), P()),
        out_specs=(rows, rows, rows, band),
        check_vma=False,
    )
```

```python
import functools

import jax
import jax.numpy as jnp
from jax import lax
from jax.experimental import pallas as pl
from jax.experimental.pallas import tpu as pltpu
from jax.sharding import Mesh
from jax.sharding import PartitionSpec as P

DH = 64
W = 128
PLANE = 4
MIB = 2**20
F32 = jnp.float32
BF16 = jnp.bfloat16


def mm(a, b):
    return jnp.dot(a, b, preferred_element_type=F32)


def mm_nt(a, b):
    return lax.dot_general(a, b, (((1,), (1,)), ((), ())), preferred_element_type=F32)


def iota(shape, axis):
    return lax.broadcasted_iota(jnp.int32, shape, axis)


def as_bf16(hit):
    return hit.astype(F32).astype(BF16)


CHUNK = 32


def shear(x, frames, row):
    return pltpu.roll(x, frames + 1 + row, 1, stride=1, stride_axis=0)


def columns(start, size):
    return pl.ds(pl.multiple_of(start, W), size)


class Masks:
    def __init__(self, frames):
        span = 2 * frames
        lane = iota((frames, W), 1)
        sub = iota((W, frames), 0)
        self.first = lane < DH
        scale = jnp.bfloat16(DH**-0.5)
        self.lanes = [as_bf16(lane < DH) * scale, as_bf16(lane >= DH) * scale]
        self.subs = [as_bf16(sub < DH), as_bf16(sub >= DH)]
        self.flip = as_bf16(iota((span, span), 0) + iota((span, span), 1) == span - 1)
        row, col = iota((frames, frames), 0), iota((frames, frames), 1)
        self.forward = col + row >= frames - 1
        self.back = [as_bf16(col > row), as_bf16(col <= row)]

    def stack(self, x):
        return jnp.concatenate([x * self.lanes[0], x * self.lanes[1]], axis=0)

    def stack_t(self, x):
        x = x.T
        return jnp.concatenate([x * self.subs[0], x * self.subs[1]], axis=1)


def unit(masks, q, k, v, g, k_before, v_before, tables, bias_c, bias_p):
    frames = q.shape[0]
    band0, band1, band0_rev, band1_rev = tables
    kw = jnp.concatenate([k, k_before], axis=0)
    vw = jnp.concatenate([v, v_before], axis=0)
    qf = q.astype(F32)
    qc = (qf + bias_c).astype(BF16)
    qp = (qf + bias_p).astype(BF16)
    qp_stack = masks.stack(qp)
    content = mm_nt(masks.stack(qc), kw)
    near, far = mm_nt(qp_stack, band0_rev), mm_nt(qp_stack, band1_rev)
    gw = mm_nt(masks.stack(g), vw)
    yield
    ds, attention_b = [], []
    for start in range(0, 2 * frames, CHUNK):
        rows, first = slice(start, start + CHUNK), start % frames
        own = masks.forward[first : first + CHUNK]
        merged = [
            jnp.where(own, near[rows, :frames], far[rows, :frames]),
            jnp.where(own, far[rows, frames:], near[rows, frames:]),
        ]
        scores = content[rows] + shear(jnp.concatenate(merged, axis=1), frames, first)
        e = jnp.exp(scores - jnp.max(scores, axis=1, keepdims=True))
        inverse = 1.0 / jnp.sum(e, axis=1, keepdims=True)
        delta = jnp.sum(e * gw[rows], axis=1, keepdims=True) * inverse
        attention = e * inverse
        attention_b.append(attention.astype(BF16))
        ds.append((attention * (gw[rows] - delta)).astype(BF16))
        yield
    ds, attention_b = jnp.concatenate(ds, axis=0), jnp.concatenate(attention_b, axis=0)
    flipped = mm(ds, masks.flip)
    dk = mm(masks.stack_t(qc), ds)
    dv = mm(masks.stack_t(g), attention_b)
    yield
    d0, d1 = [], []
    for start in range(0, 2 * frames, CHUNK):
        first = start % frames
        placed = shear(flipped[start : start + CHUNK], frames, first).astype(BF16)
        left, right = placed[:, :frames], placed[:, frames:]
        mask = [m[first : first + CHUNK] for m in masks.back]
        d0.append(jnp.concatenate([left * mask[0], right * mask[1]], axis=1))
        d1.append(jnp.concatenate([left * mask[1], right * mask[0]], axis=1))
        yield
    d0, d1 = jnp.concatenate(d0, axis=0), jnp.concatenate(d1, axis=0)
    lhs = jnp.concatenate([ds, d0, d1], axis=1)
    rhs = jnp.concatenate([kw, band0, band1], axis=0)
    full = mm(lhs, rhs)
    dq = jnp.where(masks.first, full[:frames], full[frames:]).astype(BF16).astype(F32)
    qp_t = masks.stack_t(qp)
    g1 = mm(qp_t, d1)
    g_band = jnp.concatenate([mm(qp_t, d0), g1[:, frames:], g1[:, :frames]], axis=1)
    return dq, dk, dv, g_band


def side_by_side(groups):
    results = [None] * len(groups)
    left = list(enumerate(groups))
    while left:
        for n, group in list(left):
            try:
                next(group)
            except StopIteration as end:
                results[n] = end.value
                left.remove((n, group))
    return results


def call(body, name, out_shape, scratch=(), limit=8, **options):
    return pl.pallas_call(
        body,
        out_shape=out_shape,
        scratch_shapes=list(scratch),
        compiler_params=pltpu.CompilerParams(vmem_limit_bytes=limit * MIB),
        name=name,
        **options,
    )


def shape(dims, dtype):
    return jax.ShapeDtypeStruct(tuple(dims), dtype)


def pair_of():
    low = lax.axis_index("dl")
    return (low & 1) ^ (low >> 1)


def place(own, sib, scr, slot):
    core = lax.axis_index("core")
    span = scr.shape[3]
    here = columns((2 * core + (pair_of() ^ slot)) * span, span)
    for n, (a, b) in enumerate(zip(own, sib)):
        scr[n, core] = a[:, here]
        scr[n, 1 - core] = b[:, here]
    return here


def odd_body(steps, slot, *refs):
    own, sib, (bias_c, bias_p), bands = refs[0:4], refs[4:8], refs[8:10], refs[10:12]
    dq_out, out, carry, g_out, tables, scr, band_scr = refs[12:]
    core = lax.axis_index("core")
    frames, span = scr.shape[2:]
    share = band_scr.shape[2]
    here = place(own, sib, scr, slot)
    bias_c, bias_p = bias_c[:, here], bias_p[:, here]
    band_scr[:, core] = bands[0][...].reshape(steps, share, span)
    band_scr[:, 1 - core] = bands[1][...].reshape(steps, share, span)
    band = band_scr[...].reshape(steps * 2 * share, span)
    masks = Masks(frames)
    band0, band1 = band[: 2 * frames], band[2 * frames :]
    band1 = jnp.concatenate([band1[frames:], band1[:frames]], axis=0)
    tables[0] = band0
    tables[1] = band1
    tables[2] = mm(masks.flip, band0).astype(BF16)
    tables[3] = mm(masks.flip, band1).astype(BF16)
    cuts = [slice(j * W, (j + 1) * W) for j in range(span // W)]
    groups = [
        unit(
            masks,
            *[scr[n, 1, :, at] for n in range(4)],
            scr[1, 0, :, at],
            scr[2, 0, :, at],
            [tables[n, :, at] for n in range(4)],
            bias_c[:, at],
            bias_p[:, at],
        )
        for at in cuts
    ]
    for j, (dq, dk, dv, g_band) in enumerate(side_by_side(groups)):
        at = cuts[j]
        dq_out[:, at] = dq
        for n, term in enumerate((dk, dv)):
            out[n, at] = term[:, :frames]
            carry[n, at] = term[:, frames:].astype(BF16)
        g_out[j] = g_band


def even_body(slot, *refs):
    own, sib, (bias_c, bias_p) = refs[0:4], refs[4:8], refs[8:10]
    prev, tables, carry, g_odd = refs[10:14]
    dq_out, out, back = refs[14:17]
    g_outs, scr = refs[17:-1], refs[-1]
    frames, span = scr.shape[2:]
    here = place(own, sib, scr, slot)
    bias_c, bias_p = bias_c[:, here], bias_p[:, here]
    masks = Masks(frames)
    cuts = [slice(j * W, (j + 1) * W) for j in range(span // W)]
    groups = []
    for j, at in enumerate(cuts):
        mine = columns((pair_of() ^ slot) * span + j * W, W)
        groups.append(
            unit(
                masks,
                *[scr[n, 0, :, at] for n in range(4)],
                prev[0, :, mine],
                prev[1, :, mine],
                [tables[n, :, at] for n in range(4)],
                bias_c[:, at],
                bias_p[:, at],
            )
        )
    for j, (dq, dk, dv, g_band) in enumerate(side_by_side(groups)):
        at = cuts[j]
        dq_out[:, at] = dq
        for n, term in enumerate((dk, dv)):
            out[n, at] = term[:, :frames] + carry[n, at].astype(F32)
            back[n, at] = term[:, frames:].astype(BF16)
        g_outs[j][...] = (g_odd[j] + g_band).astype(g_outs[j].dtype)


def cost(groups, frames):
    return pl.CostEstimate(
        flops=2 * groups * 20 * frames * (2 * frames) ** 2,
        bytes_accessed=64 * groups * frames * W,
        transcendentals=groups * 4 * frames * frames,
    )


def odd_call(slot, own, sib, biases, bands, steps):
    frames = own[0].shape[0]
    rows, span = bands[0].shape
    groups = span // W
    return call(
        functools.partial(odd_body, steps, slot),
        "odd_block",
        [
            shape((frames, span), F32),
            shape((2, span, frames), F32),
            shape((2, span, frames), BF16),
            shape((groups, W, 2 * rows), F32),
            shape((4, rows, span), BF16),
        ],
        [
            pltpu.VMEM((4, 2, frames, span), BF16),
            pltpu.VMEM((steps, 2, rows // steps, span), BF16),
        ],
        limit=16,
        cost_estimate=cost(groups, frames),
    )(*own, *sib, *biases, *bands)


def even_call(slot, own, sib, biases, prev, odd):
    frames = own[0].shape[0]
    _, _, carry, g_odd, tables = odd
    groups, _, rows = g_odd.shape
    span = groups * W
    return call(
        functools.partial(even_body, slot),
        "even_block",
        [shape((frames, span), F32), shape((2, span, frames), F32), shape((2, span, frames), BF16)]
        + [shape((W, rows), F32 if slot else BF16)] * groups,
        [pltpu.VMEM((4, 2, frames, span), BF16)],
        limit=16,
        cost_estimate=cost(groups, frames),
    )(*own, *sib, *biases, prev, tables, carry, g_odd)


def band_cut_body(table, out):
    half = table.shape[1] // 2
    span = half // 2
    pair = pair_of()
    for n in range(2):
        out[:, n * span : (n + 1) * span] = table[:, columns(n * half + pair * span, span)]


def band_cut(table):
    rows, width = table.shape
    return call(band_cut_body, "band_cut", shape((rows, width // 2), BF16))(table)


def band_pack_body(steps, *refs):
    own, sib = refs[steps:]
    core, z = lax.axis_index("core"), lax.axis_index("z")
    span = own.shape[2]
    for n in range(steps):
        at = z ^ n
        own[at] = refs[n][:, columns(core * span, span)]
        sib[at] = refs[n][:, columns((1 - core) * span, span)]


def band_pack(parts):
    rows, width = parts[0].shape
    steps = len(parts)
    out = call(
        functools.partial(band_pack_body, steps),
        "band_pack",
        [shape((steps, rows, width // 2), BF16)] * 2,
    )(*parts)
    return [x.reshape(steps * rows, width // 2) for x in out]


def odd_rows_body(k, v, k_sib, v_sib, out):
    half = out.shape[2]
    core = lax.axis_index("core")
    for which, pair in enumerate(((k_sib, v_sib), (k, v))):

        @pl.when(core == which)
        def _():
            for n, x in enumerate(pair):
                out[n] = x[:, which * half : (which + 1) * half]


def odd_rows(*arrays):
    frames, width = arrays[0].shape
    return call(odd_rows_body, "odd_rows", shape((2, frames, width // 2), BF16))(*arrays)


def summed(refs):
    total = refs[0][...].astype(F32)
    for ref in refs[1:]:
        total = total + ref[...].astype(F32)
    return total


def pair_sum_body(steps, own0, own1, from_x, from_y, *refs):
    scr = refs[-1]
    z = lax.axis_index("z")
    rows = scr.shape[2]
    for n, (a, b) in enumerate(((own0, from_x), (own1, from_y))):
        total = (a[...] + b[...].astype(F32)).astype(BF16)
        for m in range(steps):
            scr[m, n * W : (n + 1) * W] = total[:, m * rows : (m + 1) * rows]
    for m in range(steps):
        refs[m][...] = scr[z ^ m]


def pair_sum(own, received, steps):
    rows = own[0].shape[1] // steps
    return call(
        functools.partial(pair_sum_body, steps),
        "pair_sum",
        [shape((2 * W, rows), BF16)] * steps,
        [pltpu.VMEM((steps, 2 * W, rows), BF16)],
    )(*own, *received)


def z_sum_body(*refs):
    refs[-1][...] = summed(refs[:-1]).astype(BF16)


def z_sum(parts):
    return call(z_sum_body, "z_sum", shape(parts[0].shape, BF16))(*parts)


def plane_sum_body(own, diagonal, from_x, from_y, mine, other, scr):
    core, pair = lax.axis_index("core"), pair_of()
    rows, half = mine.shape
    span = half // 2
    for n, terms in enumerate(((from_x, from_y), (own, diagonal))):
        total = summed(terms).T.reshape(2, rows, span)
        scr[:, :, columns((pair ^ n) * span, span)] = total
    mine[...] = scr[core]
    other[...] = scr[1 - core]


def plane_sum(parts):
    span, rows = parts[0].shape
    half = 2 * span
    return call(
        plane_sum_body,
        "plane_sum",
        [shape((rows // 2, half), F32)] * 2,
        [pltpu.VMEM((2, rows // 2, half), F32)],
    )(*parts)


def settle_body(*refs):
    odd, even, given = refs[0:4], refs[4:8], refs[8:10]
    own, sib, back = refs[10:]
    core, pair = lax.axis_index("core"), pair_of()
    span = odd[0].shape[1]
    for slot in range(2):
        here = columns((pair ^ slot) * span, span)
        for n in range(2):
            back[n, :, here] = given[slot][n].T
        for which, (first, second) in enumerate(((own, sib), (sib, own))):

            @pl.when(core == which)
            def _():
                for target, block in ((first, even), (second, odd)):
                    target[0, :, here] = block[2 * slot][...]
                    for n in range(2):
                        target[1 + n, :, here] = block[2 * slot + 1][n].T


def settle(odd, even, back):
    frames, span = odd[0].shape
    outs = [shape((3, frames, 2 * span), F32)] * 2 + [shape((2, frames, 2 * span), BF16)]
    return call(settle_body, "settle", outs)(*odd, *even, *back)


def rows_final_body(own, sib, back, back_sib, dq, dk, dv):
    core = lax.axis_index("core")
    half = own.shape[2]
    mine, other = columns(core * half, half), columns((1 - core) * half, half)
    dq[:, mine] = own[0].astype(BF16)
    dq[:, other] = sib[0].astype(BF16)
    odd = core == 1
    for n, out in enumerate((dk, dv)):
        out[:, mine] = (own[1 + n] + jnp.where(odd, back[n].astype(F32), 0.0)).astype(BF16)
        out[:, other] = (sib[1 + n] + jnp.where(odd, back_sib[n].astype(F32), 0.0)).astype(BF16)


def rows_final(own, sib, back, back_sib):
    frames, half = back.shape[1:]
    outs = [shape((frames, 2 * half), BF16)] * 3
    return call(rows_final_body, "rows_final", outs)(own, sib, back, back_sib)


def band_final_body(mine, other, out):
    core = lax.axis_index("core")
    half = mine.shape[1]
    out[:, columns(core * half, half)] = mine[...]
    out[:, columns((1 - core) * half, half)] = other[...]


def band_final(mine, other):
    rows, half = mine.shape
    return call(band_final_body, "band_final", shape((rows, 2 * half), F32))(mine, other)


def local(query_rows, key_rows, value_rows, grad_out, pos_keys, bias_content, bias_position):
    n_high, n_z = lax.axis_size("dh"), lax.axis_size("z")
    width = query_rows.shape[2]

    def along_z(x, flip):
        return lax.ppermute(x, "z", [(s, s ^ flip) for s in range(n_z)])

    def around_z(x, steps):
        return lax.ppermute(x, "z", [(s, (s + steps) % n_z) for s in range(n_z)])

    def to_sibling(x):
        return lax.ppermute(x, "core", [(0, 1), (1, 0)])

    def in_plane(x, flip, cross=0):
        pairs = [
            (2 * d + c, 2 * (d ^ flip) + (c ^ cross)) for d in range(PLANE) for c in range(2)
        ]
        return lax.ppermute(x, ("dl", "core"), pairs)

    cut = band_cut(pos_keys)
    cuts = [cut] + [along_z(cut, k) for k in range(1, n_z)]
    own = [x[0] for x in (query_rows, key_rows, value_rows, grad_out)]
    sib = [to_sibling(x) for x in own]
    prev = around_z(odd_rows(*own[1:3], *sib[1:3]), 1)
    band_own, band_sib = band_pack(cuts)
    first_bands = [band_own, to_sibling(band_sib)]
    second_bands = [in_plane(band_own, 1), in_plane(band_sib, 2, 1)]
    biases = [bias_content.reshape(1, width), bias_position.reshape(1, width)]

    inputs = (own, sib, biases)
    first = odd_call(0, *inputs, first_bands, n_z)
    second = odd_call(1, *inputs, second_bands, n_z)
    first, second = lax.optimization_barrier((first, second))
    even0 = even_call(0, *inputs, prev, first)
    received = [in_plane(even0[3], 1), in_plane(even0[4], 2)]
    even1 = even_call(1, *inputs, prev, second)
    g_own = even1[3:]

    *parts, turn = lax.optimization_barrier((*pair_sum(g_own, received, n_z), even0[2]))
    parts = [along_z(parts[k], k) for k in range(n_z - 1, 0, -1)] + [parts[0]]
    odd, even = (*first[:2], *second[:2]), (*even0[:2], *even1[:2])
    out_own, out_sib, back = settle(odd, even, (turn, even1[2]))
    *parts, back, out_sib = lax.optimization_barrier((*parts, back, out_sib))
    back = around_z(back, -1)
    out_sib = to_sibling(out_sib)
    total = z_sum(parts)
    step = 1
    while step < n_high:
        pairs = [(s, s ^ step) for s in range(n_high)]
        total = z_sum([total, lax.ppermute(total, "dh", pairs)])
        step *= 2
    planes = [in_plane(total, k) for k in (3, 1, 2)]
    *planes, back = lax.optimization_barrier((*planes, back))
    back_sib = to_sibling(back)
    mine, other = plane_sum([total, *planes])
    other = to_sibling(other)
    rows = rows_final(out_own, out_sib, back, back_sib)
    *rows, mine, other = lax.optimization_barrier((*rows, mine, other))
    return *[x[None] for x in rows], band_final(mine, other)


def solution(mesh):
    n_dp, n_blk = mesh.shape["dp"], mesh.shape["blk"]
    fine = Mesh(mesh.devices.reshape(n_dp // PLANE, PLANE, n_blk // 2, 2), ("dh", "dl", "z", "core"))
    rows = P(("dh", "dl"), ("z", "core"), None)
    band = P(("z", "core"), None)
    return jax.shard_map(
        local,
        mesh=fine,
        in_specs=(rows, rows, rows, rows, band, P(), P()),
        out_specs=(rows, rows, rows, band),
        check_vma=False,
    )
```

```python
import functools

import jax
import jax.numpy as jnp
from jax import lax
from jax.experimental import pallas as pl
from jax.experimental.pallas import tpu as pltpu
from jax.sharding import Mesh
from jax.sharding import PartitionSpec as P

DH = 64
W = 128
PLANE = 4
MIB = 2**20
F32 = jnp.float32
BF16 = jnp.bfloat16


def mm(a, b):
    return jnp.dot(a, b, preferred_element_type=F32)


def mm_nt(a, b):
    return lax.dot_general(a, b, (((1,), (1,)), ((), ())), preferred_element_type=F32)


def iota(shape, axis):
    return lax.broadcasted_iota(jnp.int32, shape, axis)


def as_bf16(hit):
    return hit.astype(F32).astype(BF16)


CHUNK = 32


def shear(x, frames, row):
    return pltpu.roll(x, frames + 1 + row, 1, stride=1, stride_axis=0)


def columns(start, size):
    return pl.ds(pl.multiple_of(start, W), size)


class Masks:
    def __init__(self, frames):
        span = 2 * frames
        lane = iota((frames, W), 1)
        sub = iota((W, frames), 0)
        self.first = lane < DH
        scale = jnp.bfloat16(DH**-0.5)
        self.lanes = [as_bf16(lane < DH) * scale, as_bf16(lane >= DH) * scale]
        self.subs = [as_bf16(sub < DH), as_bf16(sub >= DH)]
        self.flip = as_bf16(iota((span, span), 0) + iota((span, span), 1) == span - 1)
        row, col = iota((frames, frames), 0), iota((frames, frames), 1)
        self.forward = col + row >= frames - 1
        self.back = [as_bf16(col > row), as_bf16(col <= row)]

    def stack(self, x):
        return jnp.concatenate([x * self.lanes[0], x * self.lanes[1]], axis=0)

    def stack_t(self, x):
        x = x.T
        return jnp.concatenate([x * self.subs[0], x * self.subs[1]], axis=1)


def unit(masks, q, k, v, g, k_before, v_before, tables, bias_c, bias_p):
    frames = q.shape[0]
    band0, band1, band0_rev, band1_rev = tables
    kw = jnp.concatenate([k, k_before], axis=0)
    vw = jnp.concatenate([v, v_before], axis=0)
    qf = q.astype(F32)
    qc = (qf + bias_c).astype(BF16)
    qp = (qf + bias_p).astype(BF16)
    qp_stack = masks.stack(qp)
    content = mm_nt(masks.stack(qc), kw)
    near, far = mm_nt(qp_stack, band0_rev), mm_nt(qp_stack, band1_rev)
    gw = mm_nt(masks.stack(g), vw)
    yield
    ds, attention_b = [], []
    for start in range(0, 2 * frames, CHUNK):
        rows, first = slice(start, start + CHUNK), start % frames
        own = masks.forward[first : first + CHUNK]
        merged = [
            jnp.where(own, near[rows, :frames], far[rows, :frames]),
            jnp.where(own, far[rows, frames:], near[rows, frames:]),
        ]
        scores = content[rows] + shear(jnp.concatenate(merged, axis=1), frames, first)
        e = jnp.exp(scores - jnp.max(scores, axis=1, keepdims=True))
        inverse = 1.0 / jnp.sum(e, axis=1, keepdims=True)
        delta = jnp.sum(e * gw[rows], axis=1, keepdims=True) * inverse
        attention = e * inverse
        attention_b.append(attention.astype(BF16))
        ds.append((attention * (gw[rows] - delta)).astype(BF16))
        yield
    ds, attention_b = jnp.concatenate(ds, axis=0), jnp.concatenate(attention_b, axis=0)
    flipped = mm(ds, masks.flip)
    dk = mm(masks.stack_t(qc), ds)
    dv = mm(masks.stack_t(g), attention_b)
    yield
    d0, d1 = [], []
    for start in range(0, 2 * frames, CHUNK):
        first = start % frames
        placed = shear(flipped[start : start + CHUNK], frames, first).astype(BF16)
        left, right = placed[:, :frames], placed[:, frames:]
        mask = [m[first : first + CHUNK] for m in masks.back]
        d0.append(jnp.concatenate([left * mask[0], right * mask[1]], axis=1))
        d1.append(jnp.concatenate([left * mask[1], right * mask[0]], axis=1))
        yield
    d0, d1 = jnp.concatenate(d0, axis=0), jnp.concatenate(d1, axis=0)
    lhs = jnp.concatenate([ds, d0, d1], axis=1)
    rhs = jnp.concatenate([kw, band0, band1], axis=0)
    full = mm(lhs, rhs)
    dq = jnp.where(masks.first, full[:frames], full[frames:]).astype(BF16).astype(F32)
    qp_t = masks.stack_t(qp)
    g1 = mm(qp_t, d1)
    g_band = jnp.concatenate([mm(qp_t, d0), g1[:, frames:], g1[:, :frames]], axis=1)
    return dq, dk, dv, g_band


def side_by_side(groups):
    results = [None] * len(groups)
    left = list(enumerate(groups))
    while left:
        for n, group in list(left):
            try:
                next(group)
            except StopIteration as end:
                results[n] = end.value
                left.remove((n, group))
    return results


def call(body, name, out_shape, scratch=(), limit=8, **options):
    return pl.pallas_call(
        body,
        out_shape=out_shape,
        scratch_shapes=list(scratch),
        compiler_params=pltpu.CompilerParams(vmem_limit_bytes=limit * MIB),
        name=name,
        **options,
    )


def shape(dims, dtype):
    return jax.ShapeDtypeStruct(tuple(dims), dtype)


def pair_of():
    low = lax.axis_index("dl")
    return (low & 1) ^ (low >> 1)


def place(own, sib, scr, slot):
    core = lax.axis_index("core")
    span = scr.shape[3]
    here = columns((2 * core + (pair_of() ^ slot)) * span, span)
    for n, (a, b) in enumerate(zip(own, sib)):
        scr[n, core] = a[:, here]
        scr[n, 1 - core] = b[:, here]
    return here


def odd_body(steps, slot, *refs):
    own, sib, (bias_c, bias_p), bands = refs[0:4], refs[4:8], refs[8:10], refs[10:12]
    dq_out, out, carry, g_out, tables, scr, band_scr = refs[12:]
    core = lax.axis_index("core")
    frames, span = scr.shape[2:]
    share = band_scr.shape[2]
    here = place(own, sib, scr, slot)
    bias_c, bias_p = bias_c[:, here], bias_p[:, here]
    band_scr[:, core] = bands[0][...].reshape(steps, share, span)
    band_scr[:, 1 - core] = bands[1][...].reshape(steps, share, span)
    band = band_scr[...].reshape(steps * 2 * share, span)
    masks = Masks(frames)
    band0, band1 = band[: 2 * frames], band[2 * frames :]
    band1 = jnp.concatenate([band1[frames:], band1[:frames]], axis=0)
    tables[0] = band0
    tables[1] = band1
    tables[2] = mm(masks.flip, band0).astype(BF16)
    tables[3] = mm(masks.flip, band1).astype(BF16)
    cuts = [slice(j * W, (j + 1) * W) for j in range(span // W)]
    groups = [
        unit(
            masks,
            *[scr[n, 1, :, at] for n in range(4)],
            scr[1, 0, :, at],
            scr[2, 0, :, at],
            [tables[n, :, at] for n in range(4)],
            bias_c[:, at],
            bias_p[:, at],
        )
        for at in cuts
    ]
    for j, (dq, dk, dv, g_band) in enumerate(side_by_side(groups)):
        at = cuts[j]
        dq_out[:, at] = dq
        for n, term in enumerate((dk, dv)):
            out[n, at] = term[:, :frames]
            carry[n, at] = term[:, frames:].astype(BF16)
        g_out[j] = g_band


def even_body(slot, *refs):
    own, sib, (bias_c, bias_p) = refs[0:4], refs[4:8], refs[8:10]
    prev, tables, carry, g_odd = refs[10:14]
    dq_out, out, back = refs[14:17]
    g_outs, scr = refs[17:-1], refs[-1]
    frames, span = scr.shape[2:]
    here = place(own, sib, scr, slot)
    bias_c, bias_p = bias_c[:, here], bias_p[:, here]
    masks = Masks(frames)
    cuts = [slice(j * W, (j + 1) * W) for j in range(span // W)]
    groups = []
    for j, at in enumerate(cuts):
        mine = columns((pair_of() ^ slot) * span + j * W, W)
        groups.append(
            unit(
                masks,
                *[scr[n, 0, :, at] for n in range(4)],
                prev[0, :, mine],
                prev[1, :, mine],
                [tables[n, :, at] for n in range(4)],
                bias_c[:, at],
                bias_p[:, at],
            )
        )
    for j, (dq, dk, dv, g_band) in enumerate(side_by_side(groups)):
        at = cuts[j]
        dq_out[:, at] = dq
        for n, term in enumerate((dk, dv)):
            out[n, at] = term[:, :frames] + carry[n, at].astype(F32)
            back[n, at] = term[:, frames:].astype(BF16)
        g_outs[j][...] = (g_odd[j] + g_band).astype(g_outs[j].dtype)


def cost(groups, frames):
    return pl.CostEstimate(
        flops=2 * groups * 20 * frames * (2 * frames) ** 2,
        bytes_accessed=64 * groups * frames * W,
        transcendentals=groups * 4 * frames * frames,
    )


def odd_call(slot, own, sib, biases, bands, steps):
    frames = own[0].shape[0]
    rows, span = bands[0].shape
    groups = span // W
    return call(
        functools.partial(odd_body, steps, slot),
        "odd_block",
        [
            shape((frames, span), F32),
            shape((2, span, frames), F32),
            shape((2, span, frames), BF16),
            shape((groups, W, 2 * rows), F32),
            shape((4, rows, span), BF16),
        ],
        [
            pltpu.VMEM((4, 2, frames, span), BF16),
            pltpu.VMEM((steps, 2, rows // steps, span), BF16),
        ],
        limit=16,
        cost_estimate=cost(groups, frames),
    )(*own, *sib, *biases, *bands)


def even_call(slot, own, sib, biases, prev, odd):
    frames = own[0].shape[0]
    _, _, carry, g_odd, tables = odd
    groups, _, rows = g_odd.shape
    span = groups * W
    return call(
        functools.partial(even_body, slot),
        "even_block",
        [shape((frames, span), F32), shape((2, span, frames), F32), shape((2, span, frames), BF16)]
        + [shape((W, rows), F32 if slot else BF16)] * groups,
        [pltpu.VMEM((4, 2, frames, span), BF16)],
        limit=16,
        cost_estimate=cost(groups, frames),
    )(*own, *sib, *biases, prev, tables, carry, g_odd)


def band_cut_body(table, out):
    half = table.shape[1] // 2
    span = half // 2
    pair = pair_of()
    for n in range(2):
        out[:, n * span : (n + 1) * span] = table[:, columns(n * half + pair * span, span)]


def band_cut(table):
    rows, width = table.shape
    return call(band_cut_body, "band_cut", shape((rows, width // 2), BF16))(table)


def band_pack_body(steps, *refs):
    own, sib = refs[steps:]
    core, z = lax.axis_index("core"), lax.axis_index("z")
    span = own.shape[2]
    for n in range(steps):
        at = z ^ n
        own[at] = refs[n][:, columns(core * span, span)]
        sib[at] = refs[n][:, columns((1 - core) * span, span)]


def band_pack(parts):
    rows, width = parts[0].shape
    steps = len(parts)
    out = call(
        functools.partial(band_pack_body, steps),
        "band_pack",
        [shape((steps, rows, width // 2), BF16)] * 2,
    )(*parts)
    return [x.reshape(steps * rows, width // 2) for x in out]


def odd_rows_body(k, v, k_sib, v_sib, out):
    half = out.shape[2]
    core = lax.axis_index("core")
    for which, pair in enumerate(((k_sib, v_sib), (k, v))):

        @pl.when(core == which)
        def _():
            for n, x in enumerate(pair):
                out[n] = x[:, which * half : (which + 1) * half]


def odd_rows(*arrays):
    frames, width = arrays[0].shape
    return call(odd_rows_body, "odd_rows", shape((2, frames, width // 2), BF16))(*arrays)


def summed(refs):
    total = refs[0][...].astype(F32)
    for ref in refs[1:]:
        total = total + ref[...].astype(F32)
    return total


def pair_sum_body(steps, own0, own1, from_x, from_y, *refs):
    scr = refs[-1]
    z = lax.axis_index("z")
    rows = scr.shape[2]
    for n, (a, b) in enumerate(((own0, from_x), (own1, from_y))):
        total = (a[...] + b[...].astype(F32)).astype(BF16)
        for m in range(steps):
            scr[m, n * W : (n + 1) * W] = total[:, m * rows : (m + 1) * rows]
    for m in range(steps):
        refs[m][...] = scr[z ^ m]


def pair_sum(own, received, steps):
    rows = own[0].shape[1] // steps
    return call(
        functools.partial(pair_sum_body, steps),
        "pair_sum",
        [shape((2 * W, rows), BF16)] * steps,
        [pltpu.VMEM((steps, 2 * W, rows), BF16)],
    )(*own, *received)


def z_sum_body(*refs):
    refs[-1][...] = summed(refs[:-1]).astype(BF16)


def z_sum(parts):
    return call(z_sum_body, "z_sum", shape(parts[0].shape, BF16))(*parts)


def plane_sum_body(own, diagonal, from_x, from_y, mine, other, scr):
    core, pair = lax.axis_index("core"), pair_of()
    rows, half = mine.shape
    span = half // 2
    for n, terms in enumerate(((from_x, from_y), (own, diagonal))):
        total = summed(terms).T.reshape(2, rows, span)
        scr[:, :, columns((pair ^ n) * span, span)] = total
    mine[...] = scr[core]
    other[...] = scr[1 - core]


def plane_sum(parts):
    span, rows = parts[0].shape
    half = 2 * span
    return call(
        plane_sum_body,
        "plane_sum",
        [shape((rows // 2, half), F32)] * 2,
        [pltpu.VMEM((2, rows // 2, half), F32)],
    )(*parts)


def settle_body(*refs):
    odd, even, given = refs[0:4], refs[4:8], refs[8:10]
    own, sib, back = refs[10:]
    core, pair = lax.axis_index("core"), pair_of()
    span = odd[0].shape[1]
    for slot in range(2):
        here = columns((pair ^ slot) * span, span)
        for n in range(2):
            back[n, :, here] = given[slot][n].T
        for which, (first, second) in enumerate(((own, sib), (sib, own))):

            @pl.when(core == which)
            def _():
                for target, block in ((first, even), (second, odd)):
                    target[0, :, here] = block[2 * slot][...]
                    for n in range(2):
                        target[1 + n, :, here] = block[2 * slot + 1][n].T


def settle(odd, even, back):
    frames, span = odd[0].shape
    outs = [shape((3, frames, 2 * span), F32)] * 2 + [shape((2, frames, 2 * span), BF16)]
    return call(settle_body, "settle", outs)(*odd, *even, *back)


def widen_body(x, out):
    out[...] = x[...].astype(F32)


def widen(x):
    return call(widen_body, "widen", shape(x.shape, F32))(x)


def rows_final_body(own, sib, back, back_sib, dq, dk, dv):
    core = lax.axis_index("core")
    half = own.shape[2]
    mine, other = columns(core * half, half), columns((1 - core) * half, half)
    dq[:, mine] = own[0].astype(BF16)
    dq[:, other] = sib[0].astype(BF16)
    odd = core == 1
    for n, out in enumerate((dk, dv)):
        out[:, mine] = (own[1 + n] + jnp.where(odd, back[n].astype(F32), 0.0)).astype(BF16)
        out[:, other] = (sib[1 + n] + jnp.where(odd, back_sib[n], 0.0)).astype(BF16)


def rows_final(own, sib, back, back_sib):
    frames, half = back.shape[1:]
    outs = [shape((frames, 2 * half), BF16)] * 3
    return call(rows_final_body, "rows_final", outs)(own, sib, back, back_sib)


def band_final_body(mine, other, out):
    core = lax.axis_index("core")
    half = mine.shape[1]
    out[:, columns(core * half, half)] = mine[...]
    out[:, columns((1 - core) * half, half)] = other[...]


def band_final(mine, other):
    rows, half = mine.shape
    return call(band_final_body, "band_final", shape((rows, 2 * half), F32))(mine, other)


def local(query_rows, key_rows, value_rows, grad_out, pos_keys, bias_content, bias_position):
    n_high, n_z = lax.axis_size("dh"), lax.axis_size("z")
    width = query_rows.shape[2]

    def along_z(x, flip):
        return lax.ppermute(x, "z", [(s, s ^ flip) for s in range(n_z)])

    def around_z(x, steps):
        return lax.ppermute(x, "z", [(s, (s + steps) % n_z) for s in range(n_z)])

    def to_sibling(x):
        return lax.ppermute(x, "core", [(0, 1), (1, 0)])

    def in_plane(x, flip, cross=0):
        pairs = [
            (2 * d + c, 2 * (d ^ flip) + (c ^ cross)) for d in range(PLANE) for c in range(2)
        ]
        return lax.ppermute(x, ("dl", "core"), pairs)

    cut = band_cut(pos_keys)
    cuts = [cut] + [along_z(cut, k) for k in range(1, n_z)]
    own = [x[0] for x in (query_rows, key_rows, value_rows, grad_out)]
    sib = [to_sibling(x) for x in own]
    prev = around_z(odd_rows(*own[1:3], *sib[1:3]), 1)
    band_own, band_sib = band_pack(cuts)
    first_bands = [band_own, to_sibling(band_sib)]
    second_bands = [in_plane(band_own, 1), in_plane(band_sib, 2, 1)]
    biases = [bias_content.reshape(1, width), bias_position.reshape(1, width)]

    inputs = (own, sib, biases)
    first = odd_call(0, *inputs, first_bands, n_z)
    second = odd_call(1, *inputs, second_bands, n_z)
    first, second = lax.optimization_barrier((first, second))
    even0 = even_call(0, *inputs, prev, first)
    received = [in_plane(even0[3], 1), in_plane(even0[4], 2)]
    even1 = even_call(1, *inputs, prev, second)
    g_own = even1[3:]

    *parts, turn = lax.optimization_barrier((*pair_sum(g_own, received, n_z), even0[2]))
    parts = [along_z(parts[k], k) for k in range(n_z - 1, 0, -1)] + [parts[0]]
    odd, even = (*first[:2], *second[:2]), (*even0[:2], *even1[:2])
    out_own, out_sib, back = settle(odd, even, (turn, even1[2]))
    *parts, out_sib = lax.optimization_barrier((*parts, out_sib))
    back = around_z(back, -1)
    out_sib = to_sibling(out_sib)
    total = z_sum(parts)
    step = 1
    while step < n_high:
        pairs = [(s, s ^ step) for s in range(n_high)]
        total = z_sum([total, lax.ppermute(total, "dh", pairs)])
        step *= 2
    planes = [in_plane(total, k) for k in (3, 1, 2)]
    *planes, back = lax.optimization_barrier((*planes, back))
    back_sib = to_sibling(widen(back))
    mine, other = plane_sum([total, *planes])
    other = to_sibling(other)
    rows = rows_final(out_own, out_sib, back, back_sib)
    *rows, mine, other = lax.optimization_barrier((*rows, mine, other))
    return *[x[None] for x in rows], band_final(mine, other)


def solution(mesh):
    n_dp, n_blk = mesh.shape["dp"], mesh.shape["blk"]
    fine = Mesh(mesh.devices.reshape(n_dp // PLANE, PLANE, n_blk // 2, 2), ("dh", "dl", "z", "core"))
    rows = P(("dh", "dl"), ("z", "core"), None)
    band = P(("z", "core"), None)
    return jax.shard_map(
        local,
        mesh=fine,
        in_specs=(rows, rows, rows, rows, band, P(), P()),
        out_specs=(rows, rows, rows, band),
        check_vma=False,
    )
```

```python
import functools

import jax
import jax.numpy as jnp
from jax import lax
from jax.experimental import pallas as pl
from jax.experimental.pallas import tpu as pltpu
from jax.sharding import Mesh
from jax.sharding import PartitionSpec as P

DH = 64
W = 128
PLANE = 4
MIB = 2**20
F32 = jnp.float32
BF16 = jnp.bfloat16


def mm(a, b):
    return jnp.dot(a, b, preferred_element_type=F32)


def mm_nt(a, b):
    return lax.dot_general(a, b, (((1,), (1,)), ((), ())), preferred_element_type=F32)


def iota(shape, axis):
    return lax.broadcasted_iota(jnp.int32, shape, axis)


def as_bf16(hit):
    return hit.astype(F32).astype(BF16)


CHUNK = 32


def shear(x, frames, row):
    return pltpu.roll(x, frames + 1 + row, 1, stride=1, stride_axis=0)


def columns(start, size):
    return pl.ds(pl.multiple_of(start, W), size)


class Masks:
    def __init__(self, frames):
        span = 2 * frames
        lane = iota((frames, W), 1)
        sub = iota((W, frames), 0)
        self.first = lane < DH
        scale = jnp.bfloat16(DH**-0.5)
        self.lanes = [as_bf16(lane < DH) * scale, as_bf16(lane >= DH) * scale]
        self.subs = [as_bf16(sub < DH), as_bf16(sub >= DH)]
        self.flip = as_bf16(iota((span, span), 0) + iota((span, span), 1) == span - 1)
        row, col = iota((frames, frames), 0), iota((frames, frames), 1)
        self.forward = col + row >= frames - 1
        self.back = [as_bf16(col > row), as_bf16(col <= row)]

    def stack(self, x):
        return jnp.concatenate([x * self.lanes[0], x * self.lanes[1]], axis=0)

    def stack_t(self, x):
        x = x.T
        return jnp.concatenate([x * self.subs[0], x * self.subs[1]], axis=1)


def operands(masks, q, g, bias_c, bias_p):
    qf = q.astype(F32)
    rows = ((qf + bias_c).astype(BF16), (qf + bias_p).astype(BF16), g)
    return [masks.stack(x) for x in rows], [masks.stack_t(x) for x in rows]


def unit(masks, stacks, turned, kw, vw, tables, products=None):
    frames = turned[0].shape[1] // 2
    band0, band1, band0_rev, band1_rev = tables
    qp_stack = stacks[1]
    if products is None:
        products = mm_nt(stacks[0], kw), mm_nt(stacks[2], vw)
    content, gw = products
    near, far = mm_nt(qp_stack, band0_rev), mm_nt(qp_stack, band1_rev)
    yield
    ds, attention_b = [], []
    for start in range(0, 2 * frames, CHUNK):
        rows, first = slice(start, start + CHUNK), start % frames
        own = masks.forward[first : first + CHUNK]
        merged = [
            jnp.where(own, near[rows, :frames], far[rows, :frames]),
            jnp.where(own, far[rows, frames:], near[rows, frames:]),
        ]
        scores = content[rows] + shear(jnp.concatenate(merged, axis=1), frames, first)
        e = jnp.exp(scores - jnp.max(scores, axis=1, keepdims=True))
        inverse = 1.0 / jnp.sum(e, axis=1, keepdims=True)
        delta = jnp.sum(e * gw[rows], axis=1, keepdims=True) * inverse
        attention = e * inverse
        attention_b.append(attention.astype(BF16))
        ds.append((attention * (gw[rows] - delta)).astype(BF16))
        yield
    ds, attention_b = jnp.concatenate(ds, axis=0), jnp.concatenate(attention_b, axis=0)
    flipped = mm(ds, masks.flip)
    dk = mm(turned[0], ds)
    dv = mm(turned[2], attention_b)
    yield
    d0, d1 = [], []
    for start in range(0, 2 * frames, CHUNK):
        first = start % frames
        placed = shear(flipped[start : start + CHUNK], frames, first).astype(BF16)
        left, right = placed[:, :frames], placed[:, frames:]
        mask = [m[first : first + CHUNK] for m in masks.back]
        d0.append(jnp.concatenate([left * mask[0], right * mask[1]], axis=1))
        d1.append(jnp.concatenate([left * mask[1], right * mask[0]], axis=1))
        yield
    d0, d1 = jnp.concatenate(d0, axis=0), jnp.concatenate(d1, axis=0)
    lhs = jnp.concatenate([ds, d0, d1], axis=1)
    rhs = jnp.concatenate([kw, band0, band1], axis=0)
    full = mm(lhs, rhs)
    dq = jnp.where(masks.first, full[:frames], full[frames:]).astype(BF16).astype(F32)
    g1 = mm(turned[1], d1)
    g_band = jnp.concatenate([mm(turned[1], d0), g1[:, frames:], g1[:, :frames]], axis=1)
    return dq, dk, dv, g_band


def side_by_side(groups):
    results = [None] * len(groups)
    left = list(enumerate(groups))
    while left:
        for n, group in list(left):
            try:
                next(group)
            except StopIteration as end:
                results[n] = end.value
                left.remove((n, group))
    return results


def call(body, name, out_shape, scratch=(), limit=8, **options):
    return pl.pallas_call(
        body,
        out_shape=out_shape,
        scratch_shapes=list(scratch),
        compiler_params=pltpu.CompilerParams(vmem_limit_bytes=limit * MIB),
        name=name,
        **options,
    )


def shape(dims, dtype):
    return jax.ShapeDtypeStruct(tuple(dims), dtype)


def pair_of():
    low = lax.axis_index("dl")
    return (low & 1) ^ (low >> 1)


def place(own, sib, scr, slot):
    core = lax.axis_index("core")
    span = scr.shape[3]
    here = columns((2 * core + (pair_of() ^ slot)) * span, span)
    for n, (a, b) in enumerate(zip(own, sib)):
        scr[n, core] = a[:, here]
        scr[n, 1 - core] = b[:, here]
    return here


def ahead_body(*refs):
    own, sib, (bias_c, bias_p) = refs[0:4], refs[4:8], refs[8:10]
    stacks, turned, rows, products, scr = refs[10:]
    frames, span = scr.shape[2:]
    masks = Masks(frames)
    for slot in range(2):
        here = place(own, sib, scr, slot)
        at_bias = bias_c[:, here], bias_p[:, here]
        for j in range(span // W):
            at = slice(j * W, (j + 1) * W)
            for b in range(2):
                if slot == 0 and b == 1:
                    continue
                which = slot + b
                made = operands(masks, scr[0, b, :, at], scr[3, b, :, at], *[x[:, at] for x in at_bias])
                for n in range(3):
                    stacks[which, j, n] = made[0][n]
                    turned[which, j, n] = made[1][n]
                k, v = scr[1, b, :, at], scr[2, b, :, at]
                if b == 0:
                    rows[which, j] = jnp.concatenate([k, v], axis=0)
                else:
                    kw = jnp.concatenate([k, scr[1, 0, :, at]], axis=0)
                    vw = jnp.concatenate([v, scr[2, 0, :, at]], axis=0)
                    rows[which, j] = kw
                    products[j, 0] = mm_nt(made[0][0], kw)
                    products[j, 1] = mm_nt(made[0][2], vw)


def ahead(own, sib, biases):
    frames, width = own[0].shape
    span = width // 4
    groups = span // W
    return call(
        ahead_body,
        "ahead",
        [
            shape((3, groups, 3, 2 * frames, W), BF16),
            shape((3, groups, 3, W, 2 * frames), BF16),
            shape((3, groups, 2 * frames, W), BF16),
            shape((groups, 2, 2 * frames, 2 * frames), F32),
        ],
        [pltpu.VMEM((4, 2, frames, span), BF16)],
        limit=16,
    )(*own, *sib, *biases)


def odd_body(steps, slot, *refs):
    count = 4 if slot else 10
    given, bands, refs = refs[:count], refs[count : count + 2], refs[count + 2 :]
    dq_out, out, carry, g_out, tables, scr, band_scr = refs
    core = lax.axis_index("core")
    frames, span = scr.shape[2:]
    share = band_scr.shape[2]
    band_scr[:, core] = bands[0][...].reshape(steps, share, span)
    band_scr[:, 1 - core] = bands[1][...].reshape(steps, share, span)
    band = band_scr[...].reshape(steps * 2 * share, span)
    masks = Masks(frames)
    band0, band1 = band[: 2 * frames], band[2 * frames :]
    band1 = jnp.concatenate([band1[frames:], band1[:frames]], axis=0)
    tables[0] = band0
    tables[1] = band1
    tables[2] = mm(masks.flip, band0).astype(BF16)
    tables[3] = mm(masks.flip, band1).astype(BF16)
    cuts = [slice(j * W, (j + 1) * W) for j in range(span // W)]
    groups = []
    if slot:
        stacks, turned, rows, products = given
        for j, at in enumerate(cuts):
            made = [[x[2, j, n] for n in range(3)] for x in (stacks, turned)]
            table = [tables[n, :, at] for n in range(4)]
            ready = products[j, 0], products[j, 1]
            groups.append(unit(masks, *made, rows[2, j], None, table, ready))
    else:
        here = place(given[0:4], given[4:8], scr, slot)
        at_bias = given[8][:, here], given[9][:, here]
        for at in cuts:
            made = operands(masks, scr[0, 1, :, at], scr[3, 1, :, at], *[x[:, at] for x in at_bias])
            window = [
                jnp.concatenate([scr[n, 1, :, at], scr[n, 0, :, at]], axis=0) for n in (1, 2)
            ]
            groups.append(unit(masks, *made, *window, [tables[n, :, at] for n in range(4)]))
    for j, (dq, dk, dv, g_band) in enumerate(side_by_side(groups)):
        at = cuts[j]
        dq_out[:, at] = dq
        for n, term in enumerate((dk, dv)):
            out[n, at] = term[:, :frames]
            carry[n, at] = term[:, frames:].astype(BF16)
        g_out[j] = g_band


def even_body(slot, *refs):
    stacks, turned, rows, _, prev, tables, carry, g_odd = refs[:8]
    dq_out, out, back, *g_outs = refs[8:]
    frames, span = dq_out.shape
    masks = Masks(frames)
    cuts = [slice(j * W, (j + 1) * W) for j in range(span // W)]
    groups = []
    for j, at in enumerate(cuts):
        mine = columns((pair_of() ^ slot) * span + j * W, W)
        made = [[x[slot, j, n] for n in range(3)] for x in (stacks, turned)]
        window = [
            jnp.concatenate([rows[slot, j, n * frames : (n + 1) * frames], prev[n, :, mine]], axis=0)
            for n in range(2)
        ]
        groups.append(unit(masks, *made, *window, [tables[n, :, at] for n in range(4)]))
    for j, (dq, dk, dv, g_band) in enumerate(side_by_side(groups)):
        at = cuts[j]
        dq_out[:, at] = dq
        for n, term in enumerate((dk, dv)):
            out[n, at] = term[:, :frames] + carry[n, at].astype(F32)
            back[n, at] = term[:, frames:].astype(BF16)
        g_outs[j][...] = (g_odd[j] + g_band).astype(g_outs[j].dtype)


def cost(groups, frames):
    return pl.CostEstimate(
        flops=2 * groups * 20 * frames * (2 * frames) ** 2,
        bytes_accessed=64 * groups * frames * W,
        transcendentals=groups * 4 * frames * frames,
    )


def odd_call(slot, given, bands, steps, frames):
    rows, span = bands[0].shape
    groups = span // W
    return call(
        functools.partial(odd_body, steps, slot),
        "odd_block",
        [
            shape((frames, span), F32),
            shape((2, span, frames), F32),
            shape((2, span, frames), BF16),
            shape((groups, W, 2 * rows), F32),
            shape((4, rows, span), BF16),
        ],
        [
            pltpu.VMEM((4, 2, frames, span), BF16),
            pltpu.VMEM((steps, 2, rows // steps, span), BF16),
        ],
        limit=16,
        cost_estimate=cost(groups, frames),
    )(*given, *bands)


def even_call(slot, given, prev, odd):
    frames = prev.shape[1]
    _, _, carry, g_odd, tables = odd
    groups, _, rows = g_odd.shape
    span = groups * W
    return call(
        functools.partial(even_body, slot),
        "even_block",
        [shape((frames, span), F32), shape((2, span, frames), F32), shape((2, span, frames), BF16)]
        + [shape((W, rows), F32 if slot else BF16)] * groups,
        limit=16,
        cost_estimate=cost(groups, frames),
    )(*given, prev, tables, carry, g_odd)


def band_cut_body(table, out):
    half = table.shape[1] // 2
    span = half // 2
    pair = pair_of()
    for n in range(2):
        out[:, n * span : (n + 1) * span] = table[:, columns(n * half + pair * span, span)]


def band_cut(table):
    rows, width = table.shape
    return call(band_cut_body, "band_cut", shape((rows, width // 2), BF16))(table)


def band_pack_body(steps, *refs):
    own, sib = refs[steps:]
    core, z = lax.axis_index("core"), lax.axis_index("z")
    span = own.shape[2]
    for n in range(steps):
        at = z ^ n
        own[at] = refs[n][:, columns(core * span, span)]
        sib[at] = refs[n][:, columns((1 - core) * span, span)]


def band_pack(parts):
    rows, width = parts[0].shape
    steps = len(parts)
    out = call(
        functools.partial(band_pack_body, steps),
        "band_pack",
        [shape((steps, rows, width // 2), BF16)] * 2,
    )(*parts)
    return [x.reshape(steps * rows, width // 2) for x in out]


def odd_rows_body(k, v, k_sib, v_sib, out):
    half = out.shape[2]
    core = lax.axis_index("core")
    for which, pair in enumerate(((k_sib, v_sib), (k, v))):

        @pl.when(core == which)
        def _():
            for n, x in enumerate(pair):
                out[n] = x[:, which * half : (which + 1) * half]


def odd_rows(*arrays):
    frames, width = arrays[0].shape
    return call(odd_rows_body, "odd_rows", shape((2, frames, width // 2), BF16))(*arrays)


def summed(refs):
    total = refs[0][...].astype(F32)
    for ref in refs[1:]:
        total = total + ref[...].astype(F32)
    return total


def pair_sum_body(steps, own0, own1, from_x, from_y, *refs):
    scr = refs[-1]
    z = lax.axis_index("z")
    rows = scr.shape[2]
    for n, (a, b) in enumerate(((own0, from_x), (own1, from_y))):
        total = (a[...] + b[...].astype(F32)).astype(BF16)
        for m in range(steps):
            scr[m, n * W : (n + 1) * W] = total[:, m * rows : (m + 1) * rows]
    for m in range(steps):
        refs[m][...] = scr[z ^ m]


def pair_sum(own, received, steps):
    rows = own[0].shape[1] // steps
    return call(
        functools.partial(pair_sum_body, steps),
        "pair_sum",
        [shape((2 * W, rows), BF16)] * steps,
        [pltpu.VMEM((steps, 2 * W, rows), BF16)],
    )(*own, *received)


def z_sum_body(*refs):
    refs[-1][...] = summed(refs[:-1]).astype(BF16)


def z_sum(parts):
    return call(z_sum_body, "z_sum", shape(parts[0].shape, BF16))(*parts)


def plane_sum_body(own, diagonal, from_x, from_y, mine, other, scr):
    core, pair = lax.axis_index("core"), pair_of()
    rows, half = mine.shape
    span = half // 2
    for n, terms in enumerate(((from_x, from_y), (own, diagonal))):
        total = summed(terms).T.reshape(2, rows, span)
        scr[:, :, columns((pair ^ n) * span, span)] = total
    mine[...] = scr[core]
    other[...] = scr[1 - core]


def plane_sum(parts):
    span, rows = parts[0].shape
    half = 2 * span
    return call(
        plane_sum_body,
        "plane_sum",
        [shape((rows // 2, half), F32)] * 2,
        [pltpu.VMEM((2, rows // 2, half), F32)],
    )(*parts)


def settle_body(*refs):
    odd, even, given = refs[0:4], refs[4:8], refs[8:10]
    own, sib, back = refs[10:]
    core, pair = lax.axis_index("core"), pair_of()
    span = odd[0].shape[1]
    for slot in range(2):
        here = columns((pair ^ slot) * span, span)
        for n in range(2):
            back[n, :, here] = given[slot][n].T
        for which, (first, second) in enumerate(((own, sib), (sib, own))):

            @pl.when(core == which)
            def _():
                for target, block in ((first, even), (second, odd)):
                    target[0, :, here] = block[2 * slot][...]
                    for n in range(2):
                        target[1 + n, :, here] = block[2 * slot + 1][n].T


def settle(odd, even, back):
    frames, span = odd[0].shape
    outs = [shape((3, frames, 2 * span), F32)] * 2 + [shape((2, frames, 2 * span), BF16)]
    return call(settle_body, "settle", outs)(*odd, *even, *back)


def rows_final_body(own, sib, back, back_sib, dq, dk, dv):
    core = lax.axis_index("core")
    half = own.shape[2]
    mine, other = columns(core * half, half), columns((1 - core) * half, half)
    dq[:, mine] = own[0].astype(BF16)
    dq[:, other] = sib[0].astype(BF16)
    odd = core == 1
    for n, out in enumerate((dk, dv)):
        out[:, mine] = (own[1 + n] + jnp.where(odd, back[n].astype(F32), 0.0)).astype(BF16)
        out[:, other] = (sib[1 + n] + jnp.where(odd, back_sib[n].astype(F32), 0.0)).astype(BF16)


def rows_final(own, sib, back, back_sib):
    frames, half = back.shape[1:]
    outs = [shape((frames, 2 * half), BF16)] * 3
    return call(rows_final_body, "rows_final", outs)(own, sib, back, back_sib)


def band_final_body(mine, other, out):
    core = lax.axis_index("core")
    half = mine.shape[1]
    out[:, columns(core * half, half)] = mine[...]
    out[:, columns((1 - core) * half, half)] = other[...]


def band_final(mine, other):
    rows, half = mine.shape
    return call(band_final_body, "band_final", shape((rows, 2 * half), F32))(mine, other)


def local(query_rows, key_rows, value_rows, grad_out, pos_keys, bias_content, bias_position):
    n_high, n_z = lax.axis_size("dh"), lax.axis_size("z")
    width = query_rows.shape[2]

    def along_z(x, flip):
        return lax.ppermute(x, "z", [(s, s ^ flip) for s in range(n_z)])

    def around_z(x, steps):
        return lax.ppermute(x, "z", [(s, (s + steps) % n_z) for s in range(n_z)])

    def to_sibling(x):
        return lax.ppermute(x, "core", [(0, 1), (1, 0)])

    def in_plane(x, flip, cross=0):
        pairs = [
            (2 * d + c, 2 * (d ^ flip) + (c ^ cross)) for d in range(PLANE) for c in range(2)
        ]
        return lax.ppermute(x, ("dl", "core"), pairs)

    cut = band_cut(pos_keys)
    cuts = [cut] + [along_z(cut, k) for k in range(1, n_z)]
    own = [x[0] for x in (query_rows, key_rows, value_rows, grad_out)]
    sib = [to_sibling(x) for x in own]
    prev = around_z(odd_rows(*own[1:3], *sib[1:3]), 1)
    band_own, band_sib = band_pack(cuts)
    first_bands = [band_own, to_sibling(band_sib)]
    second_bands = [in_plane(band_own, 1), in_plane(band_sib, 2, 1)]
    biases = [bias_content.reshape(1, width), bias_position.reshape(1, width)]

    frames = own[0].shape[0]
    first = odd_call(0, (*own, *sib, *biases), first_bands, n_z, frames)
    *later_biases, carry = lax.optimization_barrier((*biases, first[2]))
    first = (*first[:2], carry, *first[3:])
    later = ahead(own, sib, later_biases)
    second = odd_call(1, later, second_bands, n_z, frames)
    first, second = lax.optimization_barrier((first, second))
    even0 = even_call(0, later, prev, first)
    received = [in_plane(even0[3], 1), in_plane(even0[4], 2)]
    even1 = even_call(1, later, prev, second)
    g_own = even1[3:]

    *parts, turn = lax.optimization_barrier((*pair_sum(g_own, received, n_z), even0[2]))
    parts = [along_z(parts[k], k) for k in range(n_z - 1, 0, -1)] + [parts[0]]
    odd, even = (*first[:2], *second[:2]), (*even0[:2], *even1[:2])
    out_own, out_sib, back = settle(odd, even, (turn, even1[2]))
    *parts, back, out_sib = lax.optimization_barrier((*parts, back, out_sib))
    back = around_z(back, -1)
    out_sib = to_sibling(out_sib)
    total = z_sum(parts)
    step = 1
    while step < n_high:
        pairs = [(s, s ^ step) for s in range(n_high)]
        total = z_sum([total, lax.ppermute(total, "dh", pairs)])
        step *= 2
    planes = [in_plane(total, k) for k in (3, 1, 2)]
    *planes, back = lax.optimization_barrier((*planes, back))
    back_sib = to_sibling(back)
    mine, other = plane_sum([total, *planes])
    other = to_sibling(other)
    rows = rows_final(out_own, out_sib, back, back_sib)
    *rows, mine, other = lax.optimization_barrier((*rows, mine, other))
    return *[x[None] for x in rows], band_final(mine, other)


def solution(mesh):
    n_dp, n_blk = mesh.shape["dp"], mesh.shape["blk"]
    fine = Mesh(mesh.devices.reshape(n_dp // PLANE, PLANE, n_blk // 2, 2), ("dh", "dl", "z", "core"))
    rows = P(("dh", "dl"), ("z", "core"), None)
    band = P(("z", "core"), None)
    return jax.shard_map(
        local,
        mesh=fine,
        in_specs=(rows, rows, rows, rows, band, P(), P()),
        out_specs=(rows, rows, rows, band),
        check_vma=False,
    )
```

```python
import functools

import jax
import jax.numpy as jnp
from jax import lax
from jax.experimental import pallas as pl
from jax.experimental.pallas import tpu as pltpu
from jax.sharding import Mesh
from jax.sharding import PartitionSpec as P

DH = 64
W = 128
PLANE = 4
MIB = 2**20
F32 = jnp.float32
BF16 = jnp.bfloat16


def mm(a, b):
    return jnp.dot(a, b, preferred_element_type=F32)


def mm_nt(a, b):
    return lax.dot_general(a, b, (((1,), (1,)), ((), ())), preferred_element_type=F32)


def iota(shape, axis):
    return lax.broadcasted_iota(jnp.int32, shape, axis)


def as_bf16(hit):
    return hit.astype(F32).astype(BF16)


CHUNK = 32


def shear(x, frames, row):
    return pltpu.roll(x, frames + 1 + row, 1, stride=1, stride_axis=0)


def columns(start, size):
    return pl.ds(pl.multiple_of(start, W), size)


class Masks:
    def __init__(self, frames):
        span = 2 * frames
        lane = iota((frames, W), 1)
        sub = iota((W, frames), 0)
        self.first = lane < DH
        scale = jnp.bfloat16(DH**-0.5)
        self.lanes = [as_bf16(lane < DH) * scale, as_bf16(lane >= DH) * scale]
        self.subs = [as_bf16(sub < DH), as_bf16(sub >= DH)]
        self.flip = as_bf16(iota((span, span), 0) + iota((span, span), 1) == span - 1)
        row, col = iota((frames, frames), 0), iota((frames, frames), 1)
        self.forward = col + row >= frames - 1
        self.back = [as_bf16(col > row), as_bf16(col <= row)]

    def stack(self, x):
        return jnp.concatenate([x * self.lanes[0], x * self.lanes[1]], axis=0)

    def stack_t(self, x):
        x = x.T
        return jnp.concatenate([x * self.subs[0], x * self.subs[1]], axis=1)


def operands(masks, q, g, bias_c, bias_p):
    qf = q.astype(F32)
    rows = ((qf + bias_c).astype(BF16), (qf + bias_p).astype(BF16), g)
    return [masks.stack(x) for x in rows], [masks.stack_t(x) for x in rows]


def unit(masks, stacks, turned, kw, vw, tables, products=None):
    frames = turned[0].shape[1] // 2
    band0, band1, band0_rev, band1_rev = tables
    qp_stack = stacks[1]
    if products is None:
        products = mm_nt(stacks[0], kw), mm_nt(stacks[2], vw)
    content, gw = products
    near, far = mm_nt(qp_stack, band0_rev), mm_nt(qp_stack, band1_rev)
    yield
    ds, attention_b = [], []
    for start in range(0, 2 * frames, CHUNK):
        rows, first = slice(start, start + CHUNK), start % frames
        own = masks.forward[first : first + CHUNK]
        merged = [
            jnp.where(own, near[rows, :frames], far[rows, :frames]),
            jnp.where(own, far[rows, frames:], near[rows, frames:]),
        ]
        scores = content[rows] + shear(jnp.concatenate(merged, axis=1), frames, first)
        e = jnp.exp(scores - jnp.max(scores, axis=1, keepdims=True))
        inverse = 1.0 / jnp.sum(e, axis=1, keepdims=True)
        delta = jnp.sum(e * gw[rows], axis=1, keepdims=True) * inverse
        attention = e * inverse
        attention_b.append(attention.astype(BF16))
        ds.append((attention * (gw[rows] - delta)).astype(BF16))
        yield
    ds, attention_b = jnp.concatenate(ds, axis=0), jnp.concatenate(attention_b, axis=0)
    flipped = mm(ds, masks.flip)
    dk = mm(turned[0], ds)
    dv = mm(turned[2], attention_b)
    yield
    d0, d1 = [], []
    for start in range(0, 2 * frames, CHUNK):
        first = start % frames
        placed = shear(flipped[start : start + CHUNK], frames, first).astype(BF16)
        left, right = placed[:, :frames], placed[:, frames:]
        mask = [m[first : first + CHUNK] for m in masks.back]
        d0.append(jnp.concatenate([left * mask[0], right * mask[1]], axis=1))
        d1.append(jnp.concatenate([left * mask[1], right * mask[0]], axis=1))
        yield
    d0, d1 = jnp.concatenate(d0, axis=0), jnp.concatenate(d1, axis=0)
    lhs = jnp.concatenate([ds, d0, d1], axis=1)
    rhs = jnp.concatenate([kw, band0, band1], axis=0)
    full = mm(lhs, rhs)
    dq = jnp.where(masks.first, full[:frames], full[frames:]).astype(BF16).astype(F32)
    g1 = mm(turned[1], d1)
    g_band = jnp.concatenate([mm(turned[1], d0), g1[:, frames:], g1[:, :frames]], axis=1)
    return dq, dk, dv, g_band


def side_by_side(groups):
    results = [None] * len(groups)
    left = list(enumerate(groups))
    while left:
        for n, group in list(left):
            try:
                next(group)
            except StopIteration as end:
                results[n] = end.value
                left.remove((n, group))
    return results


def call(body, name, out_shape, scratch=(), limit=8, **options):
    return pl.pallas_call(
        body,
        out_shape=out_shape,
        scratch_shapes=list(scratch),
        compiler_params=pltpu.CompilerParams(vmem_limit_bytes=limit * MIB),
        name=name,
        **options,
    )


def shape(dims, dtype):
    return jax.ShapeDtypeStruct(tuple(dims), dtype)


def pair_of():
    low = lax.axis_index("dl")
    return (low & 1) ^ (low >> 1)


def place(own, sib, scr, slot):
    core = lax.axis_index("core")
    span = scr.shape[3]
    here = columns((2 * core + (pair_of() ^ slot)) * span, span)
    for n, (a, b) in enumerate(zip(own, sib)):
        scr[n, core] = a[:, here]
        scr[n, 1 - core] = b[:, here]
    return here


def ahead_body(*refs):
    own, sib, (bias_c, bias_p) = refs[0:4], refs[4:8], refs[8:10]
    stacks, turned, rows, products, scr = refs[10:]
    frames, span = scr.shape[2:]
    masks = Masks(frames)
    for slot in range(2):
        here = place(own, sib, scr, slot)
        at_bias = bias_c[:, here], bias_p[:, here]
        for j in range(span // W):
            at = slice(j * W, (j + 1) * W)
            for b in range(2):
                if slot == 0 and b == 1:
                    continue
                which = slot + b
                made = operands(masks, scr[0, b, :, at], scr[3, b, :, at], *[x[:, at] for x in at_bias])
                for n in range(3):
                    stacks[which, j, n] = made[0][n]
                    turned[which, j, n] = made[1][n]
                k, v = scr[1, b, :, at], scr[2, b, :, at]
                if b == 0:
                    rows[which, j] = jnp.concatenate([k, v], axis=0)
                else:
                    kw = jnp.concatenate([k, scr[1, 0, :, at]], axis=0)
                    vw = jnp.concatenate([v, scr[2, 0, :, at]], axis=0)
                    rows[which, j] = kw
                    products[j, 0] = mm_nt(made[0][0], kw)
                    products[j, 1] = mm_nt(made[0][2], vw)


def ahead(own, sib, biases):
    frames, width = own[0].shape
    span = width // 4
    groups = span // W
    return call(
        ahead_body,
        "ahead",
        [
            shape((3, groups, 3, 2 * frames, W), BF16),
            shape((3, groups, 3, W, 2 * frames), BF16),
            shape((3, groups, 2 * frames, W), BF16),
            shape((groups, 2, 2 * frames, 2 * frames), F32),
        ],
        [pltpu.VMEM((4, 2, frames, span), BF16)],
        limit=16,
    )(*own, *sib, *biases)


def odd_body(steps, slot, *refs):
    count = 4 if slot else 10
    given, bands, refs = refs[:count], refs[count : count + 2], refs[count + 2 :]
    dq_out, out, carry, g_out, tables, scr, band_scr = refs
    core = lax.axis_index("core")
    frames, span = scr.shape[2:]
    share = band_scr.shape[2]
    band_scr[:, core] = bands[0][...].reshape(steps, share, span)
    band_scr[:, 1 - core] = bands[1][...].reshape(steps, share, span)
    band = band_scr[...].reshape(steps * 2 * share, span)
    masks = Masks(frames)
    band0, band1 = band[: 2 * frames], band[2 * frames :]
    band1 = jnp.concatenate([band1[frames:], band1[:frames]], axis=0)
    tables[0] = band0
    tables[1] = band1
    tables[2] = mm(masks.flip, band0).astype(BF16)
    tables[3] = mm(masks.flip, band1).astype(BF16)
    cuts = [slice(j * W, (j + 1) * W) for j in range(span // W)]
    groups = []
    if slot:
        stacks, turned, rows, products = given
        for j, at in enumerate(cuts):
            made = [[x[2, j, n] for n in range(3)] for x in (stacks, turned)]
            table = [tables[n, :, at] for n in range(4)]
            ready = products[j, 0], products[j, 1]
            groups.append(unit(masks, *made, rows[2, j], None, table, ready))
    else:
        here = place(given[0:4], given[4:8], scr, slot)
        at_bias = given[8][:, here], given[9][:, here]
        for at in cuts:
            made = operands(masks, scr[0, 1, :, at], scr[3, 1, :, at], *[x[:, at] for x in at_bias])
            window = [
                jnp.concatenate([scr[n, 1, :, at], scr[n, 0, :, at]], axis=0) for n in (1, 2)
            ]
            groups.append(unit(masks, *made, *window, [tables[n, :, at] for n in range(4)]))
    for j, (dq, dk, dv, g_band) in enumerate(side_by_side(groups)):
        at = cuts[j]
        dq_out[:, at] = dq
        for n, term in enumerate((dk, dv)):
            out[n, at] = term[:, :frames]
            carry[n, at] = term[:, frames:].astype(BF16)
        g_out[j] = g_band


def even_body(slot, *refs):
    stacks, turned, rows, _, prev, tables, carry, g_odd = refs[:8]
    dq_out, out, back, *g_outs = refs[8:]
    frames, span = dq_out.shape
    masks = Masks(frames)
    cuts = [slice(j * W, (j + 1) * W) for j in range(span // W)]
    groups = []
    for j, at in enumerate(cuts):
        mine = columns((pair_of() ^ slot) * span + j * W, W)
        made = [[x[slot, j, n] for n in range(3)] for x in (stacks, turned)]
        window = [
            jnp.concatenate([rows[slot, j, n * frames : (n + 1) * frames], prev[n, :, mine]], axis=0)
            for n in range(2)
        ]
        groups.append(unit(masks, *made, *window, [tables[n, :, at] for n in range(4)]))
    for j, (dq, dk, dv, g_band) in enumerate(side_by_side(groups)):
        at = cuts[j]
        dq_out[:, at] = dq
        for n, term in enumerate((dk, dv)):
            out[n, at] = term[:, :frames] + carry[n, at].astype(F32)
            back[n, at] = term[:, frames:].astype(BF16)
        g_outs[j][...] = (g_odd[j] + g_band).astype(g_outs[j].dtype)


def cost(groups, frames):
    return pl.CostEstimate(
        flops=2 * groups * 20 * frames * (2 * frames) ** 2,
        bytes_accessed=64 * groups * frames * W,
        transcendentals=groups * 4 * frames * frames,
    )


def odd_call(slot, given, bands, steps, frames):
    rows, span = bands[0].shape
    groups = span // W
    return call(
        functools.partial(odd_body, steps, slot),
        "odd_block",
        [
            shape((frames, span), F32),
            shape((2, span, frames), F32),
            shape((2, span, frames), BF16),
            shape((groups, W, 2 * rows), F32),
            shape((4, rows, span), BF16),
        ],
        [
            pltpu.VMEM((4, 2, frames, span), BF16),
            pltpu.VMEM((steps, 2, rows // steps, span), BF16),
        ],
        limit=16,
        cost_estimate=cost(groups, frames),
    )(*given, *bands)


def even_call(slot, given, prev, odd):
    frames = prev.shape[1]
    _, _, carry, g_odd, tables = odd
    groups, _, rows = g_odd.shape
    span = groups * W
    return call(
        functools.partial(even_body, slot),
        "even_block",
        [shape((frames, span), F32), shape((2, span, frames), F32), shape((2, span, frames), BF16)]
        + [shape((W, rows), F32 if slot else BF16)] * groups,
        limit=16,
        cost_estimate=cost(groups, frames),
    )(*given, prev, tables, carry, g_odd)


def band_cut_body(table, out):
    half = table.shape[1] // 2
    span = half // 2
    pair = pair_of()
    for n in range(2):
        out[:, n * span : (n + 1) * span] = table[:, columns(n * half + pair * span, span)]


def band_cut(table):
    rows, width = table.shape
    return call(band_cut_body, "band_cut", shape((rows, width // 2), BF16))(table)


def band_pack_body(steps, *refs):
    own, sib = refs[steps:]
    core, z = lax.axis_index("core"), lax.axis_index("z")
    span = own.shape[2]
    for n in range(steps):
        at = z ^ n
        own[at] = refs[n][:, columns(core * span, span)]
        sib[at] = refs[n][:, columns((1 - core) * span, span)]


def band_pack(parts):
    rows, width = parts[0].shape
    steps = len(parts)
    out = call(
        functools.partial(band_pack_body, steps),
        "band_pack",
        [shape((steps, rows, width // 2), BF16)] * 2,
    )(*parts)
    return [x.reshape(steps * rows, width // 2) for x in out]


def odd_rows_body(k, v, k_sib, v_sib, out):
    half = out.shape[2]
    core = lax.axis_index("core")

    @pl.when(core == 0)
    def _():
        out[0] = k_sib[:, :half]
        out[1] = v_sib[:, :half]

    @pl.when(core == 1)
    def _():
        out[0] = k[...]
        out[1] = v[...]


def odd_rows(k, v, k_sib, v_sib):
    return call(odd_rows_body, "odd_rows", shape((2, *k.shape), BF16))(k, v, k_sib, v_sib)


def summed(refs):
    total = refs[0][...].astype(F32)
    for ref in refs[1:]:
        total = total + ref[...].astype(F32)
    return total


def pair_sum_body(steps, own0, own1, from_x, from_y, *refs):
    scr = refs[-1]
    z = lax.axis_index("z")
    rows = scr.shape[2]
    for n, (a, b) in enumerate(((own0, from_x), (own1, from_y))):
        total = (a[...] + b[...].astype(F32)).astype(BF16)
        for m in range(steps):
            scr[m, n * W : (n + 1) * W] = total[:, m * rows : (m + 1) * rows]
    for m in range(steps):
        refs[m][...] = scr[z ^ m]


def pair_sum(own, received, steps):
    rows = own[0].shape[1] // steps
    return call(
        functools.partial(pair_sum_body, steps),
        "pair_sum",
        [shape((2 * W, rows), BF16)] * steps,
        [pltpu.VMEM((steps, 2 * W, rows), BF16)],
    )(*own, *received)


def z_sum_body(*refs):
    refs[-1][...] = summed(refs[:-1]).astype(BF16)


def z_sum(parts):
    return call(z_sum_body, "z_sum", shape(parts[0].shape, BF16))(*parts)


def plane_sum_body(own, diagonal, from_x, from_y, mine, other, scr):
    core, pair = lax.axis_index("core"), pair_of()
    rows, half = mine.shape
    span = half // 2
    for n, terms in enumerate(((from_x, from_y), (own, diagonal))):
        total = summed(terms).T.reshape(2, rows, span)
        scr[:, :, columns((pair ^ n) * span, span)] = total
    mine[...] = scr[core]
    other[...] = scr[1 - core]


def plane_sum(parts):
    span, rows = parts[0].shape
    half = 2 * span
    return call(
        plane_sum_body,
        "plane_sum",
        [shape((rows // 2, half), F32)] * 2,
        [pltpu.VMEM((2, rows // 2, half), F32)],
    )(*parts)


def settle_body(*refs):
    odd, even, given = refs[0:4], refs[4:8], refs[8:10]
    own, sib, back = refs[10:]
    core, pair = lax.axis_index("core"), pair_of()
    span = odd[0].shape[1]
    for slot in range(2):
        here = columns((pair ^ slot) * span, span)
        for n in range(2):
            back[n, :, here] = given[slot][n].T
        for which, (first, second) in enumerate(((own, sib), (sib, own))):

            @pl.when(core == which)
            def _():
                for target, block in ((first, even), (second, odd)):
                    target[0, :, here] = block[2 * slot][...]
                    for n in range(2):
                        target[1 + n, :, here] = block[2 * slot + 1][n].T


def settle(odd, even, back):
    frames, span = odd[0].shape
    outs = [shape((3, frames, 2 * span), F32)] * 2 + [shape((2, frames, 2 * span), BF16)]
    return call(settle_body, "settle", outs)(*odd, *even, *back)


def rows_final_body(own, sib, back, back_sib, dq, dk, dv):
    core = lax.axis_index("core")
    half = own.shape[2]
    mine, other = columns(core * half, half), columns((1 - core) * half, half)
    dq[:, mine] = own[0].astype(BF16)
    dq[:, other] = sib[0].astype(BF16)
    odd = core == 1
    for n, out in enumerate((dk, dv)):
        out[:, mine] = (own[1 + n] + jnp.where(odd, back[n].astype(F32), 0.0)).astype(BF16)
        out[:, other] = (sib[1 + n] + jnp.where(odd, back_sib[n].astype(F32), 0.0)).astype(BF16)


def rows_final(own, sib, back, back_sib):
    frames, half = back.shape[1:]
    outs = [shape((frames, 2 * half), BF16)] * 3
    return call(rows_final_body, "rows_final", outs)(own, sib, back, back_sib)


def band_final_body(mine, other, out):
    core = lax.axis_index("core")
    half = mine.shape[1]
    out[:, columns(core * half, half)] = mine[...]
    out[:, columns((1 - core) * half, half)] = other[...]


def band_final(mine, other):
    rows, half = mine.shape
    return call(band_final_body, "band_final", shape((rows, 2 * half), F32))(mine, other)


def local(query_rows, key_rows, value_rows, grad_out, pos_keys, bias_content, bias_position):
    n_high, n_z = lax.axis_size("dh"), lax.axis_size("z")
    width = query_rows.shape[2]

    def along_z(x, flip):
        return lax.ppermute(x, "z", [(s, s ^ flip) for s in range(n_z)])

    def around_z(x, steps):
        return lax.ppermute(x, "z", [(s, (s + steps) % n_z) for s in range(n_z)])

    def to_sibling(x):
        return lax.ppermute(x, "core", [(0, 1), (1, 0)])

    def in_plane(x, flip, cross=0):
        pairs = [
            (2 * d + c, 2 * (d ^ flip) + (c ^ cross)) for d in range(PLANE) for c in range(2)
        ]
        return lax.ppermute(x, ("dl", "core"), pairs)

    cut = band_cut(pos_keys)
    cuts = [cut] + [along_z(cut, k) for k in range(1, n_z)]
    own = [x[0] for x in (query_rows, key_rows, value_rows, grad_out)]
    sib = [to_sibling(x) for x in own]
    prev = around_z(odd_rows(*[x[:, width // 2 :] for x in own[1:3]], *sib[1:3]), 1)
    band_own, band_sib = band_pack(cuts)
    first_bands = [band_own, to_sibling(band_sib)]
    second_bands = [in_plane(band_own, 1), in_plane(band_sib, 2, 1)]
    biases = [bias_content.reshape(1, width), bias_position.reshape(1, width)]

    frames = own[0].shape[0]
    first = odd_call(0, (*own, *sib, *biases), first_bands, n_z, frames)
    *later_biases, carry = lax.optimization_barrier((*biases, first[2]))
    first = (*first[:2], carry, *first[3:])
    later = ahead(own, sib, later_biases)
    second = odd_call(1, later, second_bands, n_z, frames)
    first, second = lax.optimization_barrier((first, second))
    even0 = even_call(0, later, prev, first)
    received = [in_plane(even0[3], 1), in_plane(even0[4], 2)]
    even1 = even_call(1, later, prev, second)
    g_own = even1[3:]

    *parts, turn = lax.optimization_barrier((*pair_sum(g_own, received, n_z), even0[2]))
    parts = [along_z(parts[k], k) for k in range(n_z - 1, 0, -1)] + [parts[0]]
    odd, even = (*first[:2], *second[:2]), (*even0[:2], *even1[:2])
    out_own, out_sib, back = settle(odd, even, (turn, even1[2]))
    *parts, back, out_sib = lax.optimization_barrier((*parts, back, out_sib))
    back = around_z(back, -1)
    out_sib = to_sibling(out_sib)
    total = z_sum(parts)
    step = 1
    while step < n_high:
        pairs = [(s, s ^ step) for s in range(n_high)]
        total = z_sum([total, lax.ppermute(total, "dh", pairs)])
        step *= 2
    planes = [in_plane(total, k) for k in (3, 1, 2)]
    *planes, back = lax.optimization_barrier((*planes, back))
    back_sib = to_sibling(back)
    mine, other = plane_sum([total, *planes])
    other = to_sibling(other)
    rows = rows_final(out_own, out_sib, back, back_sib)
    *rows, mine, other = lax.optimization_barrier((*rows, mine, other))
    return *[x[None] for x in rows], band_final(mine, other)


def solution(mesh):
    n_dp, n_blk = mesh.shape["dp"], mesh.shape["blk"]
    fine = Mesh(mesh.devices.reshape(n_dp // PLANE, PLANE, n_blk // 2, 2), ("dh", "dl", "z", "core"))
    rows = P(("dh", "dl"), ("z", "core"), None)
    band = P(("z", "core"), None)
    return jax.shard_map(
        local,
        mesh=fine,
        in_specs=(rows, rows, rows, rows, band, P(), P()),
        out_specs=(rows, rows, rows, band),
        check_vma=False,
    )
```

```python
import functools

import jax
import jax.numpy as jnp
from jax import lax
from jax.experimental import pallas as pl
from jax.experimental.pallas import tpu as pltpu
from jax.sharding import Mesh
from jax.sharding import PartitionSpec as P

DH = 64
W = 128
PLANE = 4
MIB = 2**20
F32 = jnp.float32
BF16 = jnp.bfloat16


def mm(a, b):
    return jnp.dot(a, b, preferred_element_type=F32)


def mm_nt(a, b):
    return lax.dot_general(a, b, (((1,), (1,)), ((), ())), preferred_element_type=F32)


def iota(shape, axis):
    return lax.broadcasted_iota(jnp.int32, shape, axis)


def as_bf16(hit):
    return hit.astype(F32).astype(BF16)


CHUNK = 32


def shear(x, frames, row):
    return pltpu.roll(x, frames + 1 + row, 1, stride=1, stride_axis=0)


def columns(start, size):
    return pl.ds(pl.multiple_of(start, W), size)


class Masks:
    def __init__(self, frames):
        span = 2 * frames
        lane = iota((frames, W), 1)
        sub = iota((W, frames), 0)
        self.first = lane < DH
        scale = jnp.bfloat16(DH**-0.5)
        self.lanes = [as_bf16(lane < DH) * scale, as_bf16(lane >= DH) * scale]
        self.subs = [as_bf16(sub < DH), as_bf16(sub >= DH)]
        self.flip = as_bf16(iota((span, span), 0) + iota((span, span), 1) == span - 1)
        row, col = iota((frames, frames), 0), iota((frames, frames), 1)
        self.forward = col + row >= frames - 1
        self.back = [as_bf16(col > row), as_bf16(col <= row)]

    def stack(self, x):
        return jnp.concatenate([x * self.lanes[0], x * self.lanes[1]], axis=0)

    def stack_t(self, x):
        x = x.T
        return jnp.concatenate([x * self.subs[0], x * self.subs[1]], axis=1)


def operands(masks, q, g, bias_c, bias_p):
    qf = q.astype(F32)
    rows = ((qf + bias_c).astype(BF16), (qf + bias_p).astype(BF16), g)
    return [masks.stack(x) for x in rows], [masks.stack_t(x) for x in rows]


def unit(masks, stacks, turned, kw, vw, tables, products=None):
    frames = turned[0].shape[1] // 2
    band0, band1, band0_rev, band1_rev = tables
    qp_stack = stacks[1]
    if products is None:
        products = mm_nt(stacks[0], kw), mm_nt(stacks[2], vw)
    content, gw = products
    near, far = mm_nt(qp_stack, band0_rev), mm_nt(qp_stack, band1_rev)
    yield
    ds, attention_b = [], []
    for start in range(0, 2 * frames, CHUNK):
        rows, first = slice(start, start + CHUNK), start % frames
        own = masks.forward[first : first + CHUNK]
        merged = [
            jnp.where(own, near[rows, :frames], far[rows, :frames]),
            jnp.where(own, far[rows, frames:], near[rows, frames:]),
        ]
        scores = content[rows] + shear(jnp.concatenate(merged, axis=1), frames, first)
        e = jnp.exp(scores - jnp.max(scores, axis=1, keepdims=True))
        inverse = 1.0 / jnp.sum(e, axis=1, keepdims=True)
        delta = jnp.sum(e * gw[rows], axis=1, keepdims=True) * inverse
        attention = e * inverse
        attention_b.append(attention.astype(BF16))
        ds.append((attention * (gw[rows] - delta)).astype(BF16))
        yield
    ds, attention_b = jnp.concatenate(ds, axis=0), jnp.concatenate(attention_b, axis=0)
    flipped = mm(ds, masks.flip)
    dk = mm(turned[0], ds)
    dv = mm(turned[2], attention_b)
    yield
    d0, d1 = [], []
    for start in range(0, 2 * frames, CHUNK):
        first = start % frames
        placed = shear(flipped[start : start + CHUNK], frames, first).astype(BF16)
        left, right = placed[:, :frames], placed[:, frames:]
        mask = [m[first : first + CHUNK] for m in masks.back]
        d0.append(jnp.concatenate([left * mask[0], right * mask[1]], axis=1))
        d1.append(jnp.concatenate([left * mask[1], right * mask[0]], axis=1))
        yield
    d0, d1 = jnp.concatenate(d0, axis=0), jnp.concatenate(d1, axis=0)
    lhs = jnp.concatenate([ds, d0, d1], axis=1)
    rhs = jnp.concatenate([kw, band0, band1], axis=0)
    full = mm(lhs, rhs)
    dq = jnp.where(masks.first, full[:frames], full[frames:]).astype(BF16).astype(F32)
    g1 = mm(turned[1], d1)
    g_band = jnp.concatenate([mm(turned[1], d0), g1[:, frames:], g1[:, :frames]], axis=1)
    return dq, dk, dv, g_band


def side_by_side(groups):
    results = [None] * len(groups)
    left = list(enumerate(groups))
    while left:
        for n, group in list(left):
            try:
                next(group)
            except StopIteration as end:
                results[n] = end.value
                left.remove((n, group))
    return results


def call(body, name, out_shape, scratch=(), limit=8, **options):
    return pl.pallas_call(
        body,
        out_shape=out_shape,
        scratch_shapes=list(scratch),
        compiler_params=pltpu.CompilerParams(vmem_limit_bytes=limit * MIB),
        name=name,
        **options,
    )


def shape(dims, dtype):
    return jax.ShapeDtypeStruct(tuple(dims), dtype)


def pair_of():
    low = lax.axis_index("dl")
    return (low & 1) ^ (low >> 1)


def place(own, sib, scr, slot):
    core = lax.axis_index("core")
    span = scr.shape[3]
    here = columns((2 * core + (pair_of() ^ slot)) * span, span)
    for n, (a, b) in enumerate(zip(own, sib)):
        scr[n, core] = a[:, here]
        scr[n, 1 - core] = b[:, here]
    return here


def ahead_body(*refs):
    own, sib, (bias_c, bias_p) = refs[0:4], refs[4:8], refs[8:10]
    stacks, turned, rows, products, scr = refs[10:]
    frames, span = scr.shape[2:]
    masks = Masks(frames)
    for slot in range(2):
        here = place(own, sib, scr, slot)
        at_bias = bias_c[:, here], bias_p[:, here]
        for j in range(span // W):
            at = slice(j * W, (j + 1) * W)
            for b in range(2):
                if slot == 0 and b == 1:
                    continue
                which = slot + b
                made = operands(masks, scr[0, b, :, at], scr[3, b, :, at], *[x[:, at] for x in at_bias])
                for n in range(3):
                    stacks[which, j, n] = made[0][n]
                    turned[which, j, n] = made[1][n]
                k, v = scr[1, b, :, at], scr[2, b, :, at]
                if b == 0:
                    rows[which, j] = jnp.concatenate([k, v], axis=0)
                else:
                    kw = jnp.concatenate([k, scr[1, 0, :, at]], axis=0)
                    vw = jnp.concatenate([v, scr[2, 0, :, at]], axis=0)
                    rows[which, j] = kw
                    products[j, 0] = mm_nt(made[0][0], kw)
                    products[j, 1] = mm_nt(made[0][2], vw)


def ahead(own, sib, biases):
    frames, width = own[0].shape
    span = width // 4
    groups = span // W
    return call(
        ahead_body,
        "ahead",
        [
            shape((3, groups, 3, 2 * frames, W), BF16),
            shape((3, groups, 3, W, 2 * frames), BF16),
            shape((3, groups, 2 * frames, W), BF16),
            shape((groups, 2, 2 * frames, 2 * frames), F32),
        ],
        [pltpu.VMEM((4, 2, frames, span), BF16)],
        limit=16,
    )(*own, *sib, *biases)


def odd_body(steps, slot, *refs):
    count = 4 if slot else 10
    given, bands, refs = refs[:count], refs[count : count + 2], refs[count + 2 :]
    dq_out, out, carry, g_out, tables, scr, band_scr = refs
    core = lax.axis_index("core")
    frames, span = scr.shape[2:]
    share = band_scr.shape[2]
    band_scr[:, core] = bands[0][...].reshape(steps, share, span)
    band_scr[:, 1 - core] = bands[1][...].reshape(steps, share, span)
    band = band_scr[...].reshape(steps * 2 * share, span)
    masks = Masks(frames)
    band0, band1 = band[: 2 * frames], band[2 * frames :]
    band1 = jnp.concatenate([band1[frames:], band1[:frames]], axis=0)
    tables[0] = band0
    tables[1] = band1
    tables[2] = mm(masks.flip, band0).astype(BF16)
    tables[3] = mm(masks.flip, band1).astype(BF16)
    cuts = [slice(j * W, (j + 1) * W) for j in range(span // W)]
    groups = []
    if slot:
        stacks, turned, rows, products = given
        for j, at in enumerate(cuts):
            made = [[x[2, j, n] for n in range(3)] for x in (stacks, turned)]
            table = [tables[n, :, at] for n in range(4)]
            ready = products[j, 0], products[j, 1]
            groups.append(unit(masks, *made, rows[2, j], None, table, ready))
    else:
        here = place(given[0:4], given[4:8], scr, slot)
        at_bias = given[8][:, here], given[9][:, here]
        for at in cuts:
            made = operands(masks, scr[0, 1, :, at], scr[3, 1, :, at], *[x[:, at] for x in at_bias])
            window = [
                jnp.concatenate([scr[n, 1, :, at], scr[n, 0, :, at]], axis=0) for n in (1, 2)
            ]
            groups.append(unit(masks, *made, *window, [tables[n, :, at] for n in range(4)]))
    for j, (dq, dk, dv, g_band) in enumerate(side_by_side(groups)):
        at = cuts[j]
        dq_out[:, at] = dq
        for n, term in enumerate((dk, dv)):
            out[n, at] = term[:, :frames]
            carry[n, at] = term[:, frames:].astype(BF16)
        g_out[j] = g_band


def even_body(slot, *refs):
    stacks, turned, rows, _, prev, tables, carry, g_odd = refs[:8]
    dq_out, out, back, *g_outs = refs[8:]
    frames, span = dq_out.shape
    masks = Masks(frames)
    cuts = [slice(j * W, (j + 1) * W) for j in range(span // W)]
    groups = []
    for j, at in enumerate(cuts):
        mine = columns((pair_of() ^ slot) * span + j * W, W)
        made = [[x[slot, j, n] for n in range(3)] for x in (stacks, turned)]
        window = [
            jnp.concatenate([rows[slot, j, n * frames : (n + 1) * frames], prev[n, :, mine]], axis=0)
            for n in range(2)
        ]
        groups.append(unit(masks, *made, *window, [tables[n, :, at] for n in range(4)]))
    for j, (dq, dk, dv, g_band) in enumerate(side_by_side(groups)):
        at = cuts[j]
        dq_out[:, at] = dq
        for n, term in enumerate((dk, dv)):
            out[n, at] = term[:, :frames] + carry[n, at].astype(F32)
            back[n, at] = term[:, frames:].astype(BF16)
        g_outs[j][...] = (g_odd[j] + g_band).astype(g_outs[j].dtype)


def cost(groups, frames):
    return pl.CostEstimate(
        flops=2 * groups * 20 * frames * (2 * frames) ** 2,
        bytes_accessed=64 * groups * frames * W,
        transcendentals=groups * 4 * frames * frames,
    )


def odd_call(slot, given, bands, steps, frames):
    rows, span = bands[0].shape
    groups = span // W
    return call(
        functools.partial(odd_body, steps, slot),
        "odd_block",
        [
            shape((frames, span), F32),
            shape((2, span, frames), F32),
            shape((2, span, frames), BF16),
            shape((groups, W, 2 * rows), F32),
            shape((4, rows, span), BF16),
        ],
        [
            pltpu.VMEM((4, 2, frames, span), BF16),
            pltpu.VMEM((steps, 2, rows // steps, span), BF16),
        ],
        limit=16,
        cost_estimate=cost(groups, frames),
    )(*given, *bands)


def even_call(slot, given, prev, odd):
    frames = prev.shape[1]
    _, _, carry, g_odd, tables = odd
    groups, _, rows = g_odd.shape
    span = groups * W
    return call(
        functools.partial(even_body, slot),
        "even_block",
        [shape((frames, span), F32), shape((2, span, frames), F32), shape((2, span, frames), BF16)]
        + [shape((W, rows), F32 if slot else BF16)] * groups,
        limit=16,
        cost_estimate=cost(groups, frames),
    )(*given, prev, tables, carry, g_odd)


def band_cut_body(table, out):
    half = table.shape[1] // 2
    span = half // 2
    pair = pair_of()
    for n in range(2):
        out[:, n * span : (n + 1) * span] = table[:, columns(n * half + pair * span, span)]


def band_cut(table):
    rows, width = table.shape
    return call(band_cut_body, "band_cut", shape((rows, width // 2), BF16))(table)


def band_pack_body(steps, *refs):
    own, sib = refs[steps:]
    core, z = lax.axis_index("core"), lax.axis_index("z")
    span = own.shape[2]
    for n in range(steps):
        at = z ^ n
        own[at] = refs[n][:, columns(core * span, span)]
        sib[at] = refs[n][:, columns((1 - core) * span, span)]


def band_pack(parts):
    rows, width = parts[0].shape
    steps = len(parts)
    out = call(
        functools.partial(band_pack_body, steps),
        "band_pack",
        [shape((steps, rows, width // 2), BF16)] * 2,
    )(*parts)
    return [x.reshape(steps * rows, width // 2) for x in out]


def odd_rows(own, sib, half):
    mine = jnp.stack([x[:, half:] for x in own])
    other = jnp.stack([x[:, :half] for x in sib])
    return jnp.where(lax.axis_index("core") == 1, mine, other)


def summed(refs):
    total = refs[0][...].astype(F32)
    for ref in refs[1:]:
        total = total + ref[...].astype(F32)
    return total


def pair_sum_body(steps, own0, own1, from_x, from_y, *refs):
    scr = refs[-1]
    z = lax.axis_index("z")
    rows = scr.shape[2]
    for n, (a, b) in enumerate(((own0, from_x), (own1, from_y))):
        total = (a[...] + b[...].astype(F32)).astype(BF16)
        for m in range(steps):
            scr[m, n * W : (n + 1) * W] = total[:, m * rows : (m + 1) * rows]
    for m in range(steps):
        refs[m][...] = scr[z ^ m]


def pair_sum(own, received, steps):
    rows = own[0].shape[1] // steps
    return call(
        functools.partial(pair_sum_body, steps),
        "pair_sum",
        [shape((2 * W, rows), BF16)] * steps,
        [pltpu.VMEM((steps, 2 * W, rows), BF16)],
    )(*own, *received)


def z_sum_body(*refs):
    refs[-1][...] = summed(refs[:-1]).astype(BF16)


def z_sum(parts):
    return call(z_sum_body, "z_sum", shape(parts[0].shape, BF16))(*parts)


def plane_sum_body(own, diagonal, from_x, from_y, mine, other, scr):
    core, pair = lax.axis_index("core"), pair_of()
    rows, half = mine.shape
    span = half // 2
    for n, terms in enumerate(((from_x, from_y), (own, diagonal))):
        total = summed(terms).T.reshape(2, rows, span)
        scr[:, :, columns((pair ^ n) * span, span)] = total
    mine[...] = scr[core]
    other[...] = scr[1 - core]


def plane_sum(parts):
    span, rows = parts[0].shape
    half = 2 * span
    return call(
        plane_sum_body,
        "plane_sum",
        [shape((rows // 2, half), F32)] * 2,
        [pltpu.VMEM((2, rows // 2, half), F32)],
    )(*parts)


def settle_body(*refs):
    odd, even, given = refs[0:4], refs[4:8], refs[8:10]
    own, sib, back = refs[10:]
    core, pair = lax.axis_index("core"), pair_of()
    span = odd[0].shape[1]
    for slot in range(2):
        here = columns((pair ^ slot) * span, span)
        for n in range(2):
            back[n, :, here] = given[slot][n].T
        for which, (first, second) in enumerate(((own, sib), (sib, own))):

            @pl.when(core == which)
            def _():
                for target, block in ((first, even), (second, odd)):
                    target[0, :, here] = block[2 * slot][...]
                    for n in range(2):
                        target[1 + n, :, here] = block[2 * slot + 1][n].T


def settle(odd, even, back):
    frames, span = odd[0].shape
    outs = [shape((3, frames, 2 * span), F32)] * 2 + [shape((2, frames, 2 * span), BF16)]
    return call(settle_body, "settle", outs)(*odd, *even, *back)


def rows_final_body(own, sib, back, back_sib, dq, dk, dv):
    core = lax.axis_index("core")
    half = own.shape[2]
    mine, other = columns(core * half, half), columns((1 - core) * half, half)
    dq[:, mine] = own[0].astype(BF16)
    dq[:, other] = sib[0].astype(BF16)
    odd = core == 1
    for n, out in enumerate((dk, dv)):
        out[:, mine] = (own[1 + n] + jnp.where(odd, back[n].astype(F32), 0.0)).astype(BF16)
        out[:, other] = (sib[1 + n] + jnp.where(odd, back_sib[n].astype(F32), 0.0)).astype(BF16)


def rows_final(own, sib, back, back_sib):
    frames, half = back.shape[1:]
    outs = [shape((frames, 2 * half), BF16)] * 3
    return call(rows_final_body, "rows_final", outs)(own, sib, back, back_sib)


def band_final_body(mine, other, out):
    core = lax.axis_index("core")
    half = mine.shape[1]
    out[:, columns(core * half, half)] = mine[...]
    out[:, columns((1 - core) * half, half)] = other[...]


def band_final(mine, other):
    rows, half = mine.shape
    return call(band_final_body, "band_final", shape((rows, 2 * half), F32))(mine, other)


def local(query_rows, key_rows, value_rows, grad_out, pos_keys, bias_content, bias_position):
    n_high, n_z = lax.axis_size("dh"), lax.axis_size("z")
    width = query_rows.shape[2]

    def along_z(x, flip):
        return lax.ppermute(x, "z", [(s, s ^ flip) for s in range(n_z)])

    def around_z(x, steps):
        return lax.ppermute(x, "z", [(s, (s + steps) % n_z) for s in range(n_z)])

    def to_sibling(x):
        return lax.ppermute(x, "core", [(0, 1), (1, 0)])

    def in_plane(x, flip, cross=0):
        pairs = [
            (2 * d + c, 2 * (d ^ flip) + (c ^ cross)) for d in range(PLANE) for c in range(2)
        ]
        return lax.ppermute(x, ("dl", "core"), pairs)

    cut = band_cut(pos_keys)
    cuts = [cut] + [along_z(cut, k) for k in range(1, n_z)]
    own = [x[0] for x in (query_rows, key_rows, value_rows, grad_out)]
    sib = [to_sibling(x) for x in own]
    prev = around_z(odd_rows(own[1:3], sib[1:3], width // 2), 1)
    band_own, band_sib = band_pack(cuts)
    first_bands = [band_own, to_sibling(band_sib)]
    second_bands = [in_plane(band_own, 1), in_plane(band_sib, 2, 1)]
    biases = [bias_content.reshape(1, width), bias_position.reshape(1, width)]

    frames = own[0].shape[0]
    first = odd_call(0, (*own, *sib, *biases), first_bands, n_z, frames)
    *later_biases, carry = lax.optimization_barrier((*biases, first[2]))
    first = (*first[:2], carry, *first[3:])
    later = ahead(own, sib, later_biases)
    second = odd_call(1, later, second_bands, n_z, frames)
    first, second = lax.optimization_barrier((first, second))
    even0 = even_call(0, later, prev, first)
    received = [in_plane(even0[3], 1), in_plane(even0[4], 2)]
    even1 = even_call(1, later, prev, second)
    g_own = even1[3:]

    *parts, turn = lax.optimization_barrier((*pair_sum(g_own, received, n_z), even0[2]))
    parts = [along_z(parts[k], k) for k in range(n_z - 1, 0, -1)] + [parts[0]]
    odd, even = (*first[:2], *second[:2]), (*even0[:2], *even1[:2])
    out_own, out_sib, back = settle(odd, even, (turn, even1[2]))
    *parts, back, out_sib = lax.optimization_barrier((*parts, back, out_sib))
    back = around_z(back, -1)
    out_sib = to_sibling(out_sib)
    total = z_sum(parts)
    step = 1
    while step < n_high:
        pairs = [(s, s ^ step) for s in range(n_high)]
        total = z_sum([total, lax.ppermute(total, "dh", pairs)])
        step *= 2
    planes = [in_plane(total, k) for k in (3, 1, 2)]
    *planes, back = lax.optimization_barrier((*planes, back))
    back_sib = to_sibling(back)
    mine, other = plane_sum([total, *planes])
    other = to_sibling(other)
    rows = rows_final(out_own, out_sib, back, back_sib)
    *rows, mine, other = lax.optimization_barrier((*rows, mine, other))
    return *[x[None] for x in rows], band_final(mine, other)


def solution(mesh):
    n_dp, n_blk = mesh.shape["dp"], mesh.shape["blk"]
    fine = Mesh(mesh.devices.reshape(n_dp // PLANE, PLANE, n_blk // 2, 2), ("dh", "dl", "z", "core"))
    rows = P(("dh", "dl"), ("z", "core"), None)
    band = P(("z", "core"), None)
    return jax.shard_map(
        local,
        mesh=fine,
        in_specs=(rows, rows, rows, rows, band, P(), P()),
        out_specs=(rows, rows, rows, band),
        check_vma=False,
    )
```

```python
import functools

import jax
import jax.numpy as jnp
from jax import lax
from jax.experimental import pallas as pl
from jax.experimental.pallas import tpu as pltpu
from jax.sharding import Mesh
from jax.sharding import PartitionSpec as P

DH = 64
W = 128
PLANE = 4
MIB = 2**20
F32 = jnp.float32
BF16 = jnp.bfloat16


def mm(a, b):
    return jnp.dot(a, b, preferred_element_type=F32)


def mm_nt(a, b):
    return lax.dot_general(a, b, (((1,), (1,)), ((), ())), preferred_element_type=F32)


def iota(shape, axis):
    return lax.broadcasted_iota(jnp.int32, shape, axis)


def as_bf16(hit):
    return hit.astype(F32).astype(BF16)


CHUNK = 32


def shear(x, frames, row):
    return pltpu.roll(x, frames + 1 + row, 1, stride=1, stride_axis=0)


def columns(start, size):
    return pl.ds(pl.multiple_of(start, W), size)


class Masks:
    def __init__(self, frames):
        span = 2 * frames
        lane = iota((frames, W), 1)
        sub = iota((W, frames), 0)
        self.first = lane < DH
        scale = jnp.bfloat16(DH**-0.5)
        self.lanes = [as_bf16(lane < DH) * scale, as_bf16(lane >= DH) * scale]
        self.subs = [as_bf16(sub < DH), as_bf16(sub >= DH)]
        self.flip = as_bf16(iota((span, span), 0) + iota((span, span), 1) == span - 1)
        row, col = iota((frames, frames), 0), iota((frames, frames), 1)
        self.forward = col + row >= frames - 1
        self.back = [as_bf16(col > row), as_bf16(col <= row)]

    def stack(self, x):
        return jnp.concatenate([x * self.lanes[0], x * self.lanes[1]], axis=0)

    def stack_t(self, x):
        x = x.T
        return jnp.concatenate([x * self.subs[0], x * self.subs[1]], axis=1)


def operands(masks, q, g, bias_c, bias_p):
    qf = q.astype(F32)
    rows = ((qf + bias_c).astype(BF16), (qf + bias_p).astype(BF16), g)
    return [masks.stack(x) for x in rows], [masks.stack_t(x) for x in rows]


def unit(masks, stacks, turned, kw, vw, tables, products=None):
    frames = turned[0].shape[1] // 2
    band0, band1, band0_rev, band1_rev = tables
    qp_stack = stacks[1]
    if products is None:
        products = mm_nt(stacks[0], kw), mm_nt(stacks[2], vw)
    content, gw = products
    near, far = mm_nt(qp_stack, band0_rev), mm_nt(qp_stack, band1_rev)
    yield
    ds, attention_b = [], []
    for start in range(0, 2 * frames, CHUNK):
        rows, first = slice(start, start + CHUNK), start % frames
        own = masks.forward[first : first + CHUNK]
        merged = [
            jnp.where(own, near[rows, :frames], far[rows, :frames]),
            jnp.where(own, far[rows, frames:], near[rows, frames:]),
        ]
        scores = content[rows] + shear(jnp.concatenate(merged, axis=1), frames, first)
        e = jnp.exp(scores - jnp.max(scores, axis=1, keepdims=True))
        inverse = 1.0 / jnp.sum(e, axis=1, keepdims=True)
        delta = jnp.sum(e * gw[rows], axis=1, keepdims=True) * inverse
        attention = e * inverse
        attention_b.append(attention.astype(BF16))
        ds.append((attention * (gw[rows] - delta)).astype(BF16))
        yield
    ds, attention_b = jnp.concatenate(ds, axis=0), jnp.concatenate(attention_b, axis=0)
    flipped = mm(ds, masks.flip)
    dk = mm(turned[0], ds)
    dv = mm(turned[2], attention_b)
    yield
    d0, d1 = [], []
    for start in range(0, 2 * frames, CHUNK):
        first = start % frames
        placed = shear(flipped[start : start + CHUNK], frames, first).astype(BF16)
        left, right = placed[:, :frames], placed[:, frames:]
        mask = [m[first : first + CHUNK] for m in masks.back]
        d0.append(jnp.concatenate([left * mask[0], right * mask[1]], axis=1))
        d1.append(jnp.concatenate([left * mask[1], right * mask[0]], axis=1))
        yield
    d0, d1 = jnp.concatenate(d0, axis=0), jnp.concatenate(d1, axis=0)
    lhs = jnp.concatenate([ds, d0, d1], axis=1)
    rhs = jnp.concatenate([kw, band0, band1], axis=0)
    full = mm(lhs, rhs)
    dq = jnp.where(masks.first, full[:frames], full[frames:]).astype(BF16).astype(F32)
    g1 = mm(turned[1], d1)
    g_band = jnp.concatenate([mm(turned[1], d0), g1[:, frames:], g1[:, :frames]], axis=1)
    return dq, dk, dv, g_band


def side_by_side(groups):
    results = [None] * len(groups)
    left = list(enumerate(groups))
    while left:
        for n, group in list(left):
            try:
                next(group)
            except StopIteration as end:
                results[n] = end.value
                left.remove((n, group))
    return results


def call(body, name, out_shape, scratch=(), limit=8, **options):
    return pl.pallas_call(
        body,
        out_shape=out_shape,
        scratch_shapes=list(scratch),
        compiler_params=pltpu.CompilerParams(vmem_limit_bytes=limit * MIB),
        name=name,
        **options,
    )


def shape(dims, dtype):
    return jax.ShapeDtypeStruct(tuple(dims), dtype)


def pair_of():
    low = lax.axis_index("dl")
    return (low & 1) ^ (low >> 1)


def place(own, sib, scr, slot):
    core = lax.axis_index("core")
    span = scr.shape[3]
    here = columns((2 * core + (pair_of() ^ slot)) * span, span)
    for n, (a, b) in enumerate(zip(own, sib)):
        scr[n, core] = a[:, here]
        scr[n, 1 - core] = b[:, here]
    return here


def ahead_body(*refs):
    own, sib, (bias_c, bias_p) = refs[0:4], refs[4:8], refs[8:10]
    stacks, turned, rows, products, scr = refs[10:]
    frames, span = scr.shape[2:]
    masks = Masks(frames)
    for slot in range(2):
        here = place(own, sib, scr, slot)
        at_bias = bias_c[:, here], bias_p[:, here]
        for j in range(span // W):
            at = slice(j * W, (j + 1) * W)
            for b in range(2):
                if slot == 0 and b == 1:
                    continue
                which = slot + b
                made = operands(masks, scr[0, b, :, at], scr[3, b, :, at], *[x[:, at] for x in at_bias])
                for n in range(3):
                    stacks[which, j, n] = made[0][n]
                    turned[which, j, n] = made[1][n]
                k, v = scr[1, b, :, at], scr[2, b, :, at]
                if b == 0:
                    rows[which, j] = jnp.concatenate([k, v], axis=0)
                else:
                    kw = jnp.concatenate([k, scr[1, 0, :, at]], axis=0)
                    vw = jnp.concatenate([v, scr[2, 0, :, at]], axis=0)
                    rows[which, j] = kw
                    products[j, 0] = mm_nt(made[0][0], kw)
                    products[j, 1] = mm_nt(made[0][2], vw)


def ahead(own, sib, biases):
    frames, width = own[0].shape
    span = width // 4
    groups = span // W
    return call(
        ahead_body,
        "ahead",
        [
            shape((3, groups, 3, 2 * frames, W), BF16),
            shape((3, groups, 3, W, 2 * frames), BF16),
            shape((3, groups, 2 * frames, W), BF16),
            shape((groups, 2, 2 * frames, 2 * frames), F32),
        ],
        [pltpu.VMEM((4, 2, frames, span), BF16)],
        limit=16,
    )(*own, *sib, *biases)


def odd_body(steps, slot, *refs):
    count = 4 if slot else 10
    given, bands, refs = refs[:count], refs[count : count + 2], refs[count + 2 :]
    dq_out, out, carry, g_out, tables, scr, band_scr = refs
    core = lax.axis_index("core")
    frames, span = scr.shape[2:]
    share = band_scr.shape[2]
    band_scr[:, core] = bands[0][...].reshape(steps, share, span)
    band_scr[:, 1 - core] = bands[1][...].reshape(steps, share, span)
    band = band_scr[...].reshape(steps * 2 * share, span)
    masks = Masks(frames)
    band0, band1 = band[: 2 * frames], band[2 * frames :]
    band1 = jnp.concatenate([band1[frames:], band1[:frames]], axis=0)
    tables[0] = band0
    tables[1] = band1
    tables[2] = mm(masks.flip, band0).astype(BF16)
    tables[3] = mm(masks.flip, band1).astype(BF16)
    cuts = [slice(j * W, (j + 1) * W) for j in range(span // W)]
    groups = []
    if slot:
        stacks, turned, rows, products = given
        for j, at in enumerate(cuts):
            made = [[x[2, j, n] for n in range(3)] for x in (stacks, turned)]
            table = [tables[n, :, at] for n in range(4)]
            ready = products[j, 0], products[j, 1]
            groups.append(unit(masks, *made, rows[2, j], None, table, ready))
    else:
        here = place(given[0:4], given[4:8], scr, slot)
        at_bias = given[8][:, here], given[9][:, here]
        for at in cuts:
            made = operands(masks, scr[0, 1, :, at], scr[3, 1, :, at], *[x[:, at] for x in at_bias])
            window = [
                jnp.concatenate([scr[n, 1, :, at], scr[n, 0, :, at]], axis=0) for n in (1, 2)
            ]
            groups.append(unit(masks, *made, *window, [tables[n, :, at] for n in range(4)]))
    for j, (dq, dk, dv, g_band) in enumerate(side_by_side(groups)):
        at = cuts[j]
        dq_out[:, at] = dq
        for n, term in enumerate((dk, dv)):
            out[n, at] = term[:, :frames]
            carry[n, at] = term[:, frames:].astype(BF16)
        g_out[j] = g_band


def even_body(slot, *refs):
    stacks, turned, rows, _, prev, tables, carry, g_odd = refs[:8]
    dq_out, out, back, *g_outs = refs[8:]
    frames, span = dq_out.shape
    masks = Masks(frames)
    cuts = [slice(j * W, (j + 1) * W) for j in range(span // W)]
    groups = []
    for j, at in enumerate(cuts):
        mine = columns((pair_of() ^ slot) * span + j * W, W)
        made = [[x[slot, j, n] for n in range(3)] for x in (stacks, turned)]
        window = [
            jnp.concatenate([rows[slot, j, n * frames : (n + 1) * frames], prev[n, :, mine]], axis=0)
            for n in range(2)
        ]
        groups.append(unit(masks, *made, *window, [tables[n, :, at] for n in range(4)]))
    for j, (dq, dk, dv, g_band) in enumerate(side_by_side(groups)):
        at = cuts[j]
        dq_out[:, at] = dq
        for n, term in enumerate((dk, dv)):
            out[n, at] = term[:, :frames] + carry[n, at].astype(F32)
            back[n, at] = term[:, frames:].astype(BF16)
        g_outs[j][...] = (g_odd[j] + g_band).astype(g_outs[j].dtype)


def cost(groups, frames):
    return pl.CostEstimate(
        flops=2 * groups * 20 * frames * (2 * frames) ** 2,
        bytes_accessed=64 * groups * frames * W,
        transcendentals=groups * 4 * frames * frames,
    )


def odd_call(slot, given, bands, steps, frames):
    rows, span = bands[0].shape
    groups = span // W
    return call(
        functools.partial(odd_body, steps, slot),
        "odd_block",
        [
            shape((frames, span), F32),
            shape((2, span, frames), F32),
            shape((2, span, frames), BF16),
            shape((groups, W, 2 * rows), F32),
            shape((4, rows, span), BF16),
        ],
        [
            pltpu.VMEM((4, 2, frames, span), BF16),
            pltpu.VMEM((steps, 2, rows // steps, span), BF16),
        ],
        limit=16,
        cost_estimate=cost(groups, frames),
    )(*given, *bands)


def even_call(slot, given, prev, odd):
    frames = prev.shape[1]
    _, _, carry, g_odd, tables = odd
    groups, _, rows = g_odd.shape
    span = groups * W
    return call(
        functools.partial(even_body, slot),
        "even_block",
        [shape((frames, span), F32), shape((2, span, frames), F32), shape((2, span, frames), BF16)]
        + [shape((W, rows), F32 if slot else BF16)] * groups,
        limit=16,
        cost_estimate=cost(groups, frames),
    )(*given, prev, tables, carry, g_odd)


def band_cut_body(table, out):
    half = table.shape[1] // 2
    span = half // 2
    pair = pair_of()
    for n in range(2):
        out[:, n * span : (n + 1) * span] = table[:, columns(n * half + pair * span, span)]


def band_cut(table):
    rows, width = table.shape
    return call(band_cut_body, "band_cut", shape((rows, width // 2), BF16))(table)


def band_pack_body(steps, *refs):
    own, sib = refs[steps:]
    core, z = lax.axis_index("core"), lax.axis_index("z")
    span = own.shape[2]
    for n in range(steps):
        at = z ^ n
        own[at] = refs[n][:, columns(core * span, span)]
        sib[at] = refs[n][:, columns((1 - core) * span, span)]


def band_pack(parts):
    rows, width = parts[0].shape
    steps = len(parts)
    out = call(
        functools.partial(band_pack_body, steps),
        "band_pack",
        [shape((steps, rows, width // 2), BF16)] * 2,
    )(*parts)
    return [x.reshape(steps * rows, width // 2) for x in out]


def odd_rows(own, sib, half):
    mine = jnp.stack([x[:, half:] for x in own])
    other = jnp.stack([x[:, :half] for x in sib])
    return jnp.where(lax.axis_index("core") == 1, mine, other)


def summed(refs):
    total = refs[0][...].astype(F32)
    for ref in refs[1:]:
        total = total + ref[...].astype(F32)
    return total


def pair_sum_body(steps, own0, own1, from_x, from_y, *refs):
    scr = refs[-1]
    z = lax.axis_index("z")
    rows = scr.shape[2]
    for n, (a, b) in enumerate(((own0, from_x), (own1, from_y))):
        total = (a[...] + b[...].astype(F32)).astype(BF16)
        for m in range(steps):
            scr[m, n * W : (n + 1) * W] = total[:, m * rows : (m + 1) * rows]
    for m in range(steps):
        refs[m][...] = scr[z ^ m]


def pair_sum(own, received, steps):
    rows = own[0].shape[1] // steps
    return call(
        functools.partial(pair_sum_body, steps),
        "pair_sum",
        [shape((2 * W, rows), BF16)] * steps,
        [pltpu.VMEM((steps, 2 * W, rows), BF16)],
    )(*own, *received)


def z_sum_body(*refs):
    refs[-1][...] = summed(refs[:-1]).astype(BF16)


def z_sum(parts):
    return call(z_sum_body, "z_sum", shape(parts[0].shape, BF16))(*parts)


def plane_sum_body(own, diagonal, from_x, from_y, mine, other, scr):
    core, pair = lax.axis_index("core"), pair_of()
    rows, half = mine.shape
    span = half // 2
    for n, terms in enumerate(((from_x, from_y), (own, diagonal))):
        total = summed(terms).T.reshape(2, rows, span)
        scr[:, :, columns((pair ^ n) * span, span)] = total
    mine[...] = scr[core]
    other[...] = scr[1 - core]


def plane_sum(parts):
    span, rows = parts[0].shape
    half = 2 * span
    return call(
        plane_sum_body,
        "plane_sum",
        [shape((rows // 2, half), F32)] * 2,
        [pltpu.VMEM((2, rows // 2, half), F32)],
    )(*parts)


def settle_body(*refs):
    odd, even, given = refs[0:4], refs[4:8], refs[8:10]
    own, sib, back = refs[10:]
    core, pair = lax.axis_index("core"), pair_of()
    span = odd[0].shape[1]
    for slot in range(2):
        here = columns((pair ^ slot) * span, span)
        for n in range(2):
            back[n, :, here] = given[slot][n].T
        for which, (first, second) in enumerate(((own, sib), (sib, own))):

            @pl.when(core == which)
            def _():
                for target, block in ((first, even), (second, odd)):
                    target[0, :, here] = block[2 * slot][...]
                    for n in range(2):
                        target[1 + n, :, here] = block[2 * slot + 1][n].T


def settle(odd, even, back):
    frames, span = odd[0].shape
    outs = [shape((3, frames, 2 * span), F32)] * 2 + [shape((2, frames, 2 * span), BF16)]
    return call(settle_body, "settle", outs)(*odd, *even, *back)


def rows_final_body(own, sib, back, back_sib, dq, dk, dv):
    core = lax.axis_index("core")
    half = own.shape[2]
    mine, other = columns(core * half, half), columns((1 - core) * half, half)
    dq[:, mine] = own[0].astype(BF16)
    dq[:, other] = sib[0].astype(BF16)
    odd = core == 1
    for n, out in enumerate((dk, dv)):
        out[:, mine] = (own[1 + n] + jnp.where(odd, back[n].astype(F32), 0.0)).astype(BF16)
        out[:, other] = (sib[1 + n] + jnp.where(odd, back_sib[n].astype(F32), 0.0)).astype(BF16)


def rows_final(own, sib, back, back_sib):
    frames, half = back.shape[1:]
    outs = [shape((frames, 2 * half), BF16)] * 3
    return call(rows_final_body, "rows_final", outs)(own, sib, back, back_sib)


def band_final_body(mine, other, out):
    core = lax.axis_index("core")
    half = mine.shape[1]
    out[:, columns(core * half, half)] = mine[...]
    out[:, columns((1 - core) * half, half)] = other[...]


def band_final(mine, other):
    rows, half = mine.shape
    return call(band_final_body, "band_final", shape((rows, 2 * half), F32))(mine, other)


def local(query_rows, key_rows, value_rows, grad_out, pos_keys, bias_content, bias_position):
    n_high, n_z = lax.axis_size("dh"), lax.axis_size("z")
    width = query_rows.shape[2]

    def along_z(x, flip):
        return lax.ppermute(x, "z", [(s, s ^ flip) for s in range(n_z)])

    def around_z(x, steps):
        return lax.ppermute(x, "z", [(s, (s + steps) % n_z) for s in range(n_z)])

    def to_sibling(x):
        return lax.ppermute(x, "core", [(0, 1), (1, 0)])

    def in_plane(x, flip, cross=0):
        pairs = [
            (2 * d + c, 2 * (d ^ flip) + (c ^ cross)) for d in range(PLANE) for c in range(2)
        ]
        return lax.ppermute(x, ("dl", "core"), pairs)

    cut = band_cut(pos_keys)
    cuts = [cut] + [along_z(cut, k) for k in range(1, n_z)]
    own = [x[0] for x in (query_rows, key_rows, value_rows, grad_out)]
    sib = [to_sibling(x) for x in own]
    prev = around_z(odd_rows(own[1:3], sib[1:3], width // 2), 1)
    band_own, band_sib = band_pack(cuts)
    first_bands = [band_own, to_sibling(band_sib)]
    second_bands = [in_plane(band_own, 1), in_plane(band_sib, 2, 1)]
    biases = [bias_content.reshape(1, width), bias_position.reshape(1, width)]

    frames = own[0].shape[0]
    first = odd_call(0, (*own, *sib, *biases), first_bands, n_z, frames)
    *later_biases, carry = lax.optimization_barrier((*biases, first[2]))
    first = (*first[:2], carry, *first[3:])
    later = ahead(own, sib, later_biases)
    even0 = even_call(0, later, prev, first)
    received = [in_plane(even0[3], 1), in_plane(even0[4], 2)]
    *second_bands, e0 = lax.optimization_barrier((*second_bands, even0[0]))
    even0 = [e0, *even0[1:]]
    second = odd_call(1, later, second_bands, n_z, frames)
    even1 = even_call(1, later, prev, second)
    g_own = even1[3:]

    *parts, turn = lax.optimization_barrier((*pair_sum(g_own, received, n_z), even0[2]))
    parts = [along_z(parts[k], k) for k in range(n_z - 1, 0, -1)] + [parts[0]]
    odd, even = (*first[:2], *second[:2]), (*even0[:2], *even1[:2])
    out_own, out_sib, back = settle(odd, even, (turn, even1[2]))
    *parts, back, out_sib = lax.optimization_barrier((*parts, back, out_sib))
    back = around_z(back, -1)
    out_sib = to_sibling(out_sib)
    total = z_sum(parts)
    step = 1
    while step < n_high:
        pairs = [(s, s ^ step) for s in range(n_high)]
        total = z_sum([total, lax.ppermute(total, "dh", pairs)])
        step *= 2
    planes = [in_plane(total, k) for k in (3, 1, 2)]
    *planes, back = lax.optimization_barrier((*planes, back))
    back_sib = to_sibling(back)
    mine, other = plane_sum([total, *planes])
    other = to_sibling(other)
    rows = rows_final(out_own, out_sib, back, back_sib)
    *rows, mine, other = lax.optimization_barrier((*rows, mine, other))
    return *[x[None] for x in rows], band_final(mine, other)


def solution(mesh):
    n_dp, n_blk = mesh.shape["dp"], mesh.shape["blk"]
    fine = Mesh(mesh.devices.reshape(n_dp // PLANE, PLANE, n_blk // 2, 2), ("dh", "dl", "z", "core"))
    rows = P(("dh", "dl"), ("z", "core"), None)
    band = P(("z", "core"), None)
    return jax.shard_map(
        local,
        mesh=fine,
        in_specs=(rows, rows, rows, rows, band, P(), P()),
        out_specs=(rows, rows, rows, band),
        check_vma=False,
    )
```

```python
import functools

import jax
import jax.numpy as jnp
from jax import lax
from jax.experimental import pallas as pl
from jax.experimental.pallas import tpu as pltpu
from jax.sharding import Mesh
from jax.sharding import PartitionSpec as P

DH = 64
W = 128
PLANE = 4
MIB = 2**20
F32 = jnp.float32
BF16 = jnp.bfloat16


def mm(a, b):
    return jnp.dot(a, b, preferred_element_type=F32)


def mm_nt(a, b):
    return lax.dot_general(a, b, (((1,), (1,)), ((), ())), preferred_element_type=F32)


def iota(shape, axis):
    return lax.broadcasted_iota(jnp.int32, shape, axis)


def as_bf16(hit):
    return hit.astype(F32).astype(BF16)


CHUNK = 32


def shear(x, frames, row):
    return pltpu.roll(x, frames + 1 + row, 1, stride=1, stride_axis=0)


def columns(start, size):
    return pl.ds(pl.multiple_of(start, W), size)


class Masks:
    def __init__(self, frames):
        span = 2 * frames
        lane = iota((frames, W), 1)
        sub = iota((W, frames), 0)
        self.first = lane < DH
        scale = jnp.bfloat16(DH**-0.5)
        self.lanes = [as_bf16(lane < DH) * scale, as_bf16(lane >= DH) * scale]
        self.subs = [as_bf16(sub < DH), as_bf16(sub >= DH)]
        self.flip = as_bf16(iota((span, span), 0) + iota((span, span), 1) == span - 1)
        row, col = iota((frames, frames), 0), iota((frames, frames), 1)
        self.forward = col + row >= frames - 1
        self.back = [as_bf16(col > row), as_bf16(col <= row)]

    def stack(self, x):
        return jnp.concatenate([x * self.lanes[0], x * self.lanes[1]], axis=0)

    def stack_t(self, x):
        x = x.T
        return jnp.concatenate([x * self.subs[0], x * self.subs[1]], axis=1)


def operands(masks, q, g, bias_c, bias_p):
    qf = q.astype(F32)
    rows = ((qf + bias_c).astype(BF16), (qf + bias_p).astype(BF16), g)
    return [masks.stack(x) for x in rows], [masks.stack_t(x) for x in rows]


def unit(masks, stacks, turned, kw, vw, tables, products=None):
    frames = turned[0].shape[1] // 2
    band0, band1, band0_rev, band1_rev = tables
    qp_stack = stacks[1]
    if products is None:
        products = mm_nt(stacks[0], kw), mm_nt(stacks[2], vw)
    content, gw = products
    near, far = mm_nt(qp_stack, band0_rev), mm_nt(qp_stack, band1_rev)
    yield
    ds, attention_b = [], []
    for start in range(0, 2 * frames, CHUNK):
        rows, first = slice(start, start + CHUNK), start % frames
        own = masks.forward[first : first + CHUNK]
        merged = [
            jnp.where(own, near[rows, :frames], far[rows, :frames]),
            jnp.where(own, far[rows, frames:], near[rows, frames:]),
        ]
        scores = content[rows] + shear(jnp.concatenate(merged, axis=1), frames, first)
        e = jnp.exp(scores - jnp.max(scores, axis=1, keepdims=True))
        inverse = 1.0 / jnp.sum(e, axis=1, keepdims=True)
        delta = jnp.sum(e * gw[rows], axis=1, keepdims=True) * inverse
        attention = e * inverse
        attention_b.append(attention.astype(BF16))
        ds.append((attention * (gw[rows] - delta)).astype(BF16))
        yield
    ds, attention_b = jnp.concatenate(ds, axis=0), jnp.concatenate(attention_b, axis=0)
    flipped = mm(ds, masks.flip)
    dk = mm(turned[0], ds)
    dv = mm(turned[2], attention_b)
    yield
    d0, d1 = [], []
    for start in range(0, 2 * frames, CHUNK):
        first = start % frames
        placed = shear(flipped[start : start + CHUNK], frames, first).astype(BF16)
        left, right = placed[:, :frames], placed[:, frames:]
        mask = [m[first : first + CHUNK] for m in masks.back]
        d0.append(jnp.concatenate([left * mask[0], right * mask[1]], axis=1))
        d1.append(jnp.concatenate([left * mask[1], right * mask[0]], axis=1))
        yield
    d0, d1 = jnp.concatenate(d0, axis=0), jnp.concatenate(d1, axis=0)
    lhs = jnp.concatenate([ds, d0, d1], axis=1)
    rhs = jnp.concatenate([kw, band0, band1], axis=0)
    full = mm(lhs, rhs)
    dq = jnp.where(masks.first, full[:frames], full[frames:]).astype(BF16).astype(F32)
    g1 = mm(turned[1], d1)
    g_band = jnp.concatenate([mm(turned[1], d0), g1[:, frames:], g1[:, :frames]], axis=1)
    return dq, dk, dv, g_band


def side_by_side(groups):
    results = [None] * len(groups)
    left = list(enumerate(groups))
    while left:
        for n, group in list(left):
            try:
                next(group)
            except StopIteration as end:
                results[n] = end.value
                left.remove((n, group))
    return results


def call(body, name, out_shape, scratch=(), limit=8, **options):
    return pl.pallas_call(
        body,
        out_shape=out_shape,
        scratch_shapes=list(scratch),
        compiler_params=pltpu.CompilerParams(vmem_limit_bytes=limit * MIB),
        name=name,
        **options,
    )


def shape(dims, dtype):
    return jax.ShapeDtypeStruct(tuple(dims), dtype)


def pair_of():
    low = lax.axis_index("dl")
    return (low & 1) ^ (low >> 1)


def place(own, sib, scr, slot):
    core = lax.axis_index("core")
    span = scr.shape[3]
    here = columns((2 * core + (pair_of() ^ slot)) * span, span)
    for n, (a, b) in enumerate(zip(own, sib)):
        scr[n, core] = a[:, here]
        scr[n, 1 - core] = b[:, here]
    return here


def ahead_body(*refs):
    own, sib, (bias_c, bias_p) = refs[0:4], refs[4:8], refs[8:10]
    stacks, turned, rows, products, scr = refs[10:]
    frames, span = scr.shape[2:]
    masks = Masks(frames)
    for slot in range(2):
        here = place(own, sib, scr, slot)
        at_bias = bias_c[:, here], bias_p[:, here]
        for j in range(span // W):
            at = slice(j * W, (j + 1) * W)
            for b in range(2):
                if slot == 0 and b == 1:
                    continue
                which = slot + b
                made = operands(masks, scr[0, b, :, at], scr[3, b, :, at], *[x[:, at] for x in at_bias])
                for n in range(3):
                    stacks[which, j, n] = made[0][n]
                    turned[which, j, n] = made[1][n]
                k, v = scr[1, b, :, at], scr[2, b, :, at]
                if b == 0:
                    rows[which, j] = jnp.concatenate([k, v], axis=0)
                else:
                    kw = jnp.concatenate([k, scr[1, 0, :, at]], axis=0)
                    vw = jnp.concatenate([v, scr[2, 0, :, at]], axis=0)
                    rows[which, j] = kw
                    products[j, 0] = mm_nt(made[0][0], kw)
                    products[j, 1] = mm_nt(made[0][2], vw)


def ahead(own, sib, biases):
    frames, width = own[0].shape
    span = width // 4
    groups = span // W
    return call(
        ahead_body,
        "ahead",
        [
            shape((3, groups, 3, 2 * frames, W), BF16),
            shape((3, groups, 3, W, 2 * frames), BF16),
            shape((3, groups, 2 * frames, W), BF16),
            shape((groups, 2, 2 * frames, 2 * frames), F32),
        ],
        [pltpu.VMEM((4, 2, frames, span), BF16)],
        limit=16,
    )(*own, *sib, *biases)


def odd_body(steps, slot, *refs):
    count = 4 if slot else 10
    given, bands, refs = refs[:count], refs[count : count + 2], refs[count + 2 :]
    dq_out, out, carry, g_out, tables, scr, band_scr = refs
    core = lax.axis_index("core")
    frames, span = scr.shape[2:]
    share = band_scr.shape[2]
    band_scr[:, core] = bands[0][...].reshape(steps, share, span)
    band_scr[:, 1 - core] = bands[1][...].reshape(steps, share, span)
    band = band_scr[...].reshape(steps * 2 * share, span)
    masks = Masks(frames)
    band0, band1 = band[: 2 * frames], band[2 * frames :]
    band1 = jnp.concatenate([band1[frames:], band1[:frames]], axis=0)
    tables[0] = band0
    tables[1] = band1
    tables[2] = mm(masks.flip, band0).astype(BF16)
    tables[3] = mm(masks.flip, band1).astype(BF16)
    cuts = [slice(j * W, (j + 1) * W) for j in range(span // W)]
    groups = []
    if slot:
        stacks, turned, rows, products = given
        for j, at in enumerate(cuts):
            made = [[x[2, j, n] for n in range(3)] for x in (stacks, turned)]
            table = [tables[n, :, at] for n in range(4)]
            ready = products[j, 0], products[j, 1]
            groups.append(unit(masks, *made, rows[2, j], None, table, ready))
    else:
        here = place(given[0:4], given[4:8], scr, slot)
        at_bias = given[8][:, here], given[9][:, here]
        for at in cuts:
            made = operands(masks, scr[0, 1, :, at], scr[3, 1, :, at], *[x[:, at] for x in at_bias])
            window = [
                jnp.concatenate([scr[n, 1, :, at], scr[n, 0, :, at]], axis=0) for n in (1, 2)
            ]
            groups.append(unit(masks, *made, *window, [tables[n, :, at] for n in range(4)]))
    for j, (dq, dk, dv, g_band) in enumerate(side_by_side(groups)):
        at = cuts[j]
        dq_out[:, at] = dq
        for n, term in enumerate((dk, dv)):
            out[n, at] = term[:, :frames]
            carry[n, at] = term[:, frames:].astype(BF16)
        g_out[j] = g_band


def even_body(slot, *refs):
    stacks, turned, rows, _, prev, tables, carry, g_odd = refs[:8]
    dq_out, out, back, *g_outs = refs[8:]
    frames, span = dq_out.shape
    masks = Masks(frames)
    cuts = [slice(j * W, (j + 1) * W) for j in range(span // W)]
    groups = []
    for j, at in enumerate(cuts):
        mine = columns((pair_of() ^ slot) * span + j * W, W)
        made = [[x[slot, j, n] for n in range(3)] for x in (stacks, turned)]
        window = [
            jnp.concatenate([rows[slot, j, n * frames : (n + 1) * frames], prev[n, :, mine]], axis=0)
            for n in range(2)
        ]
        groups.append(unit(masks, *made, *window, [tables[n, :, at] for n in range(4)]))
    for j, (dq, dk, dv, g_band) in enumerate(side_by_side(groups)):
        at = cuts[j]
        dq_out[:, at] = dq
        for n, term in enumerate((dk, dv)):
            out[n, at] = term[:, :frames] + carry[n, at].astype(F32)
            back[n, at] = term[:, frames:].astype(BF16)
        g_outs[j][...] = (g_odd[j] + g_band).astype(g_outs[j].dtype)


def cost(groups, frames):
    return pl.CostEstimate(
        flops=2 * groups * 20 * frames * (2 * frames) ** 2,
        bytes_accessed=64 * groups * frames * W,
        transcendentals=groups * 4 * frames * frames,
    )


def odd_call(slot, given, bands, steps, frames):
    rows, span = bands[0].shape
    groups = span // W
    return call(
        functools.partial(odd_body, steps, slot),
        "odd_block",
        [
            shape((frames, span), F32),
            shape((2, span, frames), F32),
            shape((2, span, frames), BF16),
            shape((groups, W, 2 * rows), F32),
            shape((4, rows, span), BF16),
        ],
        [
            pltpu.VMEM((4, 2, frames, span), BF16),
            pltpu.VMEM((steps, 2, rows // steps, span), BF16),
        ],
        limit=16,
        cost_estimate=cost(groups, frames),
    )(*given, *bands)


def even_call(slot, given, prev, odd):
    frames = prev.shape[1]
    _, _, carry, g_odd, tables = odd
    groups, _, rows = g_odd.shape
    span = groups * W
    return call(
        functools.partial(even_body, slot),
        "even_block",
        [shape((frames, span), F32), shape((2, span, frames), F32), shape((2, span, frames), BF16)]
        + [shape((W, rows), F32 if slot else BF16)] * groups,
        limit=16,
        cost_estimate=cost(groups, frames),
    )(*given, prev, tables, carry, g_odd)


def band_cut_body(table, out):
    half = table.shape[1] // 2
    span = half // 2
    pair = pair_of()
    for n in range(2):
        out[:, n * span : (n + 1) * span] = table[:, columns(n * half + pair * span, span)]


def band_cut(table):
    rows, width = table.shape
    return call(band_cut_body, "band_cut", shape((rows, width // 2), BF16))(table)


def band_pack_body(steps, *refs):
    own, sib = refs[steps:]
    core, z = lax.axis_index("core"), lax.axis_index("z")
    span = own.shape[2]
    for n in range(steps):
        at = z ^ n
        own[at] = refs[n][:, columns(core * span, span)]
        sib[at] = refs[n][:, columns((1 - core) * span, span)]


def band_pack(parts):
    rows, width = parts[0].shape
    steps = len(parts)
    out = call(
        functools.partial(band_pack_body, steps),
        "band_pack",
        [shape((steps, rows, width // 2), BF16)] * 2,
    )(*parts)
    return [x.reshape(steps * rows, width // 2) for x in out]


def odd_rows(own, sib, half):
    mine = jnp.stack([x[:, half:] for x in own])
    other = jnp.stack([x[:, :half] for x in sib])
    return jnp.where(lax.axis_index("core") == 1, mine, other)


def summed(refs):
    total = refs[0][...].astype(F32)
    for ref in refs[1:]:
        total = total + ref[...].astype(F32)
    return total


def pair_sum_body(steps, own0, own1, from_x, from_y, *refs):
    scr = refs[-1]
    z = lax.axis_index("z")
    rows = scr.shape[2]
    for n, (a, b) in enumerate(((own0, from_x), (own1, from_y))):
        total = (a[...] + b[...].astype(F32)).astype(BF16)
        for m in range(steps):
            scr[m, n * W : (n + 1) * W] = total[:, m * rows : (m + 1) * rows]
    for m in range(steps):
        refs[m][...] = scr[z ^ m]


def pair_sum(own, received, steps):
    rows = own[0].shape[1] // steps
    return call(
        functools.partial(pair_sum_body, steps),
        "pair_sum",
        [shape((2 * W, rows), BF16)] * steps,
        [pltpu.VMEM((steps, 2 * W, rows), BF16)],
    )(*own, *received)


def z_sum_body(*refs):
    refs[-1][...] = summed(refs[:-1]).astype(BF16)


def z_sum(parts):
    return call(z_sum_body, "z_sum", shape(parts[0].shape, BF16))(*parts)


def plane_sum_body(own, diagonal, from_x, from_y, mine, other, scr):
    core, pair = lax.axis_index("core"), pair_of()
    rows, half = mine.shape
    span = half // 2
    for n, terms in enumerate(((from_x, from_y), (own, diagonal))):
        total = summed(terms).T.reshape(2, rows, span)
        scr[:, :, columns((pair ^ n) * span, span)] = total
    mine[...] = scr[core]
    other[...] = scr[1 - core]


def plane_sum(parts):
    span, rows = parts[0].shape
    half = 2 * span
    return call(
        plane_sum_body,
        "plane_sum",
        [shape((rows // 2, half), F32)] * 2,
        [pltpu.VMEM((2, rows // 2, half), F32)],
    )(*parts)


def settle_body(*refs):
    odd, even, given = refs[0:4], refs[4:8], refs[8:10]
    own, sib, back = refs[10:]
    core, pair = lax.axis_index("core"), pair_of()
    span = odd[0].shape[1]
    for slot in range(2):
        here = columns((pair ^ slot) * span, span)
        for n in range(2):
            back[n, :, here] = given[slot][n].T
        for which, (first, second) in enumerate(((own, sib), (sib, own))):

            @pl.when(core == which)
            def _():
                for target, block in ((first, even), (second, odd)):
                    target[0, :, here] = block[2 * slot][...]
                    for n in range(2):
                        target[1 + n, :, here] = block[2 * slot + 1][n].T


def settle(odd, even, back):
    frames, span = odd[0].shape
    outs = [shape((3, frames, 2 * span), F32)] * 2 + [shape((2, frames, 2 * span), BF16)]
    return call(settle_body, "settle", outs)(*odd, *even, *back)


def final_body(own, sib, back, back_sib, band_mine, band_other, dq, dk, dv, band):
    core = lax.axis_index("core")
    half = own.shape[2]
    mine, other = columns(core * half, half), columns((1 - core) * half, half)
    band[:, mine] = band_mine[...]
    band[:, other] = band_other[...]
    dq[:, mine] = own[0].astype(BF16)
    dq[:, other] = sib[0].astype(BF16)
    odd = core == 1
    for n, out in enumerate((dk, dv)):
        out[:, mine] = (own[1 + n] + jnp.where(odd, back[n].astype(F32), 0.0)).astype(BF16)
        out[:, other] = (sib[1 + n] + jnp.where(odd, back_sib[n].astype(F32), 0.0)).astype(BF16)


def final(own, sib, back, back_sib, mine, other):
    frames, half = back.shape[1:]
    outs = [shape((frames, 2 * half), BF16)] * 3 + [shape((mine.shape[0], 2 * half), F32)]
    return call(final_body, "final", outs)(own, sib, back, back_sib, mine, other)


def local(query_rows, key_rows, value_rows, grad_out, pos_keys, bias_content, bias_position):
    n_high, n_z = lax.axis_size("dh"), lax.axis_size("z")
    width = query_rows.shape[2]

    def along_z(x, flip):
        return lax.ppermute(x, "z", [(s, s ^ flip) for s in range(n_z)])

    def around_z(x, steps):
        return lax.ppermute(x, "z", [(s, (s + steps) % n_z) for s in range(n_z)])

    def to_sibling(x):
        return lax.ppermute(x, "core", [(0, 1), (1, 0)])

    def in_plane(x, flip, cross=0):
        pairs = [
            (2 * d + c, 2 * (d ^ flip) + (c ^ cross)) for d in range(PLANE) for c in range(2)
        ]
        return lax.ppermute(x, ("dl", "core"), pairs)

    cut = band_cut(pos_keys)
    cuts = [cut] + [along_z(cut, k) for k in range(1, n_z)]
    own = [x[0] for x in (query_rows, key_rows, value_rows, grad_out)]
    sib = [to_sibling(x) for x in own]
    prev = around_z(odd_rows(own[1:3], sib[1:3], width // 2), 1)
    band_own, band_sib = band_pack(cuts)
    first_bands = [band_own, to_sibling(band_sib)]
    second_bands = [in_plane(band_own, 1), in_plane(band_sib, 2, 1)]
    biases = [bias_content.reshape(1, width), bias_position.reshape(1, width)]

    frames = own[0].shape[0]
    first = odd_call(0, (*own, *sib, *biases), first_bands, n_z, frames)
    *later_biases, carry = lax.optimization_barrier((*biases, first[2]))
    first = (*first[:2], carry, *first[3:])
    later = ahead(own, sib, later_biases)
    second = odd_call(1, later, second_bands, n_z, frames)
    first, second = lax.optimization_barrier((first, second))
    even0 = even_call(0, later, prev, first)
    received = [in_plane(even0[3], 1), in_plane(even0[4], 2)]
    even1 = even_call(1, later, prev, second)
    g_own = even1[3:]

    *parts, turn = lax.optimization_barrier((*pair_sum(g_own, received, n_z), even0[2]))
    parts = [along_z(parts[k], k) for k in range(n_z - 1, 0, -1)] + [parts[0]]
    odd, even = (*first[:2], *second[:2]), (*even0[:2], *even1[:2])
    out_own, out_sib, back = settle(odd, even, (turn, even1[2]))
    *parts, back, out_sib = lax.optimization_barrier((*parts, back, out_sib))
    back = around_z(back, -1)
    out_sib = to_sibling(out_sib)
    total = z_sum(parts)
    step = 1
    while step < n_high:
        pairs = [(s, s ^ step) for s in range(n_high)]
        total = z_sum([total, lax.ppermute(total, "dh", pairs)])
        step *= 2
    planes = [in_plane(total, k) for k in (3, 1, 2)]
    *planes, back = lax.optimization_barrier((*planes, back))
    back_sib = to_sibling(back)
    mine, other = plane_sum([total, *planes])
    other = to_sibling(other)
    *rows, grad_pos = final(out_own, out_sib, back, back_sib, mine, other)
    return *[x[None] for x in rows], grad_pos


def solution(mesh):
    n_dp, n_blk = mesh.shape["dp"], mesh.shape["blk"]
    fine = Mesh(mesh.devices.reshape(n_dp // PLANE, PLANE, n_blk // 2, 2), ("dh", "dl", "z", "core"))
    rows = P(("dh", "dl"), ("z", "core"), None)
    band = P(("z", "core"), None)
    return jax.shard_map(
        local,
        mesh=fine,
        in_specs=(rows, rows, rows, rows, band, P(), P()),
        out_specs=(rows, rows, rows, band),
        check_vma=False,
    )
```

```python
import functools

import jax
import jax.numpy as jnp
from jax import lax
from jax.experimental import pallas as pl
from jax.experimental.pallas import tpu as pltpu
from jax.sharding import Mesh
from jax.sharding import PartitionSpec as P

DH = 64
W = 128
PLANE = 4
MIB = 2**20
F32 = jnp.float32
BF16 = jnp.bfloat16


def mm(a, b):
    return jnp.dot(a, b, preferred_element_type=F32)


def mm_nt(a, b):
    return lax.dot_general(a, b, (((1,), (1,)), ((), ())), preferred_element_type=F32)


def iota(shape, axis):
    return lax.broadcasted_iota(jnp.int32, shape, axis)


def as_bf16(hit):
    return hit.astype(F32).astype(BF16)


CHUNK = 32


def shear(x, frames, row):
    return pltpu.roll(x, frames + 1 + row, 1, stride=1, stride_axis=0)


def columns(start, size):
    return pl.ds(pl.multiple_of(start, W), size)


class Masks:
    def __init__(self, frames):
        span = 2 * frames
        lane = iota((frames, W), 1)
        sub = iota((W, frames), 0)
        self.first = lane < DH
        scale = jnp.bfloat16(DH**-0.5)
        self.lanes = [as_bf16(lane < DH) * scale, as_bf16(lane >= DH) * scale]
        self.subs = [as_bf16(sub < DH), as_bf16(sub >= DH)]
        self.flip = as_bf16(iota((span, span), 0) + iota((span, span), 1) == span - 1)
        row, col = iota((frames, frames), 0), iota((frames, frames), 1)
        self.forward = col + row >= frames - 1
        self.back = [as_bf16(col > row), as_bf16(col <= row)]

    def stack(self, x):
        return jnp.concatenate([x * self.lanes[0], x * self.lanes[1]], axis=0)

    def stack_t(self, x):
        x = x.T
        return jnp.concatenate([x * self.subs[0], x * self.subs[1]], axis=1)


def operands(masks, q, g, bias_c, bias_p):
    qf = q.astype(F32)
    rows = ((qf + bias_c).astype(BF16), (qf + bias_p).astype(BF16), g)
    return [masks.stack(x) for x in rows], [masks.stack_t(x) for x in rows]


def unit(masks, stacks, turned, kw, vw, tables, products=None):
    frames = turned[0].shape[1] // 2
    band0, band1, band0_rev, band1_rev = tables
    qp_stack = stacks[1]
    if products is None:
        products = mm_nt(stacks[0], kw), mm_nt(stacks[2], vw)
    content, gw = products
    near, far = mm_nt(qp_stack, band0_rev), mm_nt(qp_stack, band1_rev)
    yield
    ds, attention_b = [], []
    for start in range(0, 2 * frames, CHUNK):
        rows, first = slice(start, start + CHUNK), start % frames
        own = masks.forward[first : first + CHUNK]
        merged = [
            jnp.where(own, near[rows, :frames], far[rows, :frames]),
            jnp.where(own, far[rows, frames:], near[rows, frames:]),
        ]
        scores = content[rows] + shear(jnp.concatenate(merged, axis=1), frames, first)
        e = jnp.exp(scores - jnp.max(scores, axis=1, keepdims=True))
        inverse = 1.0 / jnp.sum(e, axis=1, keepdims=True)
        delta = jnp.sum(e * gw[rows], axis=1, keepdims=True) * inverse
        attention = e * inverse
        attention_b.append(attention.astype(BF16))
        ds.append((attention * (gw[rows] - delta)).astype(BF16))
        yield
    ds, attention_b = jnp.concatenate(ds, axis=0), jnp.concatenate(attention_b, axis=0)
    flipped = mm(ds, masks.flip)
    dk = mm(turned[0], ds)
    dv = mm(turned[2], attention_b)
    yield
    d0, d1 = [], []
    for start in range(0, 2 * frames, CHUNK):
        first = start % frames
        placed = shear(flipped[start : start + CHUNK], frames, first).astype(BF16)
        left, right = placed[:, :frames], placed[:, frames:]
        mask = [m[first : first + CHUNK] for m in masks.back]
        d0.append(jnp.concatenate([left * mask[0], right * mask[1]], axis=1))
        d1.append(jnp.concatenate([left * mask[1], right * mask[0]], axis=1))
        yield
    d0, d1 = jnp.concatenate(d0, axis=0), jnp.concatenate(d1, axis=0)
    lhs = jnp.concatenate([ds, d0, d1], axis=1)
    rhs = jnp.concatenate([kw, band0, band1], axis=0)
    full = mm(lhs, rhs)
    dq = jnp.where(masks.first, full[:frames], full[frames:]).astype(BF16).astype(F32)
    g1 = mm(turned[1], d1)
    g_band = jnp.concatenate([mm(turned[1], d0), g1[:, frames:], g1[:, :frames]], axis=1)
    return dq, dk, dv, g_band


def side_by_side(groups):
    results = [None] * len(groups)
    left = list(enumerate(groups))
    while left:
        for n, group in list(left):
            try:
                next(group)
            except StopIteration as end:
                results[n] = end.value
                left.remove((n, group))
    return results


def call(body, name, out_shape, scratch=(), limit=8, **options):
    return pl.pallas_call(
        body,
        out_shape=out_shape,
        scratch_shapes=list(scratch),
        compiler_params=pltpu.CompilerParams(vmem_limit_bytes=limit * MIB),
        name=name,
        **options,
    )


def shape(dims, dtype):
    return jax.ShapeDtypeStruct(tuple(dims), dtype)


def pair_of():
    low = lax.axis_index("dl")
    return (low & 1) ^ (low >> 1)


def place(own, sib, scr, slot):
    core = lax.axis_index("core")
    span = scr.shape[3]
    here = columns((2 * core + (pair_of() ^ slot)) * span, span)
    for n, (a, b) in enumerate(zip(own, sib)):
        scr[n, core] = a[:, here]
        scr[n, 1 - core] = b[:, here]
    return here


def ahead_body(*refs):
    own, sib, (bias_c, bias_p) = refs[0:4], refs[4:8], refs[8:10]
    stacks, turned, rows, products, scr = refs[10:]
    frames, span = scr.shape[2:]
    masks = Masks(frames)
    for slot in range(2):
        here = place(own, sib, scr, slot)
        at_bias = bias_c[:, here], bias_p[:, here]
        for j in range(span // W):
            at = slice(j * W, (j + 1) * W)
            for b in range(2):
                if slot == 0 and b == 1:
                    continue
                which = slot + b
                made = operands(masks, scr[0, b, :, at], scr[3, b, :, at], *[x[:, at] for x in at_bias])
                for n in range(3):
                    stacks[which, j, n] = made[0][n]
                    turned[which, j, n] = made[1][n]
                k, v = scr[1, b, :, at], scr[2, b, :, at]
                if b == 0:
                    rows[which, j] = jnp.concatenate([k, v], axis=0)
                else:
                    kw = jnp.concatenate([k, scr[1, 0, :, at]], axis=0)
                    vw = jnp.concatenate([v, scr[2, 0, :, at]], axis=0)
                    rows[which, j] = kw
                    products[j, 0] = mm_nt(made[0][0], kw)
                    products[j, 1] = mm_nt(made[0][2], vw)


def ahead(own, sib, biases):
    frames, width = own[0].shape
    span = width // 4
    groups = span // W
    return call(
        ahead_body,
        "ahead",
        [
            shape((3, groups, 3, 2 * frames, W), BF16),
            shape((3, groups, 3, W, 2 * frames), BF16),
            shape((3, groups, 2 * frames, W), BF16),
            shape((groups, 2, 2 * frames, 2 * frames), F32),
        ],
        [pltpu.VMEM((4, 2, frames, span), BF16)],
        limit=16,
    )(*own, *sib, *biases)


def odd_body(steps, slot, *refs):
    count = 4 if slot else 10
    given, bands, refs = refs[:count], refs[count : count + 2], refs[count + 2 :]
    dq_out, out, carry, g_out, tables, scr, band_scr = refs
    core = lax.axis_index("core")
    frames, span = scr.shape[2:]
    share = band_scr.shape[2]
    band_scr[:, core] = bands[0][...].reshape(steps, share, span)
    band_scr[:, 1 - core] = bands[1][...].reshape(steps, share, span)
    band = band_scr[...].reshape(steps * 2 * share, span)
    masks = Masks(frames)
    band0, band1 = band[: 2 * frames], band[2 * frames :]
    band1 = jnp.concatenate([band1[frames:], band1[:frames]], axis=0)
    tables[0] = band0
    tables[1] = band1
    tables[2] = mm(masks.flip, band0).astype(BF16)
    tables[3] = mm(masks.flip, band1).astype(BF16)
    cuts = [slice(j * W, (j + 1) * W) for j in range(span // W)]
    groups = []
    if slot:
        stacks, turned, rows, products = given
        for j, at in enumerate(cuts):
            made = [[x[2, j, n] for n in range(3)] for x in (stacks, turned)]
            table = [tables[n, :, at] for n in range(4)]
            ready = products[j, 0], products[j, 1]
            groups.append(unit(masks, *made, rows[2, j], None, table, ready))
    else:
        here = place(given[0:4], given[4:8], scr, slot)
        at_bias = given[8][:, here], given[9][:, here]
        for at in cuts:
            made = operands(masks, scr[0, 1, :, at], scr[3, 1, :, at], *[x[:, at] for x in at_bias])
            window = [
                jnp.concatenate([scr[n, 1, :, at], scr[n, 0, :, at]], axis=0) for n in (1, 2)
            ]
            groups.append(unit(masks, *made, *window, [tables[n, :, at] for n in range(4)]))
    for j, (dq, dk, dv, g_band) in enumerate(side_by_side(groups)):
        at = cuts[j]
        dq_out[:, at] = dq
        for n, term in enumerate((dk, dv)):
            out[n, at] = term[:, :frames]
            carry[n, at] = term[:, frames:].astype(BF16)
        g_out[j] = g_band


def even_body(slot, *refs):
    stacks, turned, rows, _, prev, tables, carry, g_odd = refs[:8]
    dq_out, out, back, *g_outs = refs[8:]
    frames, span = dq_out.shape
    masks = Masks(frames)
    cuts = [slice(j * W, (j + 1) * W) for j in range(span // W)]
    groups = []
    for j, at in enumerate(cuts):
        mine = columns((pair_of() ^ slot) * span + j * W, W)
        made = [[x[slot, j, n] for n in range(3)] for x in (stacks, turned)]
        window = [
            jnp.concatenate([rows[slot, j, n * frames : (n + 1) * frames], prev[n, :, mine]], axis=0)
            for n in range(2)
        ]
        groups.append(unit(masks, *made, *window, [tables[n, :, at] for n in range(4)]))
    for j, (dq, dk, dv, g_band) in enumerate(side_by_side(groups)):
        at = cuts[j]
        dq_out[:, at] = dq
        for n, term in enumerate((dk, dv)):
            out[n, at] = term[:, :frames] + carry[n, at].astype(F32)
            back[n, at] = term[:, frames:].astype(BF16)
        g_outs[j][...] = (g_odd[j] + g_band).astype(g_outs[j].dtype)


def cost(groups, frames):
    return pl.CostEstimate(
        flops=2 * groups * 20 * frames * (2 * frames) ** 2,
        bytes_accessed=64 * groups * frames * W,
        transcendentals=groups * 4 * frames * frames,
    )


def odd_call(slot, given, bands, steps, frames):
    rows, span = bands[0].shape
    groups = span // W
    return call(
        functools.partial(odd_body, steps, slot),
        "odd_block",
        [
            shape((frames, span), F32),
            shape((2, span, frames), F32),
            shape((2, span, frames), BF16),
            shape((groups, W, 2 * rows), F32),
            shape((4, rows, span), BF16),
        ],
        [
            pltpu.VMEM((4, 2, frames, span), BF16),
            pltpu.VMEM((steps, 2, rows // steps, span), BF16),
        ],
        limit=16,
        cost_estimate=cost(groups, frames),
    )(*given, *bands)


def even_call(slot, given, prev, odd):
    frames = prev.shape[1]
    _, _, carry, g_odd, tables = odd
    groups, _, rows = g_odd.shape
    span = groups * W
    return call(
        functools.partial(even_body, slot),
        "even_block",
        [shape((frames, span), F32), shape((2, span, frames), F32), shape((2, span, frames), BF16)]
        + [shape((W, rows), F32 if slot else BF16)] * groups,
        limit=16,
        cost_estimate=cost(groups, frames),
    )(*given, prev, tables, carry, g_odd)


def band_cut_body(table, out):
    half = table.shape[1] // 2
    span = half // 2
    pair = pair_of()
    for n in range(2):
        out[:, n * span : (n + 1) * span] = table[:, columns(n * half + pair * span, span)]


def band_cut(table):
    rows, width = table.shape
    return call(band_cut_body, "band_cut", shape((rows, width // 2), BF16))(table)


def band_pack_body(steps, *refs):
    own, sib = refs[steps:]
    core, z = lax.axis_index("core"), lax.axis_index("z")
    span = own.shape[2]
    for n in range(steps):
        at = z ^ n
        own[at] = refs[n][:, columns(core * span, span)]
        sib[at] = refs[n][:, columns((1 - core) * span, span)]


def band_pack(parts):
    rows, width = parts[0].shape
    steps = len(parts)
    out = call(
        functools.partial(band_pack_body, steps),
        "band_pack",
        [shape((steps, rows, width // 2), BF16)] * 2,
    )(*parts)
    return [x.reshape(steps * rows, width // 2) for x in out]


def odd_rows(own, sib, half):
    mine = jnp.stack([x[:, half:] for x in own])
    other = jnp.stack([x[:, :half] for x in sib])
    return jnp.where(lax.axis_index("core") == 1, mine, other)


def summed(refs):
    total = refs[0][...].astype(F32)
    for ref in refs[1:]:
        total = total + ref[...].astype(F32)
    return total


def pair_sum_body(steps, own0, own1, from_x, from_y, *refs):
    scr = refs[-1]
    z = lax.axis_index("z")
    rows = scr.shape[2]
    for n, (a, b) in enumerate(((own0, from_x), (own1, from_y))):
        total = (a[...] + b[...].astype(F32)).astype(BF16)
        for m in range(steps):
            scr[m, n * W : (n + 1) * W] = total[:, m * rows : (m + 1) * rows]
    for m in range(steps):
        refs[m][...] = scr[z ^ m]


def pair_sum(own, received, steps):
    rows = own[0].shape[1] // steps
    return call(
        functools.partial(pair_sum_body, steps),
        "pair_sum",
        [shape((2 * W, rows), BF16)] * steps,
        [pltpu.VMEM((steps, 2 * W, rows), BF16)],
    )(*own, *received)


def z_sum_body(*refs):
    refs[-1][...] = summed(refs[:-1]).astype(BF16)


def z_sum(parts):
    return call(z_sum_body, "z_sum", shape(parts[0].shape, BF16))(*parts)


def plane_sum_body(own, diagonal, from_x, from_y, mine, other, scr):
    core, pair = lax.axis_index("core"), pair_of()
    rows, half = mine.shape
    span = half // 2
    for n, terms in enumerate(((from_x, from_y), (own, diagonal))):
        total = summed(terms).T.reshape(2, rows, span)
        scr[:, :, columns((pair ^ n) * span, span)] = total
    mine[...] = scr[core]
    other[...] = scr[1 - core]


def plane_sum(parts):
    span, rows = parts[0].shape
    half = 2 * span
    return call(
        plane_sum_body,
        "plane_sum",
        [shape((rows // 2, half), F32)] * 2,
        [pltpu.VMEM((2, rows // 2, half), F32)],
    )(*parts)


def settle_body(*refs):
    odd, even, given = refs[0:4], refs[4:8], refs[8:10]
    own, sib, back = refs[10:]
    core, pair = lax.axis_index("core"), pair_of()
    span = odd[0].shape[1]
    for slot in range(2):
        here = columns((pair ^ slot) * span, span)
        for n in range(2):
            back[n, :, here] = given[slot][n].T
        for which, (first, second) in enumerate(((own, sib), (sib, own))):

            @pl.when(core == which)
            def _():
                for target, block in ((first, even), (second, odd)):
                    target[0, :, here] = block[2 * slot][...]
                    for n in range(2):
                        target[1 + n, :, here] = block[2 * slot + 1][n].T


def settle(odd, even, back):
    frames, span = odd[0].shape
    outs = [shape((3, frames, 2 * span), F32)] * 2 + [shape((2, frames, 2 * span), BF16)]
    return call(settle_body, "settle", outs)(*odd, *even, *back)


def final_body(own, sib, back, back_sib, band_mine, band_other, dq, dk, dv, band):
    core = lax.axis_index("core")
    half = own.shape[2]
    mine, other = columns(core * half, half), columns((1 - core) * half, half)
    band[:, mine] = band_mine[...]
    band[:, other] = band_other[...]
    dq[:, mine] = own[0].astype(BF16)
    dq[:, other] = sib[0].astype(BF16)
    odd = core == 1
    for n, out in enumerate((dk, dv)):
        out[:, mine] = (own[1 + n] + jnp.where(odd, back[n].astype(F32), 0.0)).astype(BF16)
        out[:, other] = (sib[1 + n] + jnp.where(odd, back_sib[n].astype(F32), 0.0)).astype(BF16)


def final(own, sib, back, back_sib, mine, other):
    frames, half = back.shape[1:]
    outs = [shape((frames, 2 * half), BF16)] * 3 + [shape((mine.shape[0], 2 * half), F32)]
    return call(final_body, "final", outs)(own, sib, back, back_sib, mine, other)


def local(query_rows, key_rows, value_rows, grad_out, pos_keys, bias_content, bias_position):
    n_high, n_z = lax.axis_size("dh"), lax.axis_size("z")
    width = query_rows.shape[2]

    def along_z(x, flip):
        return lax.ppermute(x, "z", [(s, s ^ flip) for s in range(n_z)])

    def around_z(x, steps):
        return lax.ppermute(x, "z", [(s, (s + steps) % n_z) for s in range(n_z)])

    def to_sibling(x):
        return lax.ppermute(x, "core", [(0, 1), (1, 0)])

    def in_plane(x, flip, cross=0):
        pairs = [
            (2 * d + c, 2 * (d ^ flip) + (c ^ cross)) for d in range(PLANE) for c in range(2)
        ]
        return lax.ppermute(x, ("dl", "core"), pairs)

    cut = band_cut(pos_keys)
    cuts = [cut] + [along_z(cut, k) for k in range(1, n_z)]
    own = [x[0] for x in (query_rows, key_rows, value_rows, grad_out)]
    sib = [to_sibling(x) for x in own]
    moved = odd_rows(own[1:3], sib[1:3], width // 2)
    cuts[1], moved = lax.optimization_barrier((cuts[1], moved))
    prev = around_z(moved, 1)
    band_own, band_sib = band_pack(cuts)
    first_bands = [band_own, to_sibling(band_sib)]
    second_bands = [in_plane(band_own, 1), in_plane(band_sib, 2, 1)]
    biases = [bias_content.reshape(1, width), bias_position.reshape(1, width)]

    frames = own[0].shape[0]
    first = odd_call(0, (*own, *sib, *biases), first_bands, n_z, frames)
    *later_biases, carry = lax.optimization_barrier((*biases, first[2]))
    first = (*first[:2], carry, *first[3:])
    later = ahead(own, sib, later_biases)
    second = odd_call(1, later, second_bands, n_z, frames)
    first, second = lax.optimization_barrier((first, second))
    even0 = even_call(0, later, prev, first)
    received = [in_plane(even0[3], 1), in_plane(even0[4], 2)]
    even1 = even_call(1, later, prev, second)
    g_own = even1[3:]

    *parts, turn = lax.optimization_barrier((*pair_sum(g_own, received, n_z), even0[2]))
    parts = [along_z(parts[k], k) for k in range(n_z - 1, 0, -1)] + [parts[0]]
    odd, even = (*first[:2], *second[:2]), (*even0[:2], *even1[:2])
    out_own, out_sib, back = settle(odd, even, (turn, even1[2]))
    *parts, back, out_sib = lax.optimization_barrier((*parts, back, out_sib))
    back = around_z(back, -1)
    out_sib = to_sibling(out_sib)
    total = z_sum(parts)
    step = 1
    while step < n_high:
        pairs = [(s, s ^ step) for s in range(n_high)]
        total = z_sum([total, lax.ppermute(total, "dh", pairs)])
        step *= 2
    planes = [in_plane(total, k) for k in (3, 1, 2)]
    *planes, back = lax.optimization_barrier((*planes, back))
    back_sib = to_sibling(back)
    mine, other = plane_sum([total, *planes])
    other = to_sibling(other)
    *rows, grad_pos = final(out_own, out_sib, back, back_sib, mine, other)
    return *[x[None] for x in rows], grad_pos


def solution(mesh):
    n_dp, n_blk = mesh.shape["dp"], mesh.shape["blk"]
    fine = Mesh(mesh.devices.reshape(n_dp // PLANE, PLANE, n_blk // 2, 2), ("dh", "dl", "z", "core"))
    rows = P(("dh", "dl"), ("z", "core"), None)
    band = P(("z", "core"), None)
    return jax.shard_map(
        local,
        mesh=fine,
        in_specs=(rows, rows, rows, rows, band, P(), P()),
        out_specs=(rows, rows, rows, band),
        check_vma=False,
    )
```

```python
import functools

import jax
import jax.numpy as jnp
from jax import lax
from jax.experimental import pallas as pl
from jax.experimental.pallas import tpu as pltpu
from jax.sharding import Mesh
from jax.sharding import PartitionSpec as P

DH = 64
W = 128
PLANE = 4
MIB = 2**20
F32 = jnp.float32
BF16 = jnp.bfloat16


def mm(a, b):
    return jnp.dot(a, b, preferred_element_type=F32)


def mm_nt(a, b):
    return lax.dot_general(a, b, (((1,), (1,)), ((), ())), preferred_element_type=F32)


def iota(shape, axis):
    return lax.broadcasted_iota(jnp.int32, shape, axis)


def as_bf16(hit):
    return hit.astype(F32).astype(BF16)


CHUNK = 32


def shear(x, frames, row):
    return pltpu.roll(x, frames + 1 + row, 1, stride=1, stride_axis=0)


def columns(start, size):
    return pl.ds(pl.multiple_of(start, W), size)


class Masks:
    def __init__(self, frames):
        span = 2 * frames
        lane = iota((frames, W), 1)
        sub = iota((W, frames), 0)
        self.first = lane < DH
        scale = jnp.bfloat16(DH**-0.5)
        self.lanes = [as_bf16(lane < DH) * scale, as_bf16(lane >= DH) * scale]
        self.subs = [as_bf16(sub < DH), as_bf16(sub >= DH)]
        self.flip = as_bf16(iota((span, span), 0) + iota((span, span), 1) == span - 1)
        row, col = iota((frames, frames), 0), iota((frames, frames), 1)
        self.forward = col + row >= frames - 1
        self.back = [as_bf16(col > row), as_bf16(col <= row)]

    def stack(self, x):
        return jnp.concatenate([x * self.lanes[0], x * self.lanes[1]], axis=0)

    def stack_t(self, x):
        x = x.T
        return jnp.concatenate([x * self.subs[0], x * self.subs[1]], axis=1)


def operands(masks, q, g, bias_c, bias_p):
    qf = q.astype(F32)
    rows = ((qf + bias_c).astype(BF16), (qf + bias_p).astype(BF16), g)
    return [masks.stack(x) for x in rows], [masks.stack_t(x) for x in rows]


def unit(masks, stacks, turned, kw, vw, tables, products=None):
    frames = turned[0].shape[1] // 2
    band0, band1, band0_rev, band1_rev = tables
    qp_stack = stacks[1]
    if products is None:
        products = mm_nt(stacks[0], kw), mm_nt(stacks[2], vw)
    content, gw = products
    near, far = mm_nt(qp_stack, band0_rev), mm_nt(qp_stack, band1_rev)
    yield
    ds, attention_b = [], []
    for start in range(0, 2 * frames, CHUNK):
        rows, first = slice(start, start + CHUNK), start % frames
        own = masks.forward[first : first + CHUNK]
        merged = [
            jnp.where(own, near[rows, :frames], far[rows, :frames]),
            jnp.where(own, far[rows, frames:], near[rows, frames:]),
        ]
        scores = content[rows] + shear(jnp.concatenate(merged, axis=1), frames, first)
        e = jnp.exp(scores - jnp.max(scores, axis=1, keepdims=True))
        inverse = 1.0 / jnp.sum(e, axis=1, keepdims=True)
        delta = jnp.sum(e * gw[rows], axis=1, keepdims=True) * inverse
        attention = e * inverse
        attention_b.append(attention.astype(BF16))
        ds.append((attention * (gw[rows] - delta)).astype(BF16))
        yield
    ds, attention_b = jnp.concatenate(ds, axis=0), jnp.concatenate(attention_b, axis=0)
    flipped = mm(ds, masks.flip)
    dk = mm(turned[0], ds)
    dv = mm(turned[2], attention_b)
    yield
    d0, d1 = [], []
    for start in range(0, 2 * frames, CHUNK):
        first = start % frames
        placed = shear(flipped[start : start + CHUNK], frames, first).astype(BF16)
        left, right = placed[:, :frames], placed[:, frames:]
        mask = [m[first : first + CHUNK] for m in masks.back]
        d0.append(jnp.concatenate([left * mask[0], right * mask[1]], axis=1))
        d1.append(jnp.concatenate([left * mask[1], right * mask[0]], axis=1))
        yield
    d0, d1 = jnp.concatenate(d0, axis=0), jnp.concatenate(d1, axis=0)
    lhs = jnp.concatenate([ds, d0, d1], axis=1)
    rhs = jnp.concatenate([kw, band0, band1], axis=0)
    full = mm(lhs, rhs)
    dq = jnp.where(masks.first, full[:frames], full[frames:]).astype(BF16).astype(F32)
    g1 = mm(turned[1], d1)
    g_band = jnp.concatenate([mm(turned[1], d0), g1[:, frames:], g1[:, :frames]], axis=1)
    return dq, dk, dv, g_band


def side_by_side(groups):
    results = [None] * len(groups)
    left = list(enumerate(groups))
    while left:
        for n, group in list(left):
            try:
                next(group)
            except StopIteration as end:
                results[n] = end.value
                left.remove((n, group))
    return results


def call(body, name, out_shape, scratch=(), limit=8, **options):
    return pl.pallas_call(
        body,
        out_shape=out_shape,
        scratch_shapes=list(scratch),
        compiler_params=pltpu.CompilerParams(vmem_limit_bytes=limit * MIB),
        name=name,
        **options,
    )


def shape(dims, dtype):
    return jax.ShapeDtypeStruct(tuple(dims), dtype)


def pair_of():
    low = lax.axis_index("dl")
    return (low & 1) ^ (low >> 1)


def place(own, sib, scr, slot):
    core = lax.axis_index("core")
    span = scr.shape[3]
    here = columns((2 * core + (pair_of() ^ slot)) * span, span)
    for n, (a, b) in enumerate(zip(own, sib)):
        scr[n, core] = a[:, here]
        scr[n, 1 - core] = b[:, here]
    return here


def ahead_body(*refs):
    own, sib, (bias_c, bias_p) = refs[0:4], refs[4:8], refs[8:10]
    stacks, turned, rows, products, scr = refs[10:]
    frames, span = scr.shape[2:]
    masks = Masks(frames)
    for slot in range(2):
        here = place(own, sib, scr, slot)
        at_bias = bias_c[:, here], bias_p[:, here]
        for j in range(span // W):
            at = slice(j * W, (j + 1) * W)
            for b in range(2):
                if slot == 0 and b == 1:
                    continue
                which = slot + b
                made = operands(masks, scr[0, b, :, at], scr[3, b, :, at], *[x[:, at] for x in at_bias])
                for n in range(3):
                    stacks[which, j, n] = made[0][n]
                    turned[which, j, n] = made[1][n]
                k, v = scr[1, b, :, at], scr[2, b, :, at]
                if b == 0:
                    rows[which, j] = jnp.concatenate([k, v], axis=0)
                else:
                    kw = jnp.concatenate([k, scr[1, 0, :, at]], axis=0)
                    vw = jnp.concatenate([v, scr[2, 0, :, at]], axis=0)
                    rows[which, j] = kw
                    products[j, 0] = mm_nt(made[0][0], kw)
                    products[j, 1] = mm_nt(made[0][2], vw)


def ahead(own, sib, biases):
    frames, width = own[0].shape
    span = width // 4
    groups = span // W
    return call(
        ahead_body,
        "ahead",
        [
            shape((3, groups, 3, 2 * frames, W), BF16),
            shape((3, groups, 3, W, 2 * frames), BF16),
            shape((3, groups, 2 * frames, W), BF16),
            shape((groups, 2, 2 * frames, 2 * frames), F32),
        ],
        [pltpu.VMEM((4, 2, frames, span), BF16)],
        limit=16,
    )(*own, *sib, *biases)


def odd_body(steps, slot, *refs):
    count = 4 if slot else 10
    given, bands, refs = refs[:count], refs[count : count + 2], refs[count + 2 :]
    dq_out, out, carry, g_out, tables, scr, band_scr = refs
    core = lax.axis_index("core")
    frames, span = scr.shape[2:]
    share = band_scr.shape[2]
    band_scr[:, core] = bands[0][...].reshape(steps, share, span)
    band_scr[:, 1 - core] = bands[1][...].reshape(steps, share, span)
    band = band_scr[...].reshape(steps * 2 * share, span)
    masks = Masks(frames)
    band0, band1 = band[: 2 * frames], band[2 * frames :]
    band1 = jnp.concatenate([band1[frames:], band1[:frames]], axis=0)
    tables[0] = band0
    tables[1] = band1
    tables[2] = mm(masks.flip, band0).astype(BF16)
    tables[3] = mm(masks.flip, band1).astype(BF16)
    cuts = [slice(j * W, (j + 1) * W) for j in range(span // W)]
    groups = []
    if slot:
        stacks, turned, rows, products = given
        for j, at in enumerate(cuts):
            made = [[x[2, j, n] for n in range(3)] for x in (stacks, turned)]
            table = [tables[n, :, at] for n in range(4)]
            ready = products[j, 0], products[j, 1]
            groups.append(unit(masks, *made, rows[2, j], None, table, ready))
    else:
        here = place(given[0:4], given[4:8], scr, slot)
        at_bias = given[8][:, here], given[9][:, here]
        for at in cuts:
            made = operands(masks, scr[0, 1, :, at], scr[3, 1, :, at], *[x[:, at] for x in at_bias])
            window = [
                jnp.concatenate([scr[n, 1, :, at], scr[n, 0, :, at]], axis=0) for n in (1, 2)
            ]
            groups.append(unit(masks, *made, *window, [tables[n, :, at] for n in range(4)]))
    for j, (dq, dk, dv, g_band) in enumerate(side_by_side(groups)):
        at = cuts[j]
        dq_out[:, at] = dq
        for n, term in enumerate((dk, dv)):
            out[n, at] = term[:, :frames]
            carry[n, at] = term[:, frames:].astype(BF16)
        g_out[j] = g_band


def even_body(slot, *refs):
    stacks, turned, rows, _, prev, tables, carry, g_odd = refs[:8]
    dq_out, out, back, *g_outs = refs[8:]
    frames, span = dq_out.shape
    masks = Masks(frames)
    cuts = [slice(j * W, (j + 1) * W) for j in range(span // W)]
    groups = []
    for j, at in enumerate(cuts):
        mine = columns((pair_of() ^ slot) * span + j * W, W)
        made = [[x[slot, j, n] for n in range(3)] for x in (stacks, turned)]
        window = [
            jnp.concatenate([rows[slot, j, n * frames : (n + 1) * frames], prev[n, :, mine]], axis=0)
            for n in range(2)
        ]
        groups.append(unit(masks, *made, *window, [tables[n, :, at] for n in range(4)]))
    for j, (dq, dk, dv, g_band) in enumerate(side_by_side(groups)):
        at = cuts[j]
        dq_out[:, at] = dq
        for n, term in enumerate((dk, dv)):
            out[n, at] = term[:, :frames] + carry[n, at].astype(F32)
            back[n, at] = term[:, frames:].astype(BF16)
        g_outs[j][...] = (g_odd[j] + g_band).astype(g_outs[j].dtype)


def cost(groups, frames):
    return pl.CostEstimate(
        flops=2 * groups * 20 * frames * (2 * frames) ** 2,
        bytes_accessed=64 * groups * frames * W,
        transcendentals=groups * 4 * frames * frames,
    )


def odd_call(slot, given, bands, steps, frames):
    rows, span = bands[0].shape
    groups = span // W
    return call(
        functools.partial(odd_body, steps, slot),
        "odd_block",
        [
            shape((frames, span), F32),
            shape((2, span, frames), F32),
            shape((2, span, frames), BF16),
            shape((groups, W, 2 * rows), F32),
            shape((4, rows, span), BF16),
        ],
        [
            pltpu.VMEM((4, 2, frames, span), BF16),
            pltpu.VMEM((steps, 2, rows // steps, span), BF16),
        ],
        limit=16,
        cost_estimate=cost(groups, frames),
    )(*given, *bands)


def even_call(slot, given, prev, odd):
    frames = prev.shape[1]
    _, _, carry, g_odd, tables = odd
    groups, _, rows = g_odd.shape
    span = groups * W
    return call(
        functools.partial(even_body, slot),
        "even_block",
        [shape((frames, span), F32), shape((2, span, frames), F32), shape((2, span, frames), BF16)]
        + [shape((W, rows), F32 if slot else BF16)] * groups,
        limit=16,
        cost_estimate=cost(groups, frames),
    )(*given, prev, tables, carry, g_odd)


def band_cut_body(table, out):
    half = table.shape[1] // 2
    span = half // 2
    pair = pair_of()
    for n in range(2):
        out[:, n * span : (n + 1) * span] = table[:, columns(n * half + pair * span, span)]


def band_cut(table):
    rows, width = table.shape
    return call(band_cut_body, "band_cut", shape((rows, width // 2), BF16))(table)


def band_pack_body(steps, *refs):
    own, sib = refs[steps:]
    core, z = lax.axis_index("core"), lax.axis_index("z")
    span = own.shape[2]
    for n in range(steps):
        at = z ^ n
        own[at] = refs[n][:, columns(core * span, span)]
        sib[at] = refs[n][:, columns((1 - core) * span, span)]


def band_pack(parts):
    rows, width = parts[0].shape
    steps = len(parts)
    out = call(
        functools.partial(band_pack_body, steps),
        "band_pack",
        [shape((steps, rows, width // 2), BF16)] * 2,
    )(*parts)
    return [x.reshape(steps * rows, width // 2) for x in out]


def odd_rows(own, sib, half):
    mine = jnp.stack([x[:, half:] for x in own])
    other = jnp.stack([x[:, :half] for x in sib])
    return jnp.where(lax.axis_index("core") == 1, mine, other)


def summed(refs):
    total = refs[0][...].astype(F32)
    for ref in refs[1:]:
        total = total + ref[...].astype(F32)
    return total


def pair_sum_body(steps, own0, own1, from_x, from_y, *refs):
    scr = refs[-1]
    z = lax.axis_index("z")
    rows = scr.shape[2]
    for n, (a, b) in enumerate(((own0, from_x), (own1, from_y))):
        total = (a[...] + b[...].astype(F32)).astype(BF16)
        for m in range(steps):
            scr[m, n * W : (n + 1) * W] = total[:, m * rows : (m + 1) * rows]
    for m in range(steps):
        refs[m][...] = scr[z ^ m]


def pair_sum(own, received, steps):
    rows = own[0].shape[1] // steps
    return call(
        functools.partial(pair_sum_body, steps),
        "pair_sum",
        [shape((2 * W, rows), BF16)] * steps,
        [pltpu.VMEM((steps, 2 * W, rows), BF16)],
    )(*own, *received)


def z_sum_body(*refs):
    refs[-1][...] = summed(refs[:-1]).astype(BF16)


def z_sum(parts):
    return call(z_sum_body, "z_sum", shape(parts[0].shape, BF16))(*parts)


def plane_sum_body(own, diagonal, from_x, from_y, mine, other, scr):
    core, pair = lax.axis_index("core"), pair_of()
    rows, half = mine.shape
    span = half // 2
    for n, terms in enumerate(((from_x, from_y), (own, diagonal))):
        total = summed(terms).T.reshape(2, rows, span)
        scr[:, :, columns((pair ^ n) * span, span)] = total
    mine[...] = scr[core]
    other[...] = scr[1 - core]


def plane_sum(parts):
    span, rows = parts[0].shape
    half = 2 * span
    return call(
        plane_sum_body,
        "plane_sum",
        [shape((rows // 2, half), F32)] * 2,
        [pltpu.VMEM((2, rows // 2, half), F32)],
    )(*parts)


def settle_body(*refs):
    odd, even, given = refs[0:4], refs[4:8], refs[8:10]
    own, sib, back = refs[10:]
    core, pair = lax.axis_index("core"), pair_of()
    span = odd[0].shape[1]
    for slot in range(2):
        here = columns((pair ^ slot) * span, span)
        for n in range(2):
            back[n, :, here] = given[slot][n].T
        for which, (first, second) in enumerate(((own, sib), (sib, own))):

            @pl.when(core == which)
            def _():
                for target, block in ((first, even), (second, odd)):
                    target[0, :, here] = block[2 * slot][...]
                    for n in range(2):
                        target[1 + n, :, here] = block[2 * slot + 1][n].T


def settle(odd, even, back):
    frames, span = odd[0].shape
    outs = [shape((3, frames, 2 * span), F32)] * 2 + [shape((2, frames, 2 * span), BF16)]
    return call(settle_body, "settle", outs)(*odd, *even, *back)


def final_body(own, sib, back, back_sib, band_mine, band_other, dq, dk, dv, band):
    core = lax.axis_index("core")
    half = own.shape[2]
    mine, other = columns(core * half, half), columns((1 - core) * half, half)
    band[:, mine] = band_mine[...]
    band[:, other] = band_other[...]
    dq[:, mine] = own[0].astype(BF16)
    dq[:, other] = sib[0].astype(BF16)
    odd = core == 1
    for n, out in enumerate((dk, dv)):
        out[:, mine] = (own[1 + n] + jnp.where(odd, back[n].astype(F32), 0.0)).astype(BF16)
        out[:, other] = (sib[1 + n] + jnp.where(odd, back_sib[n].astype(F32), 0.0)).astype(BF16)


def final(own, sib, back, back_sib, mine, other):
    frames, half = back.shape[1:]
    outs = [shape((frames, 2 * half), BF16)] * 3 + [shape((mine.shape[0], 2 * half), F32)]
    return call(final_body, "final", outs)(own, sib, back, back_sib, mine, other)


def local(query_rows, key_rows, value_rows, grad_out, pos_keys, bias_content, bias_position):
    n_high, n_z = lax.axis_size("dh"), lax.axis_size("z")
    width = query_rows.shape[2]

    def along_z(x, flip):
        return lax.ppermute(x, "z", [(s, s ^ flip) for s in range(n_z)])

    def around_z(x, steps):
        return lax.ppermute(x, "z", [(s, (s + steps) % n_z) for s in range(n_z)])

    def to_sibling(x):
        return lax.ppermute(x, "core", [(0, 1), (1, 0)])

    def in_plane(x, flip, cross=0):
        pairs = [
            (2 * d + c, 2 * (d ^ flip) + (c ^ cross)) for d in range(PLANE) for c in range(2)
        ]
        return lax.ppermute(x, ("dl", "core"), pairs)

    cut = band_cut(pos_keys)
    cuts = [cut] + [along_z(cut, k) for k in range(1, n_z)]
    own = [x[0] for x in (query_rows, key_rows, value_rows, grad_out)]
    sib = [to_sibling(x) for x in own]
    moved = odd_rows(own[1:3], sib[1:3], width // 2)
    cuts[3], moved = lax.optimization_barrier((cuts[3], moved))
    prev = around_z(moved, 1)
    band_own, band_sib = band_pack(cuts)
    first_bands = [band_own, to_sibling(band_sib)]
    second_bands = [in_plane(band_own, 1), in_plane(band_sib, 2, 1)]
    biases = [bias_content.reshape(1, width), bias_position.reshape(1, width)]

    frames = own[0].shape[0]
    first = odd_call(0, (*own, *sib, *biases), first_bands, n_z, frames)
    *later_biases, carry = lax.optimization_barrier((*biases, first[2]))
    first = (*first[:2], carry, *first[3:])
    later = ahead(own, sib, later_biases)
    second = odd_call(1, later, second_bands, n_z, frames)
    first, second = lax.optimization_barrier((first, second))
    even0 = even_call(0, later, prev, first)
    received = [in_plane(even0[3], 1), in_plane(even0[4], 2)]
    even1 = even_call(1, later, prev, second)
    g_own = even1[3:]

    *parts, turn = lax.optimization_barrier((*pair_sum(g_own, received, n_z), even0[2]))
    parts = [along_z(parts[k], k) for k in range(n_z - 1, 0, -1)] + [parts[0]]
    odd, even = (*first[:2], *second[:2]), (*even0[:2], *even1[:2])
    out_own, out_sib, back = settle(odd, even, (turn, even1[2]))
    *parts, back, out_sib = lax.optimization_barrier((*parts, back, out_sib))
    back = around_z(back, -1)
    out_sib = to_sibling(out_sib)
    total = z_sum(parts)
    step = 1
    while step < n_high:
        pairs = [(s, s ^ step) for s in range(n_high)]
        total = z_sum([total, lax.ppermute(total, "dh", pairs)])
        step *= 2
    planes = [in_plane(total, k) for k in (3, 1, 2)]
    *planes, back = lax.optimization_barrier((*planes, back))
    back_sib = to_sibling(back)
    mine, other = plane_sum([total, *planes])
    other = to_sibling(other)
    *rows, grad_pos = final(out_own, out_sib, back, back_sib, mine, other)
    return *[x[None] for x in rows], grad_pos


def solution(mesh):
    n_dp, n_blk = mesh.shape["dp"], mesh.shape["blk"]
    fine = Mesh(mesh.devices.reshape(n_dp // PLANE, PLANE, n_blk // 2, 2), ("dh", "dl", "z", "core"))
    rows = P(("dh", "dl"), ("z", "core"), None)
    band = P(("z", "core"), None)
    return jax.shard_map(
        local,
        mesh=fine,
        in_specs=(rows, rows, rows, rows, band, P(), P()),
        out_specs=(rows, rows, rows, band),
        check_vma=False,
    )
```
